32 devices in a mesh: section: 4 (over y, x), dp: 8 (over z, core).
Axes of the slice: x: 2, y: 2, z: 4, core: 2. Of those that a mesh axis runs over, the one named last changes fastest.
Arguments:
- states_in: bfloat16 [16, 1024, 512], P('dp', None, 'section'), may hold values from -6 to 6
- memory: bfloat16 [16, 1024, 512], P('dp', None, 'section'), may hold values from -6 to 6
- cotangent: bfloat16 [16, 1024, 512], P('dp', None, 'section'), may hold values from -6 to 6
- weight_bank: bfloat16 [4, 8, 512, 512], P('section')
- gain_bank: float32 [4, 2, 512], P('section'), may hold values from 0.1 to 1.9
- segments: int32 [16, 1024], P('dp'), may hold values from 0 to 7, as said below
- pad_mask: int32 [16, 1024], P('dp'), may hold values from 0 to 1, as said below
- memory_segments: int32 [16, 1024], P('dp'), may hold values from 0 to 7, as said below
- memory_mask: int32 [16, 1024], P('dp'), may hold values from 0 to 1, as said below
- exit_depths: int32 [16, 8], P('dp'), may hold values from 1 to 2
Outputs:
- states: bfloat16 [16, 1024, 512], P('dp', None, 'section')
- halting: float32 [16, 2, 1024], P('dp', None, 'section')
- input_grad: float32 [16, 1024, 512], P('dp', None, 'section')
- memory_grad: float32 [16, 1024, 512], P('dp', None, 'section')
- bank_grad: float32 [4, 8, 512, 512], P('section')
- gain_grad: float32 [4, 2, 512], P('section')
The draws below stay inside these ranges and needn't reach their ends.
Inputs may be any that keep to these rules, and one draw needn't show every extreme that they name: `segments`: each row holds 8 sentences numbered in order from 0, each at least two filled slots long; the padding slots after a row's filled slots carry the number 8 - 1. `pad_mask`: a row's filled slots come first, its padding after them. `memory_segments`: each row's memory holds 8 source sentences numbered in order from 0, each at least two filled slots long; padding slots after them carry the number 8 - 1. `memory_mask`: a row's filled memory slots come first, its padding after them. `exit_depths`: a sentence of depth 1 leaves after the first layer, of depth 2 after the second.
All inputs are finite; a program needn't handle non-finite values.
Results may differ from the reference program's by a relative error of at most 0.025.
Values may be sent and summed in bfloat16 or wider, within the bound.
A program may use at most 256 MiB of HBM per device.

```python
import jax
import jax.numpy as jnp
from jax import lax

D = 512
HEADS = 8
FF = 2048
ROW = 1024
MEM = 1024
SENTS = 8
SECTIONS = 4
ROWS = 16


def sentence_layout(key, slots, salt):
    key = jax.random.fold_in(key, salt)
    first_key, second_key = jax.random.split(key)
    weights = jax.random.randint(first_key, (ROWS, SENTS), 8, 24)
    padding = jax.random.randint(second_key, (ROWS, 1), 0, slots // 5 + 1)
    filled = slots - padding
    shares = weights * filled // jnp.sum(weights, axis=1, keepdims=True)
    bounds = jnp.cumsum(shares, axis=1)[:, :-1]
    places = jnp.arange(slots)
    numbers = jnp.sum((places[None, :, None] >= bounds[:, None, :]).astype(jnp.int32), axis=2)
    filled_mask = (places[None, :] < filled).astype(jnp.int32)
    return (numbers.astype(jnp.int32), filled_mask)


def draw_segments(key, part):
    return sentence_layout(key, ROW, 11)[0]


def draw_pad_mask(key, part):
    return sentence_layout(key, ROW, 11)[1]


def draw_memory_segments(key, part):
    return sentence_layout(key, MEM, 12)[0]


def draw_memory_mask(key, part):
    return sentence_layout(key, MEM, 12)[1]


def draw_weight_bank(key, part):
    key = jax.random.fold_in(key, 5)
    noise = jax.random.truncated_normal(key, -6.0, 6.0, (SECTIONS, 8, D, D), jnp.float32)
    section_ids = jnp.arange(SECTIONS)[:, None]
    slot_ids = jnp.arange(8)[None, :]
    odd = section_ids % 2 == 1
    dense_scale = jnp.where(slot_ids < 4, D ** (-0.5), 1.7 * FF ** (-0.5))
    attend_scale = jnp.where(slot_ids % 4 == 3, 5.0 * D ** (-0.5), D ** (-0.5))
    scale = jnp.where(odd, dense_scale, attend_scale)
    return (noise * scale[:, :, None, None]).astype(jnp.bfloat16)


def with_ends(values, own_key, smallest, top_value):
    spot = [jax.random.randint(jax.random.fold_in(own_key, axis), (), 0, length) for axis, length in enumerate(values.shape)]
    longest = values.shape.index(max(values.shape))
    next_to = spot[:longest] + [(spot[longest] + 1) % values.shape[longest]] + spot[longest + 1:]
    return values.at[tuple(spot)].set(smallest).at[tuple(next_to)].set(top_value)


def block_scale(key, extent, cuts, least, largest):
    level = 1.0
    for position, shards_of in cuts:
        heights = jax.random.uniform(jax.random.fold_in(jax.random.fold_in(key, 6), position), (shards_of,), jnp.float32, least / len(cuts), largest / len(cuts))
        level = level * jnp.repeat(jnp.exp(heights), extent[position] // shards_of).reshape((-1,) + (1,) * (len(extent) - 1 - position))
    return level


def centred(rng, dims, spread, reach, cuts=(), held_as=jnp.bfloat16):
    values = jax.random.normal(rng, dims, jnp.float32) * spread
    if len(cuts) > 0:
        values = block_scale(rng, dims, cuts, -0.22, 0.18) * values
    return jnp.clip(values, min=-reach, max=reach).astype(held_as)


def setup_inputs(seed: int = 0) -> dict:
    arg_keys = jax.random.split(jax.random.key(seed), 11)
    states_in = centred(arg_keys[0], (ROWS, ROW, D), 1.0, 6.0, ((0, 8), (2, 4)))
    memory = centred(arg_keys[1], (ROWS, MEM, D), 1.0, 6.0, ((0, 8), (2, 4)))
    cotangent = centred(arg_keys[2], (ROWS, ROW, D), 1.0, 6.0, ((0, 8), (2, 4)))
    weight_bank = draw_weight_bank(jax.random.fold_in(arg_keys[10], 71), 0)
    gain_bank = jnp.clip(1.0 + 0.18 * jax.random.normal(arg_keys[4], (SECTIONS, 2, D), jnp.float32), 0.1, 1.9)
    segments = draw_segments(jax.random.fold_in(arg_keys[10], 71), 0)
    pad_mask = draw_pad_mask(jax.random.fold_in(arg_keys[10], 71), 0)
    memory_segments = draw_memory_segments(jax.random.fold_in(arg_keys[10], 71), 0)
    memory_mask = draw_memory_mask(jax.random.fold_in(arg_keys[10], 71), 0)
    exit_depths = with_ends(jax.random.randint(arg_keys[9], (ROWS, SENTS), 1, 3), jax.random.fold_in(arg_keys[9], 1), 1, 2).astype(jnp.int32)
    return {"states_in": states_in, "memory": memory, "cotangent": cotangent, "weight_bank": weight_bank, "gain_bank": gain_bank, "segments": segments, "pad_mask": pad_mask, "memory_segments": memory_segments, "memory_mask": memory_mask, "exit_depths": exit_depths}


@jax.custom_vjp
def low(v):
    return lax.optimization_barrier(v.astype(jnp.bfloat16)).astype(jnp.float32)

@jax.custom_vjp
def low_back(v):
    return v

def low_keep(v):
    return (low(v), None)

def low_pass(kept, grad):
    return (grad,)

def back_keep(v):
    return (v, None)

def back_low(kept, grad):
    return (low(grad),)
low.defvjp(low_keep, low_pass)
low_back.defvjp(back_keep, back_low)
eps = 1e-06
finest = lax.Precision.HIGHEST

def rms_norm(state, gain):
    return state * lax.rsqrt(lax.optimization_barrier(jnp.mean(state * state, axis=-1, keepdims=True)) + eps) * gain

def product(left, right):
    return jnp.dot(left, right, precision=finest, preferred_element_type=jnp.float32)

def row_masks(segments, pad_mask, memory_segments, memory_mask, depths):
    places = jnp.arange(segments.shape[0])
    self_allow = (segments[:, None] == segments[None, :]) & (places[None, :] <= places[:, None]) & ((pad_mask[None, :] == 1) | (pad_mask[:, None] == 0))
    cross_allow = (memory_segments[None, :] == segments[:, None]) & (memory_mask[None, :] == 1) | (pad_mask[:, None] == 0)
    table = segments[:, None] == jnp.arange(depths.shape[0])[None, :]
    token_depth = lax.optimization_barrier(jnp.sum(jnp.where(table, depths[None, :], 0), axis=1))
    return (self_allow, cross_allow, token_depth)

def attention(state, source, gain, weights, allowed, onward):
    length, width = state.shape
    size = width // HEADS
    normed = low(rms_norm(state, gain))
    keys_from = normed if source is None else source
    query = low(low_back(product(normed, weights[0])))
    keys = low(low_back(product(keys_from, weights[1])))
    values = low(low_back(product(keys_from, weights[2])))
    scores = jnp.einsum('qhe,khe->hqk', query.reshape(length, HEADS, size), keys.reshape(-1, HEADS, size), precision=finest) * size ** (-0.5)
    scores = low_back(jnp.where(allowed[None], scores, -1e+30))
    probs = low(jax.nn.softmax(scores, axis=-1))
    mixed = jnp.einsum('hqk,khe->qhe', probs, values.reshape(-1, HEADS, size), precision=finest).reshape(length, width)
    mixed = low(low_back(mixed))
    branch = low_back(product(mixed, weights[3]))
    return state + onward[:, None] * branch

def feed_forward(state, gain, weights, onward):
    normed = low(rms_norm(state, gain))
    hidden = low_back(jnp.einsum('td,jde->tje', normed, weights[:4], precision=finest))
    active = low(jax.nn.gelu(hidden, approximate=True))
    branch = low_back(jnp.einsum('tje,jed->td', active, weights[4:], precision=finest))
    return state + onward[:, None] * branch

def decode_row(row_in, memory_row, bank, gains, segments, pad_mask, memory_segments, memory_mask, depths):
    self_allow, cross_allow, token_depth = row_masks(segments, pad_mask, memory_segments, memory_mask, depths)
    keep = (token_depth == 2).astype(jnp.float32)
    every = jnp.ones_like(keep)
    state = attention(row_in, None, gains[0, 0], bank[0, :4], self_allow, every)
    state = attention(state, memory_row, gains[0, 1], bank[0, 4:], cross_allow, every)
    state = low(low_back(state))
    layer_one = feed_forward(state, gains[1, 0], bank[1], every)
    state = low(low_back(layer_one))
    state = attention(state, None, gains[2, 0], bank[2, :4], self_allow, keep)
    state = attention(state, memory_row, gains[2, 1], bank[2, 4:], cross_allow, keep)
    state = low(low_back(state))
    layer_two = feed_forward(state, gains[3, 0], bank[3], keep)
    return (layer_two, layer_one)

def reference(states_in, memory, cotangent, weight_bank, gain_bank, segments, pad_mask, memory_segments, memory_mask, exit_depths):
    rows_in = states_in.astype(jnp.float32)
    memory_in = memory.astype(jnp.float32)
    bank = weight_bank.astype(jnp.float32)
    gains = gain_bank.astype(jnp.float32)

    def forward(rows_in, memory_in, bank, gains):
        row_fn = jax.checkpoint(decode_row)

        def step(carry, items):
            row_in, memory_row, row_segments, row_pads, row_memory_segments, row_memory_mask, row_depths = items
            layer_two, layer_one = row_fn(row_in, memory_row, bank, gains, row_segments, row_pads, row_memory_segments, row_memory_mask, row_depths)
            return (carry, (layer_two, layer_one))
        _, outs = lax.scan(step, jnp.zeros((), jnp.float32), (rows_in, memory_in, segments, pad_mask, memory_segments, memory_mask, exit_depths))
        return outs
    (final, first), back = jax.vjp(forward, rows_in, memory_in, bank, gains)
    grad_rows, grad_memory, grad_bank, grad_gains = back((cotangent.astype(jnp.float32), jnp.zeros_like(first)))
    table = segments[:, :, None] == jnp.arange(SENTS)[None, None, :]
    token_depth = lax.optimization_barrier(jnp.sum(jnp.where(table, exit_depths[:, None, :], 0), axis=2))
    valid = pad_mask.astype(jnp.float32)
    targets = jnp.stack([(token_depth == 1).astype(jnp.float32), jnp.ones_like(valid)], axis=1)
    layers = jnp.stack([first, final], axis=1)
    vectors = jnp.stack([gains[1, 1], gains[3, 1]])

    def exit_loss(exit_vectors):
        logits = lax.optimization_barrier(jnp.sum(layers * exit_vectors[None, :, None, :], axis=-1)) * D ** (-0.5)
        terms = -(targets * jax.nn.log_sigmoid(logits) + (1.0 - targets) * jax.nn.log_sigmoid(-logits))
        return jnp.sum(valid[:, None, :] * terms) / SENTS
    exit_grad = jax.grad(exit_loss)(vectors)
    halting = jax.nn.sigmoid(lax.optimization_barrier(jnp.sum(layers * vectors[None, :, None, :], axis=-1)) * D ** (-0.5))
    grad_gains = grad_gains.at[1, 1].add(exit_grad[0]).at[3, 1].add(exit_grad[1])
    return (final.astype(jnp.bfloat16), halting, grad_rows, grad_memory, grad_bank, grad_gains)
```

```python
import functools

import jax
import jax.numpy as jnp
from jax import lax
from jax.experimental import pallas as pl
from jax.experimental.pallas import tpu as pltpu
from jax.sharding import PartitionSpec as P

HEADS = 8
EPS = 1e-06
BLOCK = 128
NEG = -1e30

bf16 = jnp.bfloat16
f32 = jnp.float32

CORE, FLAG_T, FLAG_M, FIRST, LAST = 0, 1, 2, 3, 4
SELF_LO, SELF_HI, CROSS_LO, CROSS_HI = 8, 16, 24, 32
META = 40


def dot(left, right):
    return jnp.dot(left, right, preferred_element_type=f32)


def dot_nt(left, right):
    return lax.dot_general(left, right, (((1,), (1,)), ((), ())), preferred_element_type=f32)


def dot_tn(left, right):
    return lax.dot_general(left, right, (((0,), (0,)), ((), ())), preferred_element_type=f32)


def exact_nt(left, right):
    return lax.dot_general(
        left, right, (((1,), (1,)), ((), ())), precision=lax.Precision.HIGHEST, preferred_element_type=f32
    )


def exact(left, right):
    return jnp.dot(left, right, precision=lax.Precision.HIGHEST, preferred_element_type=f32)


def norm(x, gain):
    return x * lax.rsqrt(jnp.mean(x * x, axis=-1, keepdims=True) + EPS) * gain


def norm_back(x, gain, grad):
    rate = lax.rsqrt(jnp.mean(x * x, axis=-1, keepdims=True) + EPS)
    scaled = x * rate
    inner = grad * gain
    grad_x = rate * (inner - scaled * jnp.mean(inner * scaled, axis=-1, keepdims=True))
    return grad_x, jnp.sum(grad * scaled, axis=0, keepdims=True)


GELU_A = 0.7978845608028654
GELU_B = 0.044715


def gelu(z):
    return 0.5 * z * (1.0 + jnp.tanh(GELU_A * (z + GELU_B * z * z * z)))


def gelu_both(z):
    square = z * z
    bend = jnp.tanh(GELU_A * z * (1.0 + GELU_B * square))
    half = 0.5 * (1.0 + bend)
    slope = half + 0.5 * z * (1.0 - bend * bend) * (GELU_A * (1.0 + 3.0 * GELU_B * square))
    return z * half, slope


def windows(meta, length):
    wide = length * 5 // 8
    slim = length - wide
    core = meta[CORE]
    return (
        pl.ds(pl.multiple_of(core * slim, BLOCK), wide),
        pl.ds(pl.multiple_of((1 - core) * wide, BLOCK), slim),
    )


def over(meta, flag, length, work):
    main, other = windows(meta, length)
    work(main, True)

    @pl.when(meta[flag] == 1)
    def _():
        work(other, False)


def block(i):
    return pl.ds(pl.multiple_of(i * BLOCK, BLOCK), BLOCK)


def pair_lanes(p):
    return slice(p * BLOCK, (p + 1) * BLOCK)


def two_heads(tile, lane):
    zero = jnp.zeros_like(tile)
    return jnp.concatenate([jnp.where(lane < 64, tile, zero), jnp.where(lane < 64, zero, tile)], axis=0)


def attend_tiles(meta, lo_at, hi_at, low_col, q, k, v, o, lse, cols, scores, peaks, sums):
    pairs = q.shape[1] // BLOCK

    def one_block(i, _):
        first, last = meta[lo_at + i], meta[hi_at + i]

        @pl.when(last > first)
        def _():
            rows = block(i)
            lane = lax.broadcasted_iota(jnp.int32, (BLOCK, BLOCK), 1)
            low = cols[rows, low_col : low_col + 1]
            high = cols[rows, low_col + 1 : low_col + 2]
            peaks[...] = jnp.full(peaks.shape, -jnp.inf, f32)
            sums[...] = jnp.zeros(sums.shape, f32)

            def score(j, _):
                place = lane + j * BLOCK
                bias = jnp.where((place >= low) & (place < high), 0.0, NEG)
                bias = jnp.concatenate([bias, bias], axis=1)
                for p in range(pairs):
                    keys = two_heads(k[block(j), pair_lanes(p)], lane)
                    tile = dot_nt(q[rows, pair_lanes(p)], keys) + bias
                    scores[j - first, p] = tile
                    peaks[p] = jnp.maximum(peaks[p], tile)
                return 0

            lax.fori_loop(first, last, score, 0)
            for p in range(pairs):
                for e in range(2):
                    lanes = slice(e * BLOCK, (e + 1) * BLOCK)
                    top = jnp.max(peaks[p, :, lanes], axis=-1, keepdims=True)
                    peaks[p, :, lanes] = jnp.broadcast_to(top, (BLOCK, BLOCK))

            def mix(j, _):
                ones = jnp.where(lane < 64, 1.0, 0.0).astype(bf16)
                marks = jnp.concatenate([ones, 1 - ones], axis=0)
                for p in range(pairs):
                    weights = jnp.exp(scores[j - first, p] - peaks[p]).astype(bf16)
                    values = two_heads(v[block(j), pair_lanes(p)], lane)
                    sums[p] += dot(weights, jnp.concatenate([values, marks], axis=1))
                return 0

            lax.fori_loop(first, last, mix, 0)
            gathered = jnp.zeros((BLOCK, BLOCK), f32)
            for p in range(pairs):
                total = sums[p, :, BLOCK:]
                o[rows, pair_lanes(p)] = (sums[p, :, :BLOCK] / total).astype(bf16)
                top = jnp.where(lane < 64, peaks[p, :, :BLOCK], peaks[p, :, BLOCK:])
                gathered = jnp.where(lane % 64 // 16 == p, top + jnp.log(total), gathered)
            turned = gathered.T
            for p in range(pairs):
                for e in range(2):
                    lse[2 * p + e : 2 * p + e + 1, rows] = turned[e * 64 + p * 16 : e * 64 + p * 16 + 1, :]

        return 0

    lax.fori_loop(meta[FIRST], meta[LAST], one_block, 0)


def attend_tiles_back(
    meta, lo_at, hi_at, low_row, q, k, v, lse, delta, do, info, dq, dk, dv, both_q, both_o, dq_sum
):
    pairs = q.shape[1] // BLOCK

    def one_block(i, _):
        first, last = meta[lo_at + i], meta[hi_at + i]

        @pl.when(last > first)
        def _():
            rows = block(i)
            lane = lax.broadcasted_iota(jnp.int32, (BLOCK, BLOCK), 1)
            slot = lax.broadcasted_iota(jnp.int32, (BLOCK, BLOCK), 0)
            low = info[low_row : low_row + 1, rows]
            high = info[low_row + 1 : low_row + 2, rows]
            dq_sum[...] = jnp.zeros(dq_sum.shape, f32)
            for p in range(pairs):
                both_q[p] = two_heads(q[rows, pair_lanes(p)], lane)
                both_o[p] = two_heads(do[rows, pair_lanes(p)], lane)

            def tile(j, _):
                place = slot + j * BLOCK
                bias = jnp.where((place >= low) & (place < high), 0.0, NEG)
                bias = jnp.concatenate([bias, bias], axis=1)
                for p in range(pairs):
                    lanes = pair_lanes(p)
                    keys, values = k[block(j), lanes], v[block(j), lanes]
                    queries, grads = both_q[p], both_o[p]
                    log_total = jnp.concatenate([lse[2 * p : 2 * p + 1, rows], lse[2 * p + 1 : 2 * p + 2, rows]], axis=1)
                    change = jnp.concatenate([delta[2 * p : 2 * p + 1, rows], delta[2 * p + 1 : 2 * p + 2, rows]], axis=1)
                    probs = jnp.exp(dot_nt(keys, queries) + bias - log_total)
                    grad_scores = (probs * (dot_nt(values, grads) - change)).astype(bf16)
                    dv[block(j), lanes] += dot(probs.astype(bf16), grads)
                    dk[block(j), lanes] += dot(grad_scores, queries)
                    mixed = dot_tn(grad_scores, keys)
                    dq_sum[:, lanes] += jnp.where(lane < 64, mixed[:BLOCK], mixed[BLOCK:])
                return 0

            lax.fori_loop(first, last, tile, 0)
            dq[rows, :] = (dq_sum[...] * 0.125).astype(bf16)

        return 0

    lax.fori_loop(meta[FIRST], meta[LAST], one_block, 0)


def attention_forward_kernel(
    meta, x, mem, w, gain, go, cols, q1, k1, v1, o1, l1, mid, q2, k2, v2, o2, l2, out, scores, peaks, sums
):
    length = x.shape[0]

    def self_in(rows, _):
        a = norm(x[rows, :].astype(f32), gain[0:1, :]).astype(bf16)
        q1[rows, :] = (dot(a, w[0]) * 0.125).astype(bf16)
        k1[rows, :] = dot(a, w[1]).astype(bf16)
        v1[rows, :] = dot(a, w[2]).astype(bf16)
        o1[rows, :] = jnp.zeros((rows.size, x.shape[1]), bf16)

    over(meta, FLAG_T, length, self_in)

    def memory_in(rows, _):
        source = mem[rows, :]
        k2[rows, :] = dot(source, w[5]).astype(bf16)
        v2[rows, :] = dot(source, w[6]).astype(bf16)

    over(meta, FLAG_M, length, memory_in)
    l1[...] = jnp.zeros(l1.shape, f32)
    l2[...] = jnp.zeros(l2.shape, f32)
    attend_tiles(meta, SELF_LO, SELF_HI, 0, q1, k1, v1, o1, l1, cols, scores, peaks, sums)

    def cross_in(rows, _):
        state = x[rows, :].astype(f32) + go[rows, 0:1] * dot(o1[rows, :], w[3])
        mid[rows, :] = state
        a = norm(state, gain[1:2, :]).astype(bf16)
        q2[rows, :] = (dot(a, w[4]) * 0.125).astype(bf16)
        o2[rows, :] = jnp.zeros((rows.size, x.shape[1]), bf16)

    over(meta, FLAG_T, length, cross_in)
    attend_tiles(meta, CROSS_LO, CROSS_HI, 2, q2, k2, v2, o2, l2, cols, scores, peaks, sums)

    def finish(rows, _):
        out[rows, :] = (mid[rows, :] + go[rows, 0:1] * dot(o2[rows, :], w[7])).astype(bf16)

    over(meta, FLAG_T, length, finish)


def attention_backward_kernel(
    meta, x, mem, w, gain, go, info, q1, k1, v1, o1, l1, mid, q2, k2, v2, o2, l2, dh, dmem_in,
    dx, dmem, dw, dgain,
    dstate, do, dq, dk, dv, dkb, dvb, delta, both_q, both_o, dq_sum, acc, heads,
):
    length, width = x.shape
    row_of = lax.broadcasted_iota(jnp.int32, (HEADS, width), 0)
    lane_of = lax.broadcasted_iota(jnp.int32, (HEADS, width), 1)
    heads[...] = (lane_of // (width // HEADS) == row_of).astype(bf16)
    dk[...] = jnp.zeros(dk.shape, f32)
    dv[...] = jnp.zeros(dv.shape, f32)
    delta[...] = jnp.zeros(delta.shape, f32)

    def weight_grad(index, flag, left, right):
        def part(rows, fresh):
            term = dot_tn(left(rows), right(rows))
            acc[...] = term if fresh else acc[...] + term

        over(meta, flag, length, part)
        dw[index] = acc[...].astype(bf16)

    def begin(grad_of, o, out_weight):
        def part(rows, _):
            dy = (go[rows, 0:1] * grad_of(rows)).astype(bf16)
            grad = dot_nt(dy, w[out_weight]).astype(bf16)
            do[rows, :] = grad
            product = grad.astype(f32) * o[rows, :].astype(f32)
            high = product.astype(bf16)
            rest = (product - high.astype(f32)).astype(bf16)
            delta[:, rows] = dot_nt(heads[...], high) + dot_nt(heads[...], rest)
            dq[rows, :] = jnp.zeros((rows.size, width), bf16)

        over(meta, FLAG_T, length, part)
        weight_grad(out_weight, FLAG_T, lambda rows: o[rows, :], lambda rows: (go[rows, 0:1] * grad_of(rows)).astype(bf16))

    def top_grad(rows):
        return dh[rows, :].astype(f32)

    begin(top_grad, o2, 7)
    attend_tiles_back(
        meta, CROSS_LO, CROSS_HI, 2, q2, k2, v2, l2, delta, do, info, dq, dk, dv, both_q, both_o, dq_sum
    )

    dmem[...] = dmem_in[...]

    def memory_out(rows, _):
        grad_k, grad_v = dk[rows, :].astype(bf16), dv[rows, :].astype(bf16)
        dkb[rows, :] = grad_k
        dvb[rows, :] = grad_v
        dmem[rows, :] += dot_nt(grad_k, w[5]) + dot_nt(grad_v, w[6])

    over(meta, FLAG_M, length, memory_out)
    weight_grad(5, FLAG_M, lambda rows: mem[rows, :], lambda rows: dkb[rows, :])
    weight_grad(6, FLAG_M, lambda rows: mem[rows, :], lambda rows: dvb[rows, :])

    def cross_out(rows, fresh):
        state = mid[rows, :]
        grad_x, grad_gain = norm_back(state, gain[1:2, :], dot_nt(dq[rows, :], w[4]))
        dstate[rows, :] = top_grad(rows) + grad_x
        dgain[1:2, :] = grad_gain if fresh else dgain[1:2, :] + grad_gain

    over(meta, FLAG_T, length, cross_out)
    weight_grad(4, FLAG_T, lambda rows: norm(mid[rows, :], gain[1:2, :]).astype(bf16), lambda rows: dq[rows, :])

    dk[...] = jnp.zeros(dk.shape, f32)
    dv[...] = jnp.zeros(dv.shape, f32)
    begin(lambda rows: dstate[rows, :], o1, 3)
    attend_tiles_back(
        meta, SELF_LO, SELF_HI, 0, q1, k1, v1, l1, delta, do, info, dq, dk, dv, both_q, both_o, dq_sum
    )

    def self_out(rows, fresh):
        grad_k, grad_v = dk[rows, :].astype(bf16), dv[rows, :].astype(bf16)
        dkb[rows, :] = grad_k
        dvb[rows, :] = grad_v
        da = dot_nt(dq[rows, :], w[0]) + dot_nt(grad_k, w[1]) + dot_nt(grad_v, w[2])
        grad_x, grad_gain = norm_back(x[rows, :].astype(f32), gain[0:1, :], da)
        dx[rows, :] = (dstate[rows, :] + grad_x).astype(bf16)
        dgain[0:1, :] = grad_gain if fresh else dgain[0:1, :] + grad_gain

    over(meta, FLAG_T, length, self_out)

    def normed(rows):
        return norm(x[rows, :].astype(f32), gain[0:1, :]).astype(bf16)

    weight_grad(0, FLAG_T, normed, lambda rows: dq[rows, :])
    weight_grad(1, FLAG_T, normed, lambda rows: dkb[rows, :])
    weight_grad(2, FLAG_T, normed, lambda rows: dvb[rows, :])


def exit_part(layer, vector, frows, rows, target_row, halt, exit_grad, fresh, sentences):
    factor = layer.shape[1] ** (-0.5)
    vectors = jnp.broadcast_to(vector, (8, layer.shape[1]))
    score = jax.nn.sigmoid(exact_nt(vectors, layer) * factor)
    halt[:, rows] = score
    weight = frows[0:1, rows] * (score - frows[target_row : target_row + 1, rows]) / sentences
    term = exact(weight, layer)[0:1] * factor
    exit_grad[...] = term if fresh else exit_grad[...] + term


def dense_forward_kernel(sentences, meta, x, w, gain, frows, out, halt, exit_grad):
    length = x.shape[0]
    parts = w.shape[0] // 2

    def part(rows, fresh):
        state = x[rows, :].astype(f32)
        a = norm(state, gain[0:1, :]).astype(bf16)
        branch = jnp.zeros(state.shape, f32)
        for j in range(parts):
            branch = branch + dot(gelu(dot(a, w[j])).astype(bf16), w[parts + j])
        layer = state + branch
        out[rows, :] = layer.astype(bf16)
        exit_part(layer, gain[1:2, :], frows, rows, 1, halt, exit_grad, fresh, sentences)

    over(meta, FLAG_T, length, part)


def dense_backward_kernel(sentences, final, meta, x, w, gain, go, frows, dh, dx, dw, dgain, *rest):
    if final:
        out, halt, exit_grad, acc = rest
    else:
        (acc,) = rest
    length, width = x.shape
    parts = w.shape[0] // 2

    def part(rows, fresh):
        state = x[rows, :].astype(f32)
        a = norm(state, gain[0:1, :]).astype(bf16)
        dy = (go[rows, 0:1] * dh[rows, :].astype(f32)).astype(bf16)
        branch = jnp.zeros(state.shape, f32)
        da = jnp.zeros(state.shape, f32)
        for j in range(parts):
            active, slope = gelu_both(dot(a, w[j]))
            active = active.astype(bf16)
            if final:
                branch = branch + dot(active, w[parts + j])
            dhidden = (slope * dot_nt(dy, w[parts + j])).astype(bf16)
            da = da + dot_nt(dhidden, w[j])
            up, down = dot_tn(a, dhidden), dot_tn(active, dy)
            acc[j] = up if fresh else acc[j] + up
            acc[parts + j] = down if fresh else acc[parts + j] + down
        grad_x, grad_gain = norm_back(state, gain[0:1, :], da)
        dx[rows, :] = (dh[rows, :].astype(f32) + grad_x).astype(bf16)
        dgain[...] = grad_gain if fresh else dgain[...] + grad_gain
        if final:
            layer = state + go[rows, 0:1] * branch
            out[rows, :] = layer.astype(bf16)
            exit_part(layer, gain[1:2, :], frows, rows, 2, halt, exit_grad, fresh, sentences)

    over(meta, FLAG_T, length, part)
    for j in range(2 * parts):
        dw[j] = acc[j].astype(bf16)


VMEM = pl.BlockSpec(memory_space=pltpu.VMEM)
SMEM = pl.BlockSpec(memory_space=pltpu.SMEM)


def run(kernel, outs, scratch, name, flops, *args):
    return pl.pallas_call(
        kernel,
        out_shape=[jax.ShapeDtypeStruct(shape, dtype) for shape, dtype in outs],
        in_specs=[SMEM] + [VMEM] * (len(args) - 1),
        out_specs=[VMEM] * len(outs),
        scratch_shapes=[pltpu.VMEM(shape, dtype) for shape, dtype in scratch],
        compiler_params=pltpu.CompilerParams(vmem_limit_bytes=60 * 2**20),
        cost_estimate=pl.CostEstimate(flops=flops, bytes_accessed=20 * 2**20, transcendentals=0),
        name=name,
    )(*args)


def attention_forward(meta, x, mem, w, gain, go, cols, name):
    length, width = x.shape
    wide = ((length, width), bf16)
    logs = ((HEADS, length), f32)
    pairs = width // BLOCK
    tile = ((pairs, BLOCK, 2 * BLOCK), f32)
    return run(
        attention_forward_kernel,
        [wide, wide, wide, wide, logs, ((length, width), f32), wide, wide, wide, wide, logs, wide],
        [((length // BLOCK,) + tile[0], f32), tile, tile],
        name, 6 * 10**9, meta, x, mem, w, gain, go, cols,
    )


def attention_backward(meta, x, mem, w, gain, go, info, saved, dh, dmem, name):
    length, width = x.shape
    pairs = width // BLOCK
    wide, full = ((length, width), bf16), ((length, width), f32)
    both = ((pairs, 2 * BLOCK, BLOCK), bf16)
    return run(
        attention_backward_kernel,
        [wide, full, (w.shape, bf16), ((2, width), f32)],
        [full, wide, wide, full, full, wide, wide, ((HEADS, length), f32), both, both,
         ((BLOCK, width), f32), ((width, width), f32), ((HEADS, width), bf16)],
        name, 12 * 10**9, meta, x, mem, w, gain, go, info, *saved, dh, dmem,
    )


def dense_forward(meta, x, w, gain, frows, sentences, name):
    length, width = x.shape
    return run(
        functools.partial(dense_forward_kernel, sentences),
        [((length, width), bf16), ((8, length), f32), ((1, width), f32)], [],
        name, 4 * 10**9, meta, x, w, gain, frows,
    )


def dense_backward(meta, x, w, gain, go, frows, dh, sentences, final, name):
    length, width = x.shape
    outs = [((length, width), bf16), (w.shape, bf16), ((1, width), f32)]
    if final:
        outs += [((length, width), bf16), ((8, length), f32), ((1, width), f32)]
    return run(
        functools.partial(dense_backward_kernel, sentences, final), outs, [(w.shape, f32)],
        name, 8 * 10**9, meta, x, w, gain, go, frows, dh,
    )


def plan(core, seg, pad, mseg, mmask, depths):
    length, slots, sentences = seg.shape[0], mseg.shape[0], depths.shape[0]
    numbers = jnp.arange(sentences)
    place = jnp.arange(length)
    mine = (seg[:, None] == numbers[None, :]).astype(jnp.int32)

    def of_token(table):
        return jnp.sum(mine * table[None, :], axis=1)

    starts = jnp.sum((seg[:, None] < numbers[None, :]).astype(jnp.int32), axis=0)
    filled = jnp.sum(pad)
    memory_starts = jnp.sum((mseg[:, None] < numbers[None, :]).astype(jnp.int32), axis=0)
    memory_stops = jnp.sum((mseg[:, None] <= numbers[None, :]).astype(jnp.int32), axis=0)
    memory_stops = jnp.minimum(memory_stops, jnp.sum(mmask))
    low = of_token(starts)
    high = jnp.where(pad == 1, jnp.minimum(place, filled - 1), place) + 1
    cross_low = jnp.where(pad == 0, 0, of_token(memory_starts))
    cross_high = jnp.where(pad == 0, slots, of_token(memory_stops))
    depth = of_token(depths)
    keep = depth == 2

    away = jnp.abs(starts[1:] - length // 2)
    cut = jnp.min(jnp.where(away == jnp.min(away), starts[1:], length))
    owned = jnp.where(core == 0, place < cut, place >= cut)
    blocks = length // BLOCK
    begin = jnp.where(core == 0, 0, cut // BLOCK)
    end = jnp.where(core == 0, (cut + BLOCK - 1) // BLOCK, blocks)
    wide = length * 5 // 8

    def outside(from_place, to_place):
        return jnp.where(core == 0, to_place > wide, from_place < length - wide)

    def span(lows, highs, used):
        lows = jnp.min(jnp.where(used, lows, length).reshape(blocks, BLOCK), axis=1)
        highs = jnp.max(jnp.where(used, highs, 0).reshape(blocks, BLOCK), axis=1)
        return jnp.minimum(lows, highs) // BLOCK, (highs + BLOCK - 1) // BLOCK

    def steer(used):
        self_span, cross_span = span(low, high, used), span(cross_low, cross_high, used)
        flag_t = outside(begin * BLOCK, end * BLOCK)
        flag_m = outside(
            jnp.min(jnp.where(used, cross_low, slots)), jnp.max(jnp.where(used, cross_high, 0))
        )
        head = jnp.stack([core, flag_t, flag_m, begin, end, 0, 0, 0]).astype(jnp.int32)
        return jnp.concatenate([head, *self_span, *cross_span]).astype(jnp.int32)

    cols = jnp.pad(jnp.stack([low, high, cross_low, cross_high], axis=1), ((0, 0), (0, 4)))
    info = jnp.pad(jnp.stack([low, high, cross_low, cross_high]), ((0, 4), (0, 0)))
    onward = jnp.broadcast_to(keep.astype(f32)[:, None], (length, 8))
    counted = pad.astype(f32) * owned.astype(f32)
    frows = jnp.stack([counted, (depth == 1).astype(f32), jnp.ones_like(counted)])
    frows = jnp.pad(frows, ((0, 5), (0, 0)))
    return steer(owned), steer(owned & keep), cols, info, onward, frows, owned


def row_forward_backward(core, x, mem, cotangent, w, gains, ints, sentences):
    first, second, cols, info, keep, frows, owned = plan(core, *ints)
    length, width = x.shape
    every = jnp.ones_like(keep)
    cotangent = jnp.where(owned[:, None], cotangent, 0).astype(bf16)
    *saved0, zero = attention_forward(first, x, mem, w[0], gains[0], every, cols, "attend_zero")
    one, halt0, exit0 = dense_forward(first, zero, w[1], gains[1], frows, sentences, "dense_one")
    *saved2, two = attention_forward(second, one, mem, w[2], gains[2], keep, cols, "attend_two")
    dtwo, dw3, dgain3, states, halt1, exit1 = dense_backward(
        first, two, w[3], gains[3], keep, frows, cotangent, sentences, True, "dense_three"
    )
    nothing = jnp.zeros((length, width), f32)
    done, dmem, dw2, dgain2 = attention_backward(
        second, one, mem, w[2], gains[2], keep, info, saved2, dtwo, nothing, "attend_two_back"
    )
    dzero, dw1, dgain1 = dense_backward(
        first, zero, w[1], gains[1], every, frows, done, sentences, False, "dense_one_back"
    )
    dx, dmem, dw0, dgain0 = attention_backward(
        first, x, mem, w[0], gains[0], every, info, saved0, dzero, dmem, "attend_zero_back"
    )
    halt = jnp.where(owned[None, :], jnp.stack([halt0[0], halt1[0]]), 0)
    dgains = jnp.stack(
        [dgain0, jnp.concatenate([dgain1, exit0]), dgain2, jnp.concatenate([dgain3, exit1])]
    )
    states = jnp.where(owned[:, None], states, 0)
    dx = jnp.where(owned[:, None], dx, 0)
    return states, halt, dx, dmem, [dw0, dw1, dw2, dw3], dgains


def swap_cores(value):
    count = lax.axis_size("dp")
    return lax.ppermute(value, "dp", [(i, i ^ 1) for i in range(count)])


def local(
    states_in, memory, cotangent, weight_bank, gain_bank, segments, pad_mask, memory_segments, memory_mask, exit_depths
):
    section = lax.axis_index("section")
    sections = lax.axis_size("section")
    core = lax.axis_index("dp") % 2
    micro = states_in.shape[0]
    sentences = exit_depths.shape[1]
    holder = section // micro == core

    def whole_row(shares):
        gathered = lax.all_gather(shares, "section", axis=2, tiled=True)
        own = lax.dynamic_index_in_dim(gathered, section % micro, 0, keepdims=False)
        return jnp.where(holder, own, swap_cores(own))

    def row_of(ints):
        own = lax.dynamic_index_in_dim(ints, section % micro, 0, keepdims=False)
        return jnp.where(holder, own, swap_cores(own))

    x, mem, top = whole_row(states_in), whole_row(memory), whole_row(cotangent)
    ints = [row_of(t) for t in (segments, pad_mask, memory_segments, memory_mask, exit_depths)]
    w = lax.all_gather(weight_bank[0], "section")
    gains = lax.all_gather(gain_bank[0], "section")
    states, halt, dx, dmem, dw, dgains = row_forward_backward(
        core, x, mem, top, [w[i] for i in range(sections)], gains, ints, sentences
    )

    def to_shares(value, axis):
        value = value.astype(bf16)
        both = value.astype(f32) + swap_cores(value).astype(f32)
        both = jnp.where(holder, both, 0).astype(bf16)
        slots = jnp.stack([jnp.where(section % micro == i, both, 0) for i in range(micro)])
        return lax.psum_scatter(slots, "section", scatter_dimension=axis + 1, tiled=True)

    bank = lax.psum_scatter(jnp.stack(dw), "section", scatter_dimension=0, tiled=True)
    bank = lax.psum(bank.astype(f32), "dp")
    gain_sum = lax.psum_scatter(dgains, "section", scatter_dimension=0, tiled=True)
    gain_sum = lax.psum(gain_sum, "dp")
    return (
        to_shares(states, 1),
        to_shares(halt, 1).astype(f32),
        to_shares(dx, 1).astype(f32),
        to_shares(dmem, 1).astype(f32),
        bank,
        gain_sum,
    )


def solution(mesh):
    rows = P("dp", None, "section")
    return jax.shard_map(
        local,
        mesh=mesh,
        in_specs=(
            rows, rows, rows, P("section", None, None, None), P("section", None, None),
            P("dp", None), P("dp", None), P("dp", None), P("dp", None), P("dp", None),
        ),
        out_specs=(rows, rows, rows, rows, P("section", None, None, None), P("section", None, None)),
        check_vma=False,
    )
```

```python
import functools

import jax
import jax.numpy as jnp
from jax import lax
from jax.experimental import pallas as pl
from jax.experimental.pallas import tpu as pltpu
from jax.sharding import PartitionSpec as P

HEADS = 8
EPS = 1e-06
BLOCK = 128
NEG = -1e30

bf16 = jnp.bfloat16
f32 = jnp.float32

CORE, FLAG_T, FLAG_M, FIRST, LAST = 0, 1, 2, 3, 4
SELF_LO, SELF_HI, CROSS_LO, CROSS_HI = 8, 16, 24, 32
META = 40


def dot(left, right):
    return jnp.dot(left, right, preferred_element_type=f32)


def dot_nt(left, right):
    return lax.dot_general(left, right, (((1,), (1,)), ((), ())), preferred_element_type=f32)


def dot_tn(left, right):
    return lax.dot_general(left, right, (((0,), (0,)), ((), ())), preferred_element_type=f32)


def exact_nt(left, right):
    return lax.dot_general(
        left, right, (((1,), (1,)), ((), ())), precision=lax.Precision.HIGHEST, preferred_element_type=f32
    )


def exact(left, right):
    return jnp.dot(left, right, precision=lax.Precision.HIGHEST, preferred_element_type=f32)


def norm(x, gain):
    return x * lax.rsqrt(jnp.mean(x * x, axis=-1, keepdims=True) + EPS) * gain


def norm_back(x, gain, grad):
    rate = lax.rsqrt(jnp.mean(x * x, axis=-1, keepdims=True) + EPS)
    scaled = x * rate
    inner = grad * gain
    grad_x = rate * (inner - scaled * jnp.mean(inner * scaled, axis=-1, keepdims=True))
    return grad_x, jnp.sum(grad * scaled, axis=0, keepdims=True)


GELU_A = 0.7978845608028654
GELU_B = 0.044715


def gelu(z):
    return 0.5 * z * (1.0 + jnp.tanh(GELU_A * (z + GELU_B * z * z * z)))


def gelu_both(z):
    square = z * z
    bend = jnp.tanh(GELU_A * z * (1.0 + GELU_B * square))
    half = 0.5 * (1.0 + bend)
    slope = half + 0.5 * z * (1.0 - bend * bend) * (GELU_A * (1.0 + 3.0 * GELU_B * square))
    return z * half, slope


def windows(meta, length):
    wide = length * 5 // 8
    slim = length - wide
    core = meta[CORE]
    return (
        pl.ds(pl.multiple_of(core * slim, BLOCK), wide),
        pl.ds(pl.multiple_of((1 - core) * wide, BLOCK), slim),
    )


def over(meta, flag, length, work):
    main, other = windows(meta, length)
    work(main, True)

    @pl.when(meta[flag] == 1)
    def _():
        work(other, False)


def block(i):
    return pl.ds(pl.multiple_of(i * BLOCK, BLOCK), BLOCK)


def pair_lanes(p):
    return slice(p * BLOCK, (p + 1) * BLOCK)


def two_heads(tile, lane):
    zero = jnp.zeros_like(tile)
    return jnp.concatenate([jnp.where(lane < 64, tile, zero), jnp.where(lane < 64, zero, tile)], axis=0)


def attend_tiles(meta, lo_at, hi_at, low_col, q, k, v, o, lse, cols, scores, peaks, sums):
    pairs = q.shape[1] // BLOCK

    def one_block(i, _):
        first, last = meta[lo_at + i], meta[hi_at + i]

        @pl.when(last > first)
        def _():
            rows = block(i)
            lane = lax.broadcasted_iota(jnp.int32, (BLOCK, BLOCK), 1)
            low = cols[rows, low_col : low_col + 1]
            high = cols[rows, low_col + 1 : low_col + 2]
            peaks[...] = jnp.full(peaks.shape, -jnp.inf, f32)
            sums[...] = jnp.zeros(sums.shape, f32)

            def score(j, _):
                place = lane + j * BLOCK
                bias = jnp.where((place >= low) & (place < high), 0.0, NEG)
                bias = jnp.concatenate([bias, bias], axis=1)
                for p in range(pairs):
                    keys = two_heads(k[block(j), pair_lanes(p)], lane)
                    tile = dot_nt(q[rows, pair_lanes(p)], keys) + bias
                    scores[j - first, p] = tile
                    peaks[p] = jnp.maximum(peaks[p], tile)
                return 0

            lax.fori_loop(first, last, score, 0)
            for p in range(pairs):
                for e in range(2):
                    lanes = slice(e * BLOCK, (e + 1) * BLOCK)
                    top = jnp.max(peaks[p, :, lanes], axis=-1, keepdims=True)
                    peaks[p, :, lanes] = jnp.broadcast_to(top, (BLOCK, BLOCK))

            def mix(j, _):
                ones = jnp.where(lane < 64, 1.0, 0.0).astype(bf16)
                marks = jnp.concatenate([ones, 1 - ones], axis=0)
                for p in range(pairs):
                    weights = jnp.exp(scores[j - first, p] - peaks[p]).astype(bf16)
                    values = two_heads(v[block(j), pair_lanes(p)], lane)
                    sums[p] += dot(weights, jnp.concatenate([values, marks], axis=1))
                return 0

            lax.fori_loop(first, last, mix, 0)
            gathered = jnp.zeros((BLOCK, BLOCK), f32)
            for p in range(pairs):
                total = sums[p, :, BLOCK:]
                o[rows, pair_lanes(p)] = (sums[p, :, :BLOCK] / total).astype(bf16)
                top = jnp.where(lane < 64, peaks[p, :, :BLOCK], peaks[p, :, BLOCK:])
                gathered = jnp.where(lane % 64 // 16 == p, top + jnp.log(total), gathered)
            turned = gathered.T
            for p in range(pairs):
                for e in range(2):
                    lse[2 * p + e : 2 * p + e + 1, rows] = turned[e * 64 + p * 16 : e * 64 + p * 16 + 1, :]

        return 0

    lax.fori_loop(meta[FIRST], meta[LAST], one_block, 0)


def attend_tiles_back(
    meta, lo_at, hi_at, low_row, q, k, v, lse, delta, do, info, dq, dk, dv, both_q, both_o, dq_sum
):
    pairs = q.shape[1] // BLOCK

    def one_block(i, _):
        first, last = meta[lo_at + i], meta[hi_at + i]

        @pl.when(last > first)
        def _():
            rows = block(i)
            lane = lax.broadcasted_iota(jnp.int32, (BLOCK, BLOCK), 1)
            slot = lax.broadcasted_iota(jnp.int32, (BLOCK, BLOCK), 0)
            low = info[low_row : low_row + 1, rows]
            high = info[low_row + 1 : low_row + 2, rows]
            dq_sum[...] = jnp.zeros(dq_sum.shape, f32)
            for p in range(pairs):
                both_q[p] = two_heads(q[rows, pair_lanes(p)], lane)
                both_o[p] = two_heads(do[rows, pair_lanes(p)], lane)

            def tile(j, _):
                place = slot + j * BLOCK
                bias = jnp.where((place >= low) & (place < high), 0.0, NEG)
                bias = jnp.concatenate([bias, bias], axis=1)
                for p in range(pairs):
                    lanes = pair_lanes(p)
                    keys, values = k[block(j), lanes], v[block(j), lanes]
                    queries, grads = both_q[p], both_o[p]
                    log_total = jnp.concatenate([lse[2 * p : 2 * p + 1, rows], lse[2 * p + 1 : 2 * p + 2, rows]], axis=1)
                    change = jnp.concatenate([delta[2 * p : 2 * p + 1, rows], delta[2 * p + 1 : 2 * p + 2, rows]], axis=1)
                    probs = jnp.exp(dot_nt(keys, queries) + bias - log_total)
                    grad_scores = (probs * (dot_nt(values, grads) - change)).astype(bf16)
                    dv[block(j), lanes] += dot(probs.astype(bf16), grads)
                    dk[block(j), lanes] += dot(grad_scores, queries)
                    mixed = dot_tn(grad_scores, keys)
                    dq_sum[:, lanes] += jnp.where(lane < 64, mixed[:BLOCK], mixed[BLOCK:])
                return 0

            lax.fori_loop(first, last, tile, 0)
            dq[rows, :] = (dq_sum[...] * 0.125).astype(bf16)

        return 0

    lax.fori_loop(meta[FIRST], meta[LAST], one_block, 0)


def attention_forward_kernel(
    meta, w, x, mem, gain, go, cols, q1, k1, v1, o1, l1, mid, q2, k2, v2, o2, l2, out, scores, peaks, sums
):
    length = x.shape[0]

    def self_in(rows, _):
        a = norm(x[rows, :].astype(f32), gain[0:1, :]).astype(bf16)
        q1[rows, :] = (dot(a, w[0]) * 0.125).astype(bf16)
        k1[rows, :] = dot(a, w[1]).astype(bf16)
        v1[rows, :] = dot(a, w[2]).astype(bf16)
        o1[rows, :] = jnp.zeros((rows.size, x.shape[1]), bf16)

    over(meta, FLAG_T, length, self_in)

    def memory_in(rows, _):
        source = mem[rows, :]
        k2[rows, :] = dot(source, w[5]).astype(bf16)
        v2[rows, :] = dot(source, w[6]).astype(bf16)

    over(meta, FLAG_M, length, memory_in)
    l1[...] = jnp.zeros(l1.shape, f32)
    l2[...] = jnp.zeros(l2.shape, f32)
    attend_tiles(meta, SELF_LO, SELF_HI, 0, q1, k1, v1, o1, l1, cols, scores, peaks, sums)

    def cross_in(rows, _):
        state = x[rows, :].astype(f32) + go[rows, 0:1] * dot(o1[rows, :], w[3])
        mid[rows, :] = state
        a = norm(state, gain[1:2, :]).astype(bf16)
        q2[rows, :] = (dot(a, w[4]) * 0.125).astype(bf16)
        o2[rows, :] = jnp.zeros((rows.size, x.shape[1]), bf16)

    over(meta, FLAG_T, length, cross_in)
    attend_tiles(meta, CROSS_LO, CROSS_HI, 2, q2, k2, v2, o2, l2, cols, scores, peaks, sums)

    def finish(rows, _):
        out[rows, :] = (mid[rows, :] + go[rows, 0:1] * dot(o2[rows, :], w[7])).astype(bf16)

    over(meta, FLAG_T, length, finish)


def attention_backward_kernel(
    entry, meta, w, x, mem, gain, go, info, cols, q1, k1, v1, o1, l1, mid, q2, k2, v2, o2, l2, dh, *rest,
):
    if entry:
        dmem_in, *rest = rest
    attention_backward_body(
        entry, dmem_in if entry else None,
        meta, w, x, mem, gain, go, info, cols, q1, k1, v1, o1, l1, mid, q2, k2, v2, o2, l2, dh, *rest,
    )


def attention_backward_body(
    entry, dmem_in, meta, w, x, mem, gain, go, info, cols, q1, k1, v1, o1, l1, mid, q2, k2, v2, o2, l2, dh,
    dx, dmem, dw, dgain,
    dstate, do, dq, dk, dv, dkb, dvb, delta, both_q, both_o, dq_sum, acc, heads,
):
    length, width = x.shape
    row_of = lax.broadcasted_iota(jnp.int32, (HEADS, width), 0)
    lane_of = lax.broadcasted_iota(jnp.int32, (HEADS, width), 1)
    heads[...] = (lane_of // (width // HEADS) == row_of).astype(bf16)
    dk[...] = jnp.zeros(dk.shape, f32)
    dv[...] = jnp.zeros(dv.shape, f32)
    delta[...] = jnp.zeros(delta.shape, f32)

    def weight_grad(index, flag, left, right):
        def part(rows, fresh):
            term = dot_tn(left(rows), right(rows))
            acc[...] = term if fresh else acc[...] + term

        over(meta, flag, length, part)
        dw[index] = acc[...].astype(bf16)

    def begin(grad_of, o, out_weight):
        def part(rows, _):
            dy = (go[rows, 0:1] * grad_of(rows)).astype(bf16)
            grad = dot_nt(dy, w[out_weight]).astype(bf16)
            do[rows, :] = grad
            product = grad.astype(f32) * o[rows, :].astype(f32)
            high = product.astype(bf16)
            rest = (product - high.astype(f32)).astype(bf16)
            delta[:, rows] = dot_nt(heads[...], high) + dot_nt(heads[...], rest)
            dq[rows, :] = jnp.zeros((rows.size, width), bf16)

        over(meta, FLAG_T, length, part)
        weight_grad(out_weight, FLAG_T, lambda rows: o[rows, :], lambda rows: (go[rows, 0:1] * grad_of(rows)).astype(bf16))

    def top_grad(rows):
        return dh[rows, :].astype(f32)

    begin(top_grad, o2, 7)
    attend_tiles_back(
        meta, CROSS_LO, CROSS_HI, 2, q2, k2, v2, l2, delta, do, info, dq, dk, dv, both_q, both_o, dq_sum
    )

    dmem[...] = dmem_in[...] if entry else jnp.zeros(dmem.shape, bf16)

    def memory_out(rows, _):
        grad_k, grad_v = dk[rows, :].astype(bf16), dv[rows, :].astype(bf16)
        dkb[rows, :] = grad_k
        dvb[rows, :] = grad_v
        term = dot_nt(grad_k, w[5]) + dot_nt(grad_v, w[6])
        dmem[rows, :] = (dmem[rows, :].astype(f32) + term).astype(bf16)

    over(meta, FLAG_M, length, memory_out)
    weight_grad(5, FLAG_M, lambda rows: mem[rows, :], lambda rows: dkb[rows, :])
    weight_grad(6, FLAG_M, lambda rows: mem[rows, :], lambda rows: dvb[rows, :])

    def cross_out(rows, fresh):
        state = mid[rows, :]
        grad_x, grad_gain = norm_back(state, gain[1:2, :], dot_nt(dq[rows, :], w[4]))
        dstate[rows, :] = top_grad(rows) + grad_x
        dgain[1:2, :] = grad_gain if fresh else dgain[1:2, :] + grad_gain

    over(meta, FLAG_T, length, cross_out)
    weight_grad(4, FLAG_T, lambda rows: norm(mid[rows, :], gain[1:2, :]).astype(bf16), lambda rows: dq[rows, :])

    dk[...] = jnp.zeros(dk.shape, f32)
    dv[...] = jnp.zeros(dv.shape, f32)
    begin(lambda rows: dstate[rows, :], o1, 3)
    attend_tiles_back(
        meta, SELF_LO, SELF_HI, 0, q1, k1, v1, l1, delta, do, info, dq, dk, dv, both_q, both_o, dq_sum
    )

    if entry:
        dx[...] = jnp.zeros(dx.shape, bf16)

    def self_out(rows, fresh):
        grad_k, grad_v = dk[rows, :].astype(bf16), dv[rows, :].astype(bf16)
        dkb[rows, :] = grad_k
        dvb[rows, :] = grad_v
        da = dot_nt(dq[rows, :], w[0]) + dot_nt(grad_k, w[1]) + dot_nt(grad_v, w[2])
        grad_x, grad_gain = norm_back(x[rows, :].astype(f32), gain[0:1, :], da)
        value = dstate[rows, :] + grad_x
        if entry:
            value = jnp.where(cols[rows, 4:5] == 1, value, 0.0)
        dx[rows, :] = value.astype(bf16)
        dgain[0:1, :] = grad_gain if fresh else dgain[0:1, :] + grad_gain

    over(meta, FLAG_T, length, self_out)

    def normed(rows):
        return norm(x[rows, :].astype(f32), gain[0:1, :]).astype(bf16)

    weight_grad(0, FLAG_T, normed, lambda rows: dq[rows, :])
    weight_grad(1, FLAG_T, normed, lambda rows: dkb[rows, :])
    weight_grad(2, FLAG_T, normed, lambda rows: dvb[rows, :])


def exit_part(layer, vector, frows, rows, target_row, halt, exit_grad, fresh, sentences):
    factor = layer.shape[1] ** (-0.5)
    vectors = jnp.broadcast_to(vector, (8, layer.shape[1]))
    score = jax.nn.sigmoid(exact_nt(vectors, layer) * factor)
    halt[:, rows] = score
    weight = frows[0:1, rows] * (score - frows[target_row : target_row + 1, rows]) / sentences
    term = exact(weight, layer)[0:1] * factor
    exit_grad[...] = term if fresh else exit_grad[...] + term


def dense_forward_kernel(sentences, meta, w, x, gain, frows, out, halt, exit_grad):
    length = x.shape[0]
    parts = w.place.shape[0] // 2

    def part(rows, fresh):
        state = x[rows, :].astype(f32)
        a = norm(state, gain[0:1, :]).astype(bf16)
        branch = jnp.zeros(state.shape, f32)
        for j in range(parts):
            branch = branch + dot(gelu(dot(a, w[j])).astype(bf16), w[parts + j])
        layer = state + branch
        out[rows, :] = layer.astype(bf16)
        exit_part(layer, gain[1:2, :], frows, rows, 1, halt, exit_grad, fresh, sentences)

    over(meta, FLAG_T, length, part)


def dense_backward_kernel(sentences, final, meta, w, x, gain, go, frows, cols, dh, before, dx, dw, dgain, *rest):
    if final:
        out, halt, acc, exit_grad = rest
        out[...] = jnp.zeros(out.shape, bf16)
    else:
        (acc,) = rest
        dgain[1:2, :] = before[...]
    length, width = x.shape
    parts = w.place.shape[0] // 2

    def part(rows, fresh):
        grad_out = dh[rows, :].astype(f32)
        if final:
            grad_out = jnp.where(cols[rows, 4:5] == 1, grad_out, 0.0)
        state = x[rows, :].astype(f32)
        a = norm(state, gain[0:1, :]).astype(bf16)
        dy = (go[rows, 0:1] * grad_out).astype(bf16)
        branch = jnp.zeros(state.shape, f32)
        da = jnp.zeros(state.shape, f32)
        for j in range(parts):
            active, slope = gelu_both(dot(a, w[j]))
            active = active.astype(bf16)
            if final:
                branch = branch + dot(active, w[parts + j])
            dhidden = (slope * dot_nt(dy, w[parts + j])).astype(bf16)
            da = da + dot_nt(dhidden, w[j])
            up, down = dot_tn(a, dhidden), dot_tn(active, dy)
            acc[j] = up if fresh else acc[j] + up
            acc[parts + j] = down if fresh else acc[parts + j] + down
        grad_x, grad_gain = norm_back(state, gain[0:1, :], da)
        dx[rows, :] = (grad_out + grad_x).astype(bf16)
        dgain[0:1, :] = grad_gain if fresh else dgain[0:1, :] + grad_gain
        if final:
            layer = state + go[rows, 0:1] * branch
            out[rows, :] = jnp.where(cols[rows, 4:5] == 1, layer, 0.0).astype(bf16)
            exit_part(layer, gain[1:2, :], frows, rows, 2, halt, exit_grad, fresh, sentences)

    over(meta, FLAG_T, length, part)
    if final:
        dgain[1:2, :] = exit_grad[...]
        mine = frows[3:4, :] > 0.0
        halt[1:2, :] = jnp.where(mine, halt[1:2, :], 0.0)
        halt[0:1, :] = jnp.where(mine, before[0:1, :], 0.0)
    for j in range(2 * parts):
        dw[j] = acc[j].astype(bf16)


class Lazy:
    def __init__(self, bank, section, place, arrived):
        self.place, self.waiting = place, {}
        for j in range(place.shape[0]):
            copy = pltpu.make_async_copy(bank.at[section, j], place.at[j], arrived.at[j])
            copy.start()
            self.waiting[j] = copy

    def __getitem__(self, j):
        if j in self.waiting:
            self.waiting.pop(j).wait()
        return self.place[j]


ANY = pl.BlockSpec(memory_space=pl.ANY)
VMEM = pl.BlockSpec(memory_space=pltpu.VMEM)
SMEM = pl.BlockSpec(memory_space=pltpu.SMEM)


def run(kernel, section, outs, scratch, name, flops, meta, bank, *args):
    matrices = bank.shape[1:]

    def body(meta, bank, *refs):
        *refs, place, arrived = refs
        kernel(meta, Lazy(bank, section, place, arrived), *refs)

    return pl.pallas_call(
        body,
        out_shape=[jax.ShapeDtypeStruct(shape, dtype) for shape, dtype in outs],
        in_specs=[SMEM, ANY] + [VMEM] * len(args),
        out_specs=[VMEM] * len(outs),
        scratch_shapes=[pltpu.VMEM(shape, dtype) for shape, dtype in scratch]
        + [pltpu.VMEM(matrices, bf16), pltpu.SemaphoreType.DMA((matrices[0],))],
        compiler_params=pltpu.CompilerParams(vmem_limit_bytes=60 * 2**20),
        cost_estimate=pl.CostEstimate(flops=flops, bytes_accessed=20 * 2**20, transcendentals=0),
        name=name,
    )(meta, bank, *args)


def attention_forward(meta, bank, section, x, mem, gain, go, cols, name):
    length, width = x.shape
    wide = ((length, width), bf16)
    logs = ((HEADS, length), f32)
    pairs = width // BLOCK
    tile = ((pairs, BLOCK, 2 * BLOCK), f32)
    return run(
        attention_forward_kernel, section,
        [wide, wide, wide, wide, logs, ((length, width), f32), wide, wide, wide, wide, logs, wide],
        [((length // BLOCK,) + tile[0], f32), tile, tile],
        name, 6 * 10**9, meta, bank, x, mem, gain, go, cols,
    )


def attention_backward(meta, bank, section, x, mem, gain, go, info, cols, saved, dh, dmem, name):
    length, width = x.shape
    pairs = width // BLOCK
    wide, full = ((length, width), bf16), ((length, width), f32)
    both = ((pairs, 2 * BLOCK, BLOCK), bf16)
    return run(
        functools.partial(attention_backward_kernel, len(dmem) > 0), section,
        [wide, wide, (bank.shape[1:], bf16), ((2, width), f32)],
        [full, wide, wide, full, full, wide, wide, ((HEADS, length), f32), both, both,
         ((BLOCK, width), f32), ((width, width), f32), ((HEADS, width), bf16)],
        name, 12 * 10**9, meta, bank, x, mem, gain, go, info, cols, *saved, dh, *dmem,
    )


def dense_forward(meta, bank, section, x, gain, frows, sentences, name):
    length, width = x.shape
    return run(
        functools.partial(dense_forward_kernel, sentences), section,
        [((length, width), bf16), ((8, length), f32), ((1, width), f32)], [],
        name, 4 * 10**9, meta, bank, x, gain, frows,
    )


def dense_backward(meta, bank, section, x, gain, go, frows, cols, dh, before, sentences, final, name):
    length, width = x.shape
    outs = [((length, width), bf16), (bank.shape[1:], bf16), ((2, width), f32)]
    scratch = [(bank.shape[1:], f32)]
    if final:
        outs += [((length, width), bf16), ((8, length), f32)]
        scratch += [((1, width), f32)]
    return run(
        functools.partial(dense_backward_kernel, sentences, final), section, outs, scratch,
        name, 8 * 10**9, meta, bank, x, gain, go, frows, cols, dh, before,
    )


def plan(core, seg, pad, mseg, mmask, depths):
    length, slots, sentences = seg.shape[0], mseg.shape[0], depths.shape[0]
    numbers = jnp.arange(sentences)
    place = jnp.arange(length)
    mine = (seg[:, None] == numbers[None, :]).astype(jnp.int32)

    def of_token(table):
        return jnp.sum(mine * table[None, :], axis=1)

    starts = jnp.sum((seg[:, None] < numbers[None, :]).astype(jnp.int32), axis=0)
    filled = jnp.sum(pad)
    memory_starts = jnp.sum((mseg[:, None] < numbers[None, :]).astype(jnp.int32), axis=0)
    memory_stops = jnp.sum((mseg[:, None] <= numbers[None, :]).astype(jnp.int32), axis=0)
    memory_stops = jnp.minimum(memory_stops, jnp.sum(mmask))
    low = of_token(starts)
    high = jnp.where(pad == 1, jnp.minimum(place, filled - 1), place) + 1
    cross_low = jnp.where(pad == 0, 0, of_token(memory_starts))
    cross_high = jnp.where(pad == 0, slots, of_token(memory_stops))
    depth = of_token(depths)
    keep = depth == 2

    away = jnp.abs(starts[1:] - length // 2)
    cut = jnp.min(jnp.where(away == jnp.min(away), starts[1:], length))
    owned = jnp.where(core == 0, place < cut, place >= cut)
    blocks = length // BLOCK
    begin = jnp.where(core == 0, 0, cut // BLOCK)
    end = jnp.where(core == 0, (cut + BLOCK - 1) // BLOCK, blocks)
    wide = length * 5 // 8

    def outside(from_place, to_place):
        return jnp.where(core == 0, to_place > wide, from_place < length - wide)

    def span(lows, highs, used):
        lows = jnp.min(jnp.where(used, lows, length).reshape(blocks, BLOCK), axis=1)
        highs = jnp.max(jnp.where(used, highs, 0).reshape(blocks, BLOCK), axis=1)
        return jnp.minimum(lows, highs) // BLOCK, (highs + BLOCK - 1) // BLOCK

    def steer(used):
        self_span, cross_span = span(low, high, used), span(cross_low, cross_high, used)
        flag_t = outside(begin * BLOCK, end * BLOCK)
        flag_m = outside(
            jnp.min(jnp.where(used, cross_low, slots)), jnp.max(jnp.where(used, cross_high, 0))
        )
        head = jnp.stack([core, flag_t, flag_m, begin, end, 0, 0, 0]).astype(jnp.int32)
        return jnp.concatenate([head, *self_span, *cross_span]).astype(jnp.int32)

    cols = jnp.stack([low, high, cross_low, cross_high, owned.astype(jnp.int32)], axis=1)
    cols = jnp.pad(cols, ((0, 0), (0, 3)))
    info = jnp.pad(jnp.stack([low, high, cross_low, cross_high]), ((0, 4), (0, 0)))
    onward = jnp.broadcast_to(keep.astype(f32)[:, None], (length, 8))
    counted = pad.astype(f32) * owned.astype(f32)
    frows = jnp.stack([counted, (depth == 1).astype(f32), jnp.ones_like(counted), owned.astype(f32)])
    frows = jnp.pad(frows, ((0, 4), (0, 0)))
    return steer(owned), steer(owned & keep), cols, info, onward, frows


def row_forward_backward(core, x, mem, cotangent, bank, gains, ints, sentences):
    first, second, cols, info, keep, frows = plan(core, *ints)
    every = jnp.ones_like(keep)
    *saved0, zero = attention_forward(first, bank, 0, x, mem, gains[0], every, cols, "attend_zero")
    one, halt, exit0 = dense_forward(first, bank, 1, zero, gains[1], frows, sentences, "dense_one")
    *saved2, two = attention_forward(second, bank, 2, one, mem, gains[2], keep, cols, "attend_two")
    dtwo, dw3, dgain3, states, halt = dense_backward(
        first, bank, 3, two, gains[3], keep, frows, cols, cotangent, halt, sentences, True, "dense_three"
    )
    done, dmem, dw2, dgain2 = attention_backward(
        second, bank, 2, one, mem, gains[2], keep, info, cols, saved2, dtwo, (), "attend_two_back"
    )
    dzero, dw1, dgain1 = dense_backward(
        first, bank, 1, zero, gains[1], every, frows, cols, done, exit0, sentences, False, "dense_one_back"
    )
    dx, dmem, dw0, dgain0 = attention_backward(
        first, bank, 0, x, mem, gains[0], every, info, cols, saved0, dzero, (dmem,), "attend_zero_back"
    )
    return states, halt, dx, dmem, [dw0, dw1, dw2, dw3], [dgain0, dgain1, dgain2, dgain3]


MESH = pl.DeviceIdType.MESH
ANY = pl.BlockSpec(memory_space=pl.ANY)


def neighbours():
    s, d = lax.axis_index("section"), lax.axis_index("dp")
    across = [(s + 1 - 2 * (s % 2), d), ((s + 2) % 4, d), (3 - s, d)]
    layer = d // 2
    along = (s, d + 2 - 4 * (layer % 2))
    sibling = (s, d + 1 - 2 * (d % 2))
    return s, d, across, along, sibling


def greet(devices):
    barrier = pltpu.get_barrier_semaphore()
    for device in devices:
        pl.semaphore_signal(barrier, inc=1, device_id=device, device_id_type=MESH)
    pl.semaphore_wait(barrier, len(devices))


SUBS = 4


def gather_kernel(
    states, memory, cotangent, bank, gains, seg, pad, mseg, mmask, depths,
    x, mem, top, weights, gains_all, seg2, pad2, mseg2, mmask2, depths2,
    staging, send, recv, home,
):
    s, d, across, along, sibling = neighbours()
    core = d % 2
    parity = (d // 2) % 2
    greet(across + [along, sibling])
    started = []
    locals_ = []
    count = [0, 0]

    def push(src, dst, device):
        i = count[0]
        count[0] += 1
        copy = pltpu.make_async_remote_copy(src, dst, send.at[i], recv.at[i], device_id=device, device_id_type=MESH)
        return copy

    def go(src, dst, device):
        copy = push(src, dst, device)
        copy.start()
        started.append(copy)
        return copy

    def keep(src, dst):
        i = count[1]
        count[1] += 1
        copy = pltpu.make_async_copy(src, dst, home.at[i])
        return copy

    shares = states.shape[2]
    chips = [s] + [a[0] for a in across]
    sent_inputs, own_inputs = [], []
    for source, whole in ((states, x), (memory, mem), (cotangent, top)):
        for rel in range(4):
            target = chips[rel]
            mine = target // 2 == core
            dst = whole.at[:, pl.ds(pl.multiple_of(s * shares, shares), shares)]
            src = source.at[target % 2]
            if rel == 0:
                copy = keep(src, dst)
                own_inputs.append(copy)
            else:
                copy = push(src, dst, across[rel - 1])
                sent_inputs.append((copy, whole, rel))
            pl.when(mine)(copy.start)
    small = [go(source, whole.at[core], sibling)
             for source, whole in ((seg, seg2), (pad, pad2), (mseg, mseg2), (mmask, mmask2), (depths, depths2))]
    small += [go(gains, gains_all.at[s], device) for device in across]
    for source, whole in ((seg, seg2), (pad, pad2), (mseg, mseg2), (mmask, mmask2), (depths, depths2)):
        copy = keep(source, whole.at[core])
        copy.start()
        locals_.append(copy)
    copy = keep(gains, gains_all.at[s])
    copy.start()
    locals_.append(copy)

    span = bank.shape[0]
    half = span // 2
    third = half // 3 // (16 * SUBS) * (16 * SUBS)
    first = half - 2 * third
    sub0, sub1 = first // SUBS, third // SUBS

    def rows(section, part, i):
        at = section * span + core * half
        size = sub0 if part == 0 else sub1
        if part == 0:
            at = at + i * size
        elif part == 1:
            at = at + first + parity * third + i * size
        else:
            at = at + first + (1 - parity) * third + i * size
        return weights.at[pl.ds(pl.multiple_of(at, 16), size)]

    def own_rows(part, i):
        size = sub0 if part == 0 else sub1
        at = core * half + (i * size if part == 0 else first + parity * third + i * size)
        return bank.at[pl.ds(pl.multiple_of(at, 16), size)]

    direct = {}
    for part in (1, 0):
        for i in range(SUBS):
            for k in range(2):
                direct[k, part, i] = go(own_rows(part, i), rows(s, part, i), across[k])
    lift = keep(bank, staging)
    lift.start()
    drop = keep(staging, weights.at[pl.ds(pl.multiple_of(s * span, span), span)])

    holder = s // 2 == core
    handed = []
    for n, (source, whole) in enumerate(((states, x), (memory, mem), (cotangent, top))):
        for rel in range(4):
            lanes = whole.at[:, pl.ds(pl.multiple_of(chips[rel] * shares, shares), shares)]
            copy = push(lanes, lanes, sibling)
            handed.append(copy)
            arrived = own_inputs[n] if rel == 0 else sent_inputs[n * 3 + rel - 1][0]

            def hand(copy=copy, arrived=arrived, rel=rel):
                if rel == 0:
                    arrived.wait()
                else:
                    arrived.wait_recv()
                copy.start()

            pl.when(holder)(hand)

    lift.wait()
    drop.start()
    locals_.append(drop)
    far = {}
    lifted = {}
    passed = []

    def arrive(copy, section, part, i):
        copy.wait_recv()
        passed.append(go(rows(section, part, i), rows(section, part, i), sibling))

    for i in range(SUBS):
        arrive(direct[0, 1, i], chips[1], 1, i)
        far[1, i] = go(rows(chips[1], 1, i), rows(chips[1], 1, i), across[1])
        lifted[1, i] = go(rows(chips[1], 1, i), rows(chips[1], 1, i), along)
        arrive(direct[1, 1, i], chips[2], 1, i)
        lifted[2, i] = go(rows(chips[2], 1, i), rows(chips[2], 1, i), along)
    for i in range(SUBS):
        arrive(direct[1, 0, i], chips[2], 0, i)
        far[0, i] = go(rows(chips[2], 0, i), rows(chips[2], 0, i), across[0])
        arrive(direct[0, 0, i], chips[1], 0, i)
    for i in range(SUBS):
        arrive(far[1, i], chips[3], 1, i)
        lifted[3, i] = go(rows(chips[3], 1, i), rows(chips[3], 1, i), along)
    for i in range(SUBS):
        arrive(far[0, i], chips[3], 0, i)
    for k in range(1, 4):
        for i in range(SUBS):
            arrive(lifted[k, i], chips[k], 2, i)
    for copy in passed + small:
        copy.wait_recv()
    for copy in handed:
        pl.when(jnp.logical_not(holder))(copy.wait_recv)
        pl.when(holder)(copy.wait_send)
    for (copy, whole, rel) in sent_inputs:
        pl.when(chips[rel] // 2 == core)(copy.wait_send)
    for copy in started:
        copy.wait_send()
    for copy in locals_:
        copy.wait()


def gather_all(states, memory, cotangent, bank, gains, ints):
    micro, length, shares = states.shape
    sections = lax.axis_size("section")
    width = shares * sections
    wide = jax.ShapeDtypeStruct((length, width), bf16)
    copies = 9 + 12 + 8 + 4 * SUBS + 2 * SUBS + 3 * SUBS + 9 * SUBS
    outs = [wide, wide, wide, jax.ShapeDtypeStruct((sections * bank.shape[0], width), bf16),
            jax.ShapeDtypeStruct((sections,) + gains.shape, f32)]
    outs += [jax.ShapeDtypeStruct((2,) + t.shape, t.dtype) for t in ints]
    return pl.pallas_call(
        gather_kernel,
        out_shape=outs,
        in_specs=[ANY] * 10,
        out_specs=[ANY] * 10,
        scratch_shapes=[pltpu.VMEM(bank.shape, bank.dtype), pltpu.SemaphoreType.DMA((copies,)), pltpu.SemaphoreType.DMA((copies,)),
                        pltpu.SemaphoreType.DMA((12,))],
        compiler_params=pltpu.CompilerParams(collective_id=0, has_side_effects=True, vmem_limit_bytes=16 * 2**20),
        name="gather_all",
    )(states, memory, cotangent, bank, gains, *ints)


GROUPS = 8


def add_rows(target, rows, *others):
    total = target[rows].astype(f32)
    for other, places in others:
        total = total + other[places].astype(f32)
    target[rows] = total.astype(bf16)


def reduce_kernel(
    dw0, dw1, dw2, dw3, gains, states, dx, dmem, halt,
    bank, gains_sum, states_out, dx_out, dmem_out, halt_out,
    own, other, first, second, left, right, total, full, mine, theirs, score, scores,
    gain_parts, send, recv, home,
):
    s, d, across, _, sibling = neighbours()
    core, layer = d % 2, d // 2
    chips = [s] + [a[0] for a in across]
    column = [(s, (layer + k) % 4 * 2 + core) for k in range(1, 4)]
    up, down = (s, d + 2), (s, d - 2)
    pair = (s, d + 2 - 4 * (layer % 2))
    jump = (s, (layer + 2) % 4 * 2 + core)
    holder = s // 2 == core
    greet(across + [sibling] + column)
    count = [0, 0]
    always, ends = [], []

    def push(src, dst, device):
        i = count[0]
        count[0] += 1
        return pltpu.make_async_remote_copy(src, dst, send.at[i], recv.at[i], device_id=device, device_id_type=MESH)

    def go(src, dst, device):
        copy = push(src, dst, device)
        copy.start()
        always.append(copy)
        return copy

    def fetch(src, dst):
        i = count[1]
        count[1] += 1
        copy = pltpu.make_async_copy(src, dst, home.at[i])
        return copy

    span = dw0.shape[0]
    half = span // 2
    quarter = half // 2
    piece = quarter // GROUPS
    grads = (dw0, dw1, dw2, dw3)

    def at(g, side):
        return side * quarter + g * piece

    loads, swaps = {}, {}
    for g in range(GROUPS):
        for t in range(4):
            for side in range(2):
                rows = pl.ds(at(g, side), piece)
                there = pl.ds(pl.multiple_of((1 - core) * half + at(g, side), piece), piece)
                here = pl.ds(pl.multiple_of(core * half + at(g, side), piece), piece)
                swaps[g, t, side] = go(grads[t].at[there], other.at[t, rows], sibling)
                loads[g, t, side] = fetch(grads[t].at[here], own.at[t, rows])
                loads[g, t, side].start()
        if g == 0:
            outs = ((states, states_out), (dx, dx_out), (dmem, dmem_out))
            given, taken = [], []
            for n, (source, _) in enumerate(outs):
                given.append(push(source, theirs.at[n], sibling))
                taken.append(fetch(source, mine.at[n]))
            given.append(push(halt, scores, sibling))
            taken.append(fetch(halt, score))
            for copy in given:
                pl.when(jnp.logical_not(holder))(copy.start)
            for copy in taken:
                pl.when(holder)(copy.start)

    gain_steps = [sibling, across[0], across[1], pair, jump]
    gain_parts[0] = gains[...]
    gain_copies = []

    def gain_step(k):
        if k > 0:
            gain_copies[-1].wait_recv()
            gain_parts[2 * k] = gain_parts[2 * k - 2] + gain_parts[2 * k - 1]
        if k < len(gain_steps):
            gain_copies.append(go(gain_parts.at[2 * k], gain_parts.at[2 * k + 1], gain_steps[k]))
        else:
            gains_sum[...] = gain_parts[2 * k]

    step1, step2, rs, ag = {}, {}, {}, {}

    def plane_first(g):
        for t in range(4):
            for side in range(2):
                swaps[g, t, side].wait_recv()
                loads[g, t, side].wait()
                rows = pl.ds(at(g, side), piece)
                add_rows(own, (t, rows), (other, (t, rows)))
        for side in range(2):
            rows = pl.ds(at(g, side), piece)
            for n, rel in enumerate((3, 1 + side)):
                step1[g, side, n] = go(own.at[chips[rel], rows], first.at[g, side, n], across[side])

    def plane_second(g):
        for side in range(2):
            rows = pl.ds(at(g, side), piece)
            for n, rel in enumerate((2 - side, 0)):
                step1[g, side, n].wait_recv()
                add_rows(own, (chips[rel], rows), (first, (g, side, n)))
                if n == 0:
                    step2[g, side] = go(own.at[chips[rel], rows], second.at[g, side], across[1 - side])

    def plane_third(g):
        for side in range(2):
            step2[g, side].wait_recv()
            rows = pl.ds(at(g, side), piece)
            value = own[s, rows].astype(f32) + second[g, side].astype(f32)
            total[g, pl.ds(side * piece, piece)] = value.astype(bf16)

    wide = 2 * piece
    shard = wide // 4

    def span_of(k0, k1):
        return pl.ds(k0 * shard, (k1 - k0) * shard)

    def share(kind, g, low, high, src, dst, device):
        return push(src.at[g, span_of(low, high)], dst.at[g, span_of(low, high)], device)

    def line_sums(g):
        for z in range(3):
            rs[g, "up", z] = share("up", g, z + 1, 4, total, right, up)
            rs[g, "down", z + 1] = share("down", g, 0, z + 1, total, left, down)
        for k in range(4):
            for z in range(k, 3):
                ag[g, "up", z, k] = push(full.at[g, span_of(k, k + 1)], full.at[g, span_of(k, k + 1)], up)
            for z in range(1, k + 1):
                ag[g, "down", z, k] = push(full.at[g, span_of(k, k + 1)], full.at[g, span_of(k, k + 1)], down)

    def at_layer(z, action):
        pl.when(layer == z)(action)

    def close(g, k, *others):
        value = total[g, span_of(k, k + 1)].astype(f32)
        for other_ in others:
            value = value + other_[g, span_of(k, k + 1)].astype(f32)
        full[g, span_of(k, k + 1)] = value.astype(bf16)

    def line_1(g):
        line_sums(g)
        at_layer(0, lambda: rs[g, "up", 0].start())
        at_layer(3, lambda: rs[g, "down", 3].start())

    def line_2(g):
        def second_layer():
            rs[g, "up", 0].wait_recv()
            add_rows(total, (g, span_of(2, 4)), (right, (g, span_of(2, 4))))
            rs[g, "up", 1].start()

        def third_layer():
            rs[g, "down", 3].wait_recv()
            add_rows(total, (g, span_of(0, 2)), (left, (g, span_of(0, 2))))
            rs[g, "down", 2].start()

        at_layer(1, second_layer)
        at_layer(2, third_layer)

    def line_3(g):
        def third_layer():
            rs[g, "up", 1].wait_recv()
            add_rows(total, (g, span_of(3, 4)), (right, (g, span_of(3, 4))))
            rs[g, "up", 2].start()
            close(g, 2, right, left)
            ag[g, "up", 2, 2].start()
            ag[g, "down", 2, 2].start()

        def second_layer():
            rs[g, "down", 2].wait_recv()
            add_rows(total, (g, span_of(0, 1)), (left, (g, span_of(0, 1))))
            rs[g, "down", 1].start()
            close(g, 1, right, left)
            ag[g, "up", 1, 1].start()
            ag[g, "down", 1, 1].start()

        at_layer(2, third_layer)
        at_layer(1, second_layer)

    def line_4(g):
        def bottom():
            rs[g, "down", 1].wait_recv()
            close(g, 0, left)
            ag[g, "up", 0, 0].start()

        def top():
            rs[g, "up", 2].wait_recv()
            close(g, 3, right)
            ag[g, "down", 3, 3].start()

        def second_layer():
            ag[g, "down", 2, 2].wait_recv()
            ag[g, "down", 1, 2].start()

        def third_layer():
            ag[g, "up", 1, 1].wait_recv()
            ag[g, "up", 2, 1].start()

        at_layer(0, bottom)
        at_layer(3, top)
        at_layer(1, second_layer)
        at_layer(2, third_layer)

    def line_5(g):
        def bottom():
            ag[g, "down", 1, 1].wait_recv()

        def top():
            ag[g, "up", 2, 2].wait_recv()

        def second_layer():
            ag[g, "up", 0, 0].wait_recv()
            ag[g, "up", 1, 0].start()

        def third_layer():
            ag[g, "down", 3, 3].wait_recv()
            ag[g, "down", 2, 3].start()

        at_layer(0, bottom)
        at_layer(3, top)
        at_layer(1, second_layer)
        at_layer(2, third_layer)

    def line_6(g):
        def bottom():
            ag[g, "down", 1, 2].wait_recv()

        def top():
            ag[g, "up", 2, 1].wait_recv()

        def second_layer():
            ag[g, "down", 2, 3].wait_recv()
            ag[g, "down", 1, 3].start()

        def third_layer():
            ag[g, "up", 1, 0].wait_recv()
            ag[g, "up", 2, 0].start()

        at_layer(0, bottom)
        at_layer(3, top)
        at_layer(1, second_layer)
        at_layer(2, third_layer)

    finals = {}

    def line_7(g):
        at_layer(0, lambda: ag[g, "down", 1, 3].wait_recv())
        at_layer(3, lambda: ag[g, "up", 2, 0].wait_recv())
        for side in range(2):
            here = pl.ds(pl.multiple_of(core * half + at(g, side), piece), piece)
            rows = full.at[g, pl.ds(side * piece, piece)]
            finals[g, side] = go(rows, bank.at[here], sibling)
            copy = fetch(rows, bank.at[here])
            copy.start()
            ends.append(copy)

    handed = []

    def results():
        def collect():
            for copy in taken:
                copy.wait()
            for copy in given:
                copy.wait_recv()
            size = mine.shape[1] // 8

            def add(i, _):
                rows = pl.ds(pl.multiple_of(i * size, size), size)
                for n in range(3):
                    add_rows(mine, (n, rows), (theirs, (n, rows)))
                return 0

            lax.fori_loop(0, 8, add, 0)
            score[...] = score[...] + scores[...]

        pl.when(holder)(collect)
        for rel in range(4):
            target = chips[rel]
            for n in range(4):
                out = (states_out, dx_out, dmem_out, halt_out)[n]
                share_ = out.shape[2]
                src = score if n == 3 else mine.at[n]
                src = src.at[:, pl.ds(pl.multiple_of(target * share_, share_), share_)]
                if rel == 0:
                    copy = fetch(src, out.at[s % 2])
                else:
                    copy = push(src, out.at[s % 2], across[rel - 1])
                pl.when(holder)(copy.start)
                handed.append((rel, copy))

    stages = [plane_first, plane_second, plane_third, line_1, line_2, line_3, line_4, line_5, line_6, line_7]
    lags = [0, 1, 2, 2, 3, 3, 4, 4, 5, 5]
    for tick in range(GROUPS + 6):
        for stage, lag in zip(stages, lags):
            if 0 <= tick - lag < GROUPS:
                stage(tick - lag)
        if tick <= len(gain_steps):
            gain_step(tick)
        if tick == 1:
            results()

    for rel, copy in handed:
        if rel == 0:
            pl.when(holder)(copy.wait)
        else:
            pl.when(chips[rel] // 2 == core)(copy.wait_recv)
            pl.when(holder)(copy.wait_send)
    for copy in given:
        pl.when(jnp.logical_not(holder))(copy.wait_send)
    for copy in finals.values():
        copy.wait_recv()
    for copy in always:
        copy.wait_send()
    for copy in ends:
        copy.wait()
    for (g, way, z), copy in rs.items():
        at_layer(z, copy.wait_send)
    for (g, way, z, k), copy in ag.items():
        at_layer(z, copy.wait_send)


def reduce_all(dw, gains, states, dx, dmem, halt, sections):
    length, width = states.shape
    span = dw[0].shape[0]
    half = span // 2
    piece = half // 2 // GROUPS
    shares = width // sections
    micro = 2
    share = jax.ShapeDtypeStruct((micro, length, shares), bf16)
    outs = [jax.ShapeDtypeStruct((span, width), bf16), jax.ShapeDtypeStruct(gains.shape, f32), share, share, share,
            jax.ShapeDtypeStruct((micro, halt.shape[0], length // sections), f32)]
    copies = 8 * GROUPS + 4 + 5 + (4 + 2 + 6 + 12 + 2) * GROUPS + 12
    scratch = [
        pltpu.VMEM((4, half, width), bf16), pltpu.VMEM((4, half, width), bf16),
        pltpu.VMEM((GROUPS, 2, 2, piece, width), bf16), pltpu.VMEM((GROUPS, 2, piece, width), bf16),
        pltpu.VMEM((GROUPS, 2 * piece, width), bf16), pltpu.VMEM((GROUPS, 2 * piece, width), bf16),
        pltpu.VMEM((GROUPS, 2 * piece, width), bf16), pltpu.VMEM((GROUPS, 2 * piece, width), bf16),
        pltpu.VMEM((3, length, width), bf16), pltpu.VMEM((3, length, width), bf16),
        pltpu.VMEM(halt.shape, f32), pltpu.VMEM(halt.shape, f32),
        pltpu.VMEM((11,) + gains.shape, f32),
        pltpu.SemaphoreType.DMA((copies,)), pltpu.SemaphoreType.DMA((copies,)),
        pltpu.SemaphoreType.DMA((8 * GROUPS + 4 + 2 * GROUPS + 4,)),
    ]
    return pl.pallas_call(
        reduce_kernel,
        out_shape=outs,
        in_specs=[ANY] * 4 + [VMEM] + [ANY] * 4,
        out_specs=[ANY, VMEM, ANY, ANY, ANY, ANY],
        scratch_shapes=scratch,
        compiler_params=pltpu.CompilerParams(collective_id=1, has_side_effects=True, vmem_limit_bytes=52 * 2**20),
        name="reduce_all",
    )(*dw, gains, states, dx, dmem, halt)


def swap_cores(value):
    count = lax.axis_size("dp")
    return lax.ppermute(value, "dp", [(i, i ^ 1) for i in range(count)])


def gather_plain(states, memory, cotangent, bank, gains, ints):
    section, core = lax.axis_index("section"), lax.axis_index("dp") % 2
    micro = states.shape[0]
    holder = section // micro == core

    def pick(rows):
        own = lax.dynamic_index_in_dim(rows, section % micro, 0, keepdims=False)
        return jnp.where(holder, own, swap_cores(own))

    wide = [pick(lax.all_gather(t, "section", axis=2, tiled=True)) for t in (states, memory, cotangent)]
    return wide, lax.all_gather(bank, "section"), lax.all_gather(gains, "section"), [pick(t) for t in ints]


def reduce_plain(dw, dgains, states, dx, dmem, halt):
    section, core = lax.axis_index("section"), lax.axis_index("dp") % 2
    micro = 2
    holder = section // micro == core

    def to_shares(value):
        both = value.astype(f32) + swap_cores(value).astype(f32)
        both = jnp.where(holder, both, 0).astype(value.dtype)
        slots = jnp.stack([jnp.where(section % micro == i, both, 0) for i in range(micro)])
        return lax.psum_scatter(slots, "section", scatter_dimension=2, tiled=True)

    bank = lax.psum_scatter(jnp.stack(dw), "section", scatter_dimension=0, tiled=True)[0]
    bank = lax.psum(bank.astype(f32), "dp")
    gain_sum = lax.psum_scatter(jnp.stack(dgains), "section", scatter_dimension=0, tiled=True)[0]
    gain_sum = lax.psum(gain_sum, "dp")
    return bank, gain_sum, *[to_shares(t) for t in (states, dx, dmem, halt)]


def local(
    states_in, memory, cotangent, weight_bank, gain_bank, segments, pad_mask, memory_segments, memory_mask, exit_depths
):
    section, sections = lax.axis_index("section"), lax.axis_size("section")
    core = lax.axis_index("dp") % 2
    sentences = exit_depths.shape[1]
    matrices = weight_bank.shape[1:]
    width = matrices[-1]
    ints = (segments, pad_mask, memory_segments, memory_mask, exit_depths)
    near = sections == 4 and lax.axis_size("dp") == 8
    if near:
        x, mem, top, bank, gains, *ints = gather_all(
            states_in, memory, cotangent, weight_bank[0].reshape(-1, width), gain_bank[0], ints
        )
        bank = bank.reshape((sections,) + matrices)
        ints = [lax.dynamic_index_in_dim(t.reshape(-1, t.shape[-1]), section, 0, keepdims=False) for t in ints]
    else:
        (x, mem, top), bank, gains, ints = gather_plain(
            states_in, memory, cotangent, weight_bank[0], gain_bank[0], ints
        )
    states, halt, dx, dmem, dw, dgains = row_forward_backward(
        core, x, mem, top, bank, [gains[i] for i in range(sections)], ints, sentences
    )
    if near:
        grads = [t.reshape(-1, width) for t in dw]
        bank, gain_sum, states, dx, dmem, halt = reduce_all(
            grads, jnp.concatenate(dgains), states, dx, dmem, halt, sections
        )
        bank = bank.reshape(matrices)
        gain_sum = lax.dynamic_index_in_dim(gain_sum.reshape(sections, 2, width), section, 0, keepdims=False)
    else:
        bank, gain_sum, states, dx, dmem, halt = reduce_plain(dw, dgains, states, dx, dmem, halt)
    return (
        states,
        halt[:, :2],
        dx.astype(f32),
        dmem.astype(f32),
        bank.astype(f32)[None],
        gain_sum[None],
    )


def solution(mesh):
    rows = P("dp", None, "section")
    return jax.shard_map(
        local,
        mesh=mesh,
        in_specs=(
            rows, rows, rows, P("section", None, None, None), P("section", None, None),
            P("dp", None), P("dp", None), P("dp", None), P("dp", None), P("dp", None),
        ),
        out_specs=(rows, rows, rows, rows, P("section", None, None, None), P("section", None, None)),
        check_vma=False,
    )
```

```python
import functools

import jax
import jax.numpy as jnp
from jax import lax
from jax.experimental import pallas as pl
from jax.experimental.pallas import tpu as pltpu
from jax.sharding import PartitionSpec as P

HEADS = 8
EPS = 1e-06
BLOCK = 128
KEYS = 256
STEP = 16
NEG = -1e30

bf16 = jnp.bfloat16
f32 = jnp.float32
i32 = jnp.int32

SELF, CROSS = 0, 2
CORE, FLAG_T, FIRST, LAST, TOP_T = 8, 9, 10, 11, 12
FLAG_M, TOP_M = 13, 14


def dot(left, right):
    return jnp.dot(left, right, preferred_element_type=f32)


def dot_nt(left, right):
    return lax.dot_general(left, right, (((1,), (1,)), ((), ())), preferred_element_type=f32)


def dot_tn(left, right):
    return lax.dot_general(left, right, (((0,), (0,)), ((), ())), preferred_element_type=f32)


def exact_nt(left, right):
    return lax.dot_general(
        left, right, (((1,), (1,)), ((), ())), precision=lax.Precision.HIGHEST, preferred_element_type=f32
    )


def exact(left, right):
    return jnp.dot(left, right, precision=lax.Precision.HIGHEST, preferred_element_type=f32)


def norm(x, gain):
    return x * lax.rsqrt(jnp.mean(x * x, axis=-1, keepdims=True) + EPS) * gain


def norm_back(x, gain, grad):
    rate = lax.rsqrt(jnp.mean(x * x, axis=-1, keepdims=True) + EPS)
    scaled = x * rate
    inner = grad * gain
    grad_x = rate * (inner - scaled * jnp.mean(inner * scaled, axis=-1, keepdims=True))
    return grad_x, jnp.sum(grad * scaled, axis=0, keepdims=True)


GELU_A = 0.7978845608028654
GELU_B = 0.044715


def gelu(z):
    return 0.5 * z * (1.0 + jnp.tanh(GELU_A * (z + GELU_B * z * z * z)))


def gelu_both(z):
    square = z * z
    bend = jnp.tanh(GELU_A * z * (1.0 + GELU_B * square))
    half = 0.5 * (1.0 + bend)
    slope = half + 0.5 * z * (1.0 - bend * bend) * (GELU_A * (1.0 + 3.0 * GELU_B * square))
    return z * half, slope


def windows(meta, length):
    wide = length * 5 // 8
    slim = length - wide
    core = meta[0, CORE]
    return (
        pl.ds(pl.multiple_of(core * slim, BLOCK), wide),
        pl.ds(pl.multiple_of((1 - core) * wide, BLOCK), slim),
    )


def over(meta, flag, length, work):
    main, other = windows(meta, length)
    work(main, True)

    @pl.when(meta[0, flag] == 1)
    def _():
        work(other, False)


class Moves:
    def __init__(self, meta, length, semaphores):
        self.meta, self.semaphores, self.used, self.leaving = meta, semaphores, 0, []
        self.rows = windows(meta, length)

    def copy(self, src, dst):
        self.used += 1
        return pltpu.make_async_copy(src, dst, self.semaphores.at[self.used - 1])

    def whole(self, src, dst):
        copy = self.copy(src, dst)
        copy.start()
        return copy.wait

    def pair(self, src, dst, flag):
        first, second = (self.copy(src.at[rows], dst.at[rows]) for rows in self.rows)
        first.start()
        pl.when(self.meta[0, flag] == 1)(second.start)

        def wait():
            first.wait()
            pl.when(self.meta[0, flag] == 1)(second.wait)

        return wait

    def away(self, src, dst, flag=None):
        self.leaving.append(self.whole(src, dst) if flag is None else self.pair(src, dst, flag))

    def finish(self):
        for wait in self.leaving:
            wait()


def block(i):
    return pl.ds(pl.multiple_of(i * BLOCK, BLOCK), BLOCK)


def lanes_of(at, p):
    return slice(at + p * BLOCK, at + (p + 1) * BLOCK)


def two_heads(tile, lane):
    zero = jnp.zeros_like(tile)
    return jnp.concatenate([jnp.where(lane < 64, tile, zero), jnp.where(lane < 64, zero, tile)], axis=0)


def both_blocks(tile):
    return jnp.concatenate([tile[:64, :BLOCK], tile[64:, BLOCK:]], axis=0)


def key_window(meta, kind, top, i, n, low, high):
    wanted = meta[i, kind] + n * KEYS
    start = pl.multiple_of(jnp.minimum(wanted, meta[0, top]), STEP)
    place = lax.broadcasted_iota(i32, (KEYS, BLOCK), 0) + start
    bias = jnp.where((place >= jnp.maximum(low, wanted)) & (place < high), 0.0, NEG)
    return pl.ds(start, KEYS), jnp.concatenate([bias, bias], axis=1)


def two_rows(rows_ref, p, rows):
    return jnp.concatenate([rows_ref[2 * p : 2 * p + 1, rows], rows_ref[2 * p + 1 : 2 * p + 2, rows]], axis=1)


def attend(meta, kind, top, info, info_row, q, k, v, o, lse, both_q, peaks, totals, sums):
    (q, q_at), (k, k_at), (v, v_at) = q, k, v
    pairs = o.shape[1] // BLOCK

    def one_block(i, _):
        count = (meta[i, kind + 1] - meta[i, kind] + KEYS - 1) // KEYS

        @pl.when(count > 0)
        def _():
            rows = block(i)
            lane = lax.broadcasted_iota(i32, (BLOCK, BLOCK), 1)
            low, high = info[info_row : info_row + 1, rows], info[info_row + 1 : info_row + 2, rows]
            peaks[...] = jnp.full(peaks.shape, -jnp.inf, f32)
            totals[...] = jnp.zeros(totals.shape, f32)
            sums[...] = jnp.zeros(sums.shape, f32)
            for p in range(pairs):
                both_q[p] = two_heads(q[rows, lanes_of(q_at, p)], lane)

            def one_window(n, _):
                keys, bias = key_window(meta, kind, top, i, n, low, high)
                for p in range(pairs):
                    scores = dot_nt(k[keys, lanes_of(k_at, p)], both_q[p]) + bias
                    before = peaks[p : p + 1, :]
                    peak = jnp.maximum(before, jnp.max(scores, axis=0, keepdims=True))
                    fade = jnp.exp(before - peak)
                    weights = jnp.exp(scores - peak)
                    peaks[p : p + 1, :] = peak
                    totals[p : p + 1, :] = totals[p : p + 1, :] * fade + jnp.sum(weights, axis=0, keepdims=True)
                    mixed = both_blocks(dot_tn(v[keys, lanes_of(v_at, p)], weights.astype(bf16)))
                    faded = jnp.concatenate(
                        [jnp.broadcast_to(fade[:, :BLOCK], (64, BLOCK)), jnp.broadcast_to(fade[:, BLOCK:], (64, BLOCK))]
                    )
                    sums[p] = sums[p] * faded + mixed
                return 0

            lax.fori_loop(0, count, one_window, 0)
            for p in range(pairs):
                total = totals[p : p + 1, :]
                share = 1.0 / total
                shares = jnp.concatenate(
                    [jnp.broadcast_to(share[:, :BLOCK], (64, BLOCK)), jnp.broadcast_to(share[:, BLOCK:], (64, BLOCK))]
                )
                o[rows, lanes_of(0, p)] = (sums[p] * shares).T.astype(bf16)
                log_total = peaks[p : p + 1, :] + jnp.log(total)
                lse[2 * p : 2 * p + 1, rows] = log_total[:, :BLOCK]
                lse[2 * p + 1 : 2 * p + 2, rows] = log_total[:, BLOCK:]

        return 0

    lax.fori_loop(meta[0, FIRST], meta[0, LAST], one_block, 0)


def attend_back(meta, kind, top, info, info_row, q, k, v, lse, delta, do, dq, dk, dv, both_q, both_o, sums):
    (q, q_at), (k, k_at), (v, v_at), (dq, dq_at) = q, k, v, dq
    pairs = do.shape[1] // BLOCK

    def one_block(i, _):
        count = (meta[i, kind + 1] - meta[i, kind] + KEYS - 1) // KEYS

        @pl.when(count > 0)
        def _():
            rows = block(i)
            lane = lax.broadcasted_iota(i32, (BLOCK, BLOCK), 1)
            low, high = info[info_row : info_row + 1, rows], info[info_row + 1 : info_row + 2, rows]
            sums[...] = jnp.zeros(sums.shape, f32)
            for p in range(pairs):
                both_q[p] = two_heads(q[rows, lanes_of(q_at, p)], lane)
                both_o[p] = two_heads(do[rows, lanes_of(0, p)], lane)

            def one_window(n, _):
                keys, bias = key_window(meta, kind, top, i, n, low, high)
                for p in range(pairs):
                    lanes = lanes_of(0, p)
                    these = k[keys, lanes_of(k_at, p)]
                    queries, grads = both_q[p], both_o[p]
                    probs = jnp.exp(dot_nt(these, queries) + bias - two_rows(lse, p, rows))
                    grad_probs = dot_nt(v[keys, lanes_of(v_at, p)], grads)
                    grad_scores = (probs * (grad_probs - two_rows(delta, p, rows))).astype(bf16)
                    dv[keys, lanes] += dot(probs.astype(bf16), grads)
                    dk[keys, lanes] += dot(grad_scores, queries)
                    sums[p] += both_blocks(dot_tn(these, grad_scores))
                return 0

            lax.fori_loop(0, count, one_window, 0)
            for p in range(pairs):
                dq[rows, lanes_of(dq_at, p)] = (sums[p] * 0.125).T.astype(bf16)

        return 0

    lax.fori_loop(meta[0, FIRST], meta[0, LAST], one_block, 0)


def attention_forward_kernel(
    layer, meta, bank, x_in, mem_in, gain, go_rows, info,
    qkv_out, o1_out, l1, mid_out, q2_out, kv_out, o2_out, l2, final,
    x, mem, qkv, o1, mid, q2, kv, o2, out, wide, third, fourth, pairw, last, both_q, peaks, totals, sums, semaphores,
):
    length, width = x.shape
    kind, flag_m, top_m = 4 * layer, FLAG_M + 2 * layer, TOP_M + 2 * layer
    moves = Moves(meta, length, semaphores)
    section = 2 * layer
    x_here = moves.pair(x_in, x, FLAG_T)
    self_here = [moves.whole(bank.at[section, j], wide.at[:, j * width : (j + 1) * width]) for j in range(3)]
    mem_here = moves.pair(mem_in, mem, flag_m)
    pair_here = [moves.whole(bank.at[section, 5 + j], pairw.at[:, j * width : (j + 1) * width]) for j in range(2)]
    rest_here = [moves.whole(bank.at[section, j], place) for j, place in ((3, third), (4, fourth), (7, last))]
    go = (lambda rows: go_rows[rows, layer : layer + 1])
    x_here()
    for wait in self_here:
        wait()

    def self_in(rows, _):
        a = norm(x[rows, :].astype(f32), gain[0:1, :]).astype(bf16)
        both = dot(a, wide[...])
        qkv[rows, :width] = (both[:, :width] * 0.125).astype(bf16)
        qkv[rows, width:] = both[:, width:].astype(bf16)
        o1[rows, :] = jnp.zeros((rows.size, width), bf16)
        o2[rows, :] = jnp.zeros((rows.size, width), bf16)

    over(meta, FLAG_T, length, self_in)
    moves.away(qkv, qkv_out, FLAG_T)
    mem_here()
    for wait in pair_here:
        wait()

    def memory_in(rows, _):
        kv[rows, :] = dot(mem[rows, :], pairw[...]).astype(bf16)

    over(meta, flag_m, length, memory_in)
    moves.away(kv, kv_out, flag_m)
    l1[...] = jnp.zeros(l1.shape, f32)
    l2[...] = jnp.zeros(l2.shape, f32)
    attend(
        meta, SELF + kind, TOP_T, info, 0, (qkv, 0), (qkv, width), (qkv, 2 * width), o1, l1,
        both_q, peaks, totals, sums,
    )
    moves.away(o1, o1_out, FLAG_T)
    for wait in rest_here:
        wait()

    def cross_in(rows, _):
        state = x[rows, :].astype(f32) + go(rows) * dot(o1[rows, :], third[...])
        mid[rows, :] = state
        a = norm(state, gain[1:2, :]).astype(bf16)
        q2[rows, :] = (dot(a, fourth[...]) * 0.125).astype(bf16)

    over(meta, FLAG_T, length, cross_in)
    moves.away(mid, mid_out, FLAG_T)
    moves.away(q2, q2_out, FLAG_T)
    attend(
        meta, CROSS + kind, top_m, info, 2, (q2, 0), (kv, 0), (kv, width), o2, l2, both_q, peaks, totals, sums
    )
    moves.away(o2, o2_out, FLAG_T)

    def finish(rows, _):
        out[rows, :] = (mid[rows, :] + go(rows) * dot(o2[rows, :], last[...])).astype(bf16)

    over(meta, FLAG_T, length, finish)
    moves.away(out, final, FLAG_T)
    moves.finish()


def attention_backward_kernel(
    layer, meta, bank, x_in, mem_in, gain, go_rows, info,
    qkv_in, o1_in, l1, mid_in, q2_in, kv_in, o2_in, l2, dh_in, *rest,
):
    entry = layer == 0
    if entry:
        dmem_in, *rest = rest
    (
        dx_out, dmem_out, dw_out, dgain,
        x, mem, qkv, o1, mid, q2, kv, o2, dh, dx, dmem, dw,
        wide, third, fourth, pairw, last,
        dstate, do, dqkv, dk, dv, delta, heads, both_q, both_o, sums, acc, semaphores,
    ) = rest
    length, width = x.shape
    kind, flag_m, top_m = 4 * layer, FLAG_M + 2 * layer, TOP_M + 2 * layer
    moves = Moves(meta, length, semaphores)
    section = 2 * layer
    first_here = [
        moves.pair(dh_in, dh, FLAG_T), moves.whole(bank.at[section, 7], last), moves.pair(o2_in, o2, FLAG_T),
        moves.pair(q2_in, q2, FLAG_T), moves.pair(kv_in, kv, flag_m),
    ]
    if entry:
        first_here.append(moves.whole(dmem_in, dmem))
    second_here = [moves.pair(mem_in, mem, flag_m), moves.pair(mid_in, mid, FLAG_T)]
    second_here += [moves.whole(bank.at[section, 5 + j], pairw.at[:, j * width : (j + 1) * width]) for j in range(2)]
    second_here += [moves.whole(bank.at[section, 4], fourth)]
    third_here = [moves.whole(bank.at[section, 3], third), moves.pair(o1_in, o1, FLAG_T), moves.pair(qkv_in, qkv, FLAG_T)]
    fourth_here = [moves.whole(bank.at[section, j], wide.at[:, j * width : (j + 1) * width]) for j in range(3)]
    fourth_here += [moves.pair(x_in, x, FLAG_T)]
    go = (lambda rows: go_rows[rows, layer : layer + 1])

    row_of = lax.broadcasted_iota(i32, (HEADS, width), 0)
    lane_of = lax.broadcasted_iota(i32, (HEADS, width), 1)
    heads[...] = (lane_of // (width // HEADS) == row_of).astype(bf16)
    dk[...] = jnp.zeros(dk.shape, f32)
    dv[...] = jnp.zeros(dv.shape, f32)
    delta[...] = jnp.zeros(delta.shape, f32)
    if not entry:
        dmem[...] = jnp.zeros(dmem.shape, bf16)
    if entry:
        dx[...] = jnp.zeros(dx.shape, bf16)

    def weight_grad(targets, flag, left, right):
        size = len(targets) * width

        def part(rows, fresh):
            term = dot_tn(left(rows), right(rows))
            acc[:, :size] = term if fresh else acc[:, :size] + term

        over(meta, flag, length, part)
        for n, j in enumerate(targets):
            dw[j] = acc[:, n * width : (n + 1) * width].astype(bf16)
            moves.away(dw.at[j], dw_out.at[j])

    def begin(grad_of, o, out_weight, target):
        def dy(rows):
            return (go(rows) * grad_of(rows)).astype(bf16)

        def part(rows, _):
            grad = dot_nt(dy(rows), out_weight[...]).astype(bf16)
            do[rows, :] = grad
            product = grad.astype(f32) * o[rows, :].astype(f32)
            high = product.astype(bf16)
            rest = (product - high.astype(f32)).astype(bf16)
            delta[:, rows] = dot_nt(heads[...], high) + dot_nt(heads[...], rest)
            dqkv[rows, :width] = jnp.zeros((rows.size, width), bf16)

        over(meta, FLAG_T, length, part)
        weight_grad([target], FLAG_T, lambda rows: o[rows, :], dy)

    def top_grad(rows):
        return dh[rows, :].astype(f32)

    for wait in first_here:
        wait()
    begin(top_grad, o2, last, 7)
    attend_back(
        meta, CROSS + kind, top_m, info, 2, (q2, 0), (kv, 0), (kv, width), l2, delta, do, (dqkv, 0), dk, dv,
        both_q, both_o, sums,
    )
    for wait in second_here:
        wait()

    def memory_out(rows, _):
        dqkv[rows, width : 2 * width] = dk[rows, :].astype(bf16)
        dqkv[rows, 2 * width :] = dv[rows, :].astype(bf16)
        term = dot_nt(dqkv[rows, width:], pairw[...])
        dmem[rows, :] = (dmem[rows, :].astype(f32) + term).astype(bf16)

    over(meta, flag_m, length, memory_out)
    moves.away(dmem, dmem_out)
    weight_grad([5, 6], flag_m, lambda rows: mem[rows, :], lambda rows: dqkv[rows, width:])

    def cross_out(rows, fresh):
        grad_x, grad_gain = norm_back(mid[rows, :], gain[1:2, :], dot_nt(dqkv[rows, :width], fourth[...]))
        dstate[rows, :] = top_grad(rows) + grad_x
        dgain[1:2, :] = grad_gain if fresh else dgain[1:2, :] + grad_gain

    over(meta, FLAG_T, length, cross_out)
    weight_grad(
        [4], FLAG_T, lambda rows: norm(mid[rows, :], gain[1:2, :]).astype(bf16), lambda rows: dqkv[rows, :width]
    )
    for wait in third_here:
        wait()
    dk[...] = jnp.zeros(dk.shape, f32)
    dv[...] = jnp.zeros(dv.shape, f32)
    begin(lambda rows: dstate[rows, :], o1, third, 3)
    attend_back(
        meta, SELF + kind, TOP_T, info, 0, (qkv, 0), (qkv, width), (qkv, 2 * width), l1, delta, do, (dqkv, 0), dk, dv,
        both_q, both_o, sums,
    )
    for wait in fourth_here:
        wait()

    def self_out(rows, fresh):
        dqkv[rows, width : 2 * width] = dk[rows, :].astype(bf16)
        dqkv[rows, 2 * width :] = dv[rows, :].astype(bf16)
        grad_x, grad_gain = norm_back(x[rows, :].astype(f32), gain[0:1, :], dot_nt(dqkv[rows, :], wide[...]))
        value = dstate[rows, :] + grad_x
        if entry:
            value = jnp.where(go_rows[rows, 2:3] > 0.0, value, 0.0)
        dx[rows, :] = value.astype(bf16)
        dgain[0:1, :] = grad_gain if fresh else dgain[0:1, :] + grad_gain

    over(meta, FLAG_T, length, self_out)
    if entry:
        moves.away(dx, dx_out)
    else:
        moves.away(dx, dx_out, FLAG_T)
    weight_grad(
        [0, 1, 2], FLAG_T, lambda rows: norm(x[rows, :].astype(f32), gain[0:1, :]).astype(bf16),
        lambda rows: dqkv[rows, :],
    )
    moves.finish()


def exit_part(layer, vector, frows, rows, target_row, halt, exit_grad, fresh, sentences):
    factor = layer.shape[1] ** (-0.5)
    vectors = jnp.broadcast_to(vector, (8, layer.shape[1]))
    score = jax.nn.sigmoid(exact_nt(vectors, layer) * factor)
    halt[:, rows] = score
    weight = frows[0:1, rows] * (score - frows[target_row : target_row + 1, rows]) / sentences
    term = exact(weight, layer)[0:1] * factor
    exit_grad[...] = term if fresh else exit_grad[...] + term


def dense_weights(moves, bank, section, up, down, width):
    parts = up.shape[1] // width
    here = [moves.whole(bank.at[section, j], up.at[:, j * width : (j + 1) * width]) for j in range(parts)]
    later = [moves.whole(bank.at[section, parts + j], down.at[j * width : (j + 1) * width]) for j in range(parts)]
    return here, later


def dense_forward_kernel(
    sentences, meta, bank, x, gain, frows, final, halt, exit_grad, out, up, down, semaphores
):
    length, width = x.shape
    moves = Moves(meta, length, semaphores)
    here, later = dense_weights(moves, bank, 1, up, down, width)
    for wait in here:
        wait()

    def part(rows, fresh):
        state = x[rows, :].astype(f32)
        a = norm(state, gain[0:1, :]).astype(bf16)
        active = gelu(dot(a, up[...])).astype(bf16)
        if fresh:
            for wait in later:
                wait()
        layer = state + dot(active, down[...])
        out[rows, :] = layer.astype(bf16)
        exit_part(layer, gain[1:2, :], frows, rows, 1, halt, exit_grad, fresh, sentences)

    over(meta, FLAG_T, length, part)
    moves.away(out, final, FLAG_T)
    moves.finish()


def dense_backward_kernel(sentences, final, meta, bank, x, gain, go_rows, frows, dh, before, dx_out, dw_out, dgain, *rest):
    if final:
        states, halt, exit_grad, out, *rest = rest
        out[...] = jnp.zeros(out.shape, bf16)
    else:
        dgain[1:2, :] = before[...]
    dx, dw, up, down, grad_up, grad_down, semaphores = rest
    length, width = x.shape
    moves = Moves(meta, length, semaphores)
    here, later = dense_weights(moves, bank, 3 if final else 1, up, down, width)
    parts = up.shape[1] // width
    for wait in here:
        wait()

    def part(rows, fresh):
        grad_out = dh[rows, :].astype(f32)
        if final:
            grad_out = jnp.where(go_rows[rows, 2:3] > 0.0, grad_out, 0.0)
        go = go_rows[rows, int(final) : int(final) + 1]
        state = x[rows, :].astype(f32)
        a = norm(state, gain[0:1, :]).astype(bf16)
        dy = (go * grad_out).astype(bf16)
        active, slope = gelu_both(dot(a, up[...]))
        active = active.astype(bf16)
        if fresh:
            for wait in later:
                wait()
        dhidden = (slope * dot_nt(dy, down[...])).astype(bf16)
        downs, ups = dot_tn(active, dy), dot_tn(a, dhidden)
        if fresh:
            grad_down[...] = downs
            grad_up[...] = ups
        else:
            grad_down[...] += downs
            grad_up[...] += ups
        if final:
            layer = state + go * dot(active, down[...])
            out[rows, :] = jnp.where(go_rows[rows, 2:3] > 0.0, layer, 0.0).astype(bf16)
            exit_part(layer, gain[1:2, :], frows, rows, 2, halt, exit_grad, fresh, sentences)
        grad_x, grad_gain = norm_back(state, gain[0:1, :], dot_nt(dhidden, up[...]))
        dx[rows, :] = (grad_out + grad_x).astype(bf16)
        dgain[0:1, :] = grad_gain if fresh else dgain[0:1, :] + grad_gain

    over(meta, FLAG_T, length, part)
    moves.away(dx, dx_out, FLAG_T)
    if final:
        moves.away(out, states)
        dgain[1:2, :] = exit_grad[...]
        mine = frows[3:4, :] > 0.0
        halt[1:2, :] = jnp.where(mine, halt[1:2, :], 0.0)
        halt[0:1, :] = jnp.where(mine, before[0:1, :], 0.0)
    for j in range(parts):
        dw[parts + j] = grad_down[j * width : (j + 1) * width, :].astype(bf16)
        dw[j] = grad_up[:, j * width : (j + 1) * width].astype(bf16)
        moves.away(dw.at[j], dw_out.at[j])
        moves.away(dw.at[parts + j], dw_out.at[parts + j])
    moves.finish()


def plan_kernel(sentences, row, core, seg, pad, mseg, mmask, depths, meta, info, frows, cols):
    row, core = row[0], core[0]
    length, slots = seg.shape[1], mseg.shape[1]
    blocks = length // BLOCK
    seg, pad, mseg, mmask = (t[pl.ds(row, 1), :] for t in (seg, pad, mseg, mmask))
    number = lax.broadcasted_iota(i32, (sentences, length), 0)
    place = lax.broadcasted_iota(i32, (1, length), 1)

    def count(marks):
        return jnp.sum(marks.astype(f32), axis=1, keepdims=True).astype(i32)

    square = lax.broadcasted_iota(i32, (sentences, sentences), 0) == lax.broadcasted_iota(
        i32, (sentences, sentences), 1
    )
    depth_row = jnp.broadcast_to(depths[pl.ds(row, 1), :], (sentences, sentences))
    depth_table = jnp.sum(jnp.where(square, depth_row, 0).astype(f32), axis=1, keepdims=True).astype(i32)
    mine = seg == number
    starts = count(seg < number)
    filled = count(pad == 1)
    memory_number = lax.broadcasted_iota(i32, (sentences, slots), 0)
    memory_starts = count(mseg < memory_number)
    memory_stops = jnp.minimum(count(mseg <= memory_number), count(mmask == 1))

    def of_token(table):
        return jnp.sum(jnp.where(mine, table, 0), axis=0, keepdims=True)

    low = of_token(starts)
    high = jnp.where(pad == 1, jnp.minimum(place, filled - 1), place) + 1
    cross_low = jnp.where(pad == 0, 0, of_token(memory_starts))
    cross_high = jnp.where(pad == 0, slots, of_token(memory_stops))
    depth = of_token(depth_table)
    keep = depth == 2

    later = lax.broadcasted_iota(i32, (sentences, 1), 0) > 0
    away = jnp.where(later, jnp.abs(starts - length // 2), length)
    nearest = jnp.min(away, axis=0, keepdims=True)
    cut = jnp.min(jnp.where(away == nearest, starts, length), axis=0, keepdims=True)

    def by_core(first, second):
        return first * (1 - core) + second * core

    below = jnp.where(place < cut, 1, 0)
    owned = by_core(below, 1 - below) == 1
    begin = by_core(0, cut // BLOCK)
    end = by_core((cut + BLOCK - 1) // BLOCK, blocks)
    wide = length * 5 // 8
    base = by_core(0, length - wide)

    def outside(from_place, to_place):
        return by_core(jnp.where(to_place > wide, 1, 0), jnp.where(from_place < length - wide, 1, 0))

    def top_of(flag):
        return jnp.where(flag == 1, length - KEYS, base + wide - KEYS)

    def by_block(values):
        return jnp.concatenate([values[:, i * BLOCK : (i + 1) * BLOCK] for i in range(blocks)], axis=0)

    lane = lax.broadcasted_iota(i32, (blocks, 128), 1)
    table = jnp.zeros((blocks, 128), i32)
    flag_t = outside(begin * BLOCK, end * BLOCK)
    entries = {CORE: jnp.full((1, 1), core, i32), FLAG_T: flag_t, FIRST: begin, LAST: end, TOP_T: top_of(flag_t)}
    for layer in range(2):
        used = owned if layer == 0 else owned & keep
        for kind, lows, highs in ((SELF, low, high), (CROSS, cross_low, cross_high)):
            lows = jnp.min(by_block(jnp.where(used, lows, slots)), axis=1, keepdims=True)
            highs = jnp.max(by_block(jnp.where(used, highs, 0)), axis=1, keepdims=True)
            entries[kind + 4 * layer] = jnp.minimum(lows, highs) // STEP * STEP
            entries[kind + 4 * layer + 1] = highs
        flag_m = outside(
            jnp.min(jnp.where(used, cross_low, slots), axis=1, keepdims=True),
            jnp.max(jnp.where(used, cross_high, 0), axis=1, keepdims=True),
        )
        entries[FLAG_M + 2 * layer] = flag_m
        entries[TOP_M + 2 * layer] = top_of(flag_m)
    for column, values in entries.items():
        table = jnp.where(lane == column, values, table)
    meta[...] = table
    info[...] = jnp.concatenate([low, high, cross_low, cross_high, low, low, low, low], axis=0)
    ones = jnp.ones((1, length), f32)
    kept, own = keep.astype(f32), owned.astype(f32)
    counted = jnp.where(pad == 1, own, 0.0)
    frows[...] = jnp.concatenate([counted, (depth == 1).astype(f32), ones, own, ones, ones, ones, ones], axis=0)
    by_row = jnp.concatenate([ones, kept, own, own, own, own, own, own], axis=0)
    for i in range(blocks):
        cols[i * BLOCK : (i + 1) * BLOCK, :] = by_row[:, i * BLOCK : (i + 1) * BLOCK].T


ANY = pl.BlockSpec(memory_space=pl.ANY)
VMEM = pl.BlockSpec(memory_space=pltpu.VMEM)
SMEM = pl.BlockSpec(memory_space=pltpu.SMEM)


def make_plan(row, core, ints):
    seg, pad, mseg, mmask, depths = ints
    length, sentences = seg.shape[1], depths.shape[1]
    outs = [((length // BLOCK, 128), i32), ((8, length), i32), ((8, length), f32), ((length, 8), f32)]
    return pl.pallas_call(
        functools.partial(plan_kernel, sentences),
        out_shape=[jax.ShapeDtypeStruct(*out) for out in outs],
        in_specs=[SMEM, SMEM] + [VMEM] * 5,
        out_specs=[VMEM] * 4,
        name="make_plan",
    )(row.astype(i32)[None], core.astype(i32)[None], seg, pad, mseg, mmask, depths)


def run(kernel, ins, outs, scratch, semaphores, name, flops, *args):
    return pl.pallas_call(
        kernel,
        out_shape=[jax.ShapeDtypeStruct(shape, dtype) for _, shape, dtype in outs],
        in_specs=ins,
        out_specs=[spec for spec, _, _ in outs],
        scratch_shapes=[pltpu.VMEM(shape, dtype) for shape, dtype in scratch]
        + [pltpu.SemaphoreType.DMA((semaphores,))],
        compiler_params=pltpu.CompilerParams(vmem_limit_bytes=60 * 2**20),
        cost_estimate=pl.CostEstimate(flops=flops, bytes_accessed=20 * 2**20, transcendentals=0),
        name=name,
    )(*args)


def attention_forward(layer, plan, bank, x, mem, gain, name):
    meta, info, _, cols = plan
    length, width = x.shape
    pairs = width // BLOCK

    def rows(n, dtype=bf16):
        return ((length, n * width), dtype)

    logs = (VMEM, (HEADS, length), f32)
    kept = [rows(3), rows(1), logs[1:], rows(1, f32), rows(1), rows(2), rows(1), logs[1:], rows(1)]
    outs = [(VMEM if shape[0] == HEADS else ANY, shape, dtype) for shape, dtype in kept]
    square = ((width, width), bf16)
    scratch = [
        rows(1), rows(1), rows(3), rows(1), rows(1, f32), rows(1), rows(2), rows(1), rows(1),
        ((width, 3 * width), bf16), square, square, ((width, 2 * width), bf16), square,
        ((pairs, 2 * BLOCK, BLOCK), bf16), ((8, 2 * BLOCK), f32), ((8, 2 * BLOCK), f32), ((pairs, BLOCK, BLOCK), f32),
    ]
    return run(
        functools.partial(attention_forward_kernel, layer), [SMEM, ANY, ANY, ANY, VMEM, VMEM, VMEM], outs, scratch, 32,
        name, 6 * 10**9, meta, bank, x, mem, gain, cols, info,
    )


def attention_backward(layer, plan, bank, x, mem, gain, saved, dh, dmem, name):
    meta, info, _, cols = plan
    length, width = x.shape
    pairs = width // BLOCK

    def rows(n, dtype=bf16):
        return ((length, n * width), dtype)

    square, matrices = ((width, width), bf16), (bank.shape[1:], bf16)
    outs = [(ANY, *rows(1)), (ANY, *rows(1)), (ANY, *matrices), (VMEM, (2, width), f32)]
    both = ((pairs, 2 * BLOCK, BLOCK), bf16)
    scratch = [
        rows(1), rows(1), rows(3), rows(1), rows(1, f32), rows(1), rows(2), rows(1), rows(1), rows(1), rows(1), matrices,
        ((width, 3 * width), bf16), square, square, ((width, 2 * width), bf16), square,
        rows(1, f32), rows(1), rows(3), rows(1, f32), rows(1, f32), ((HEADS, length), f32), ((HEADS, width), bf16),
        both, both, ((pairs, BLOCK, BLOCK), f32), ((width, 3 * width), f32),
    ]
    ins = [SMEM, ANY, ANY, ANY, VMEM, VMEM, VMEM, ANY, ANY, VMEM, ANY, ANY, ANY, ANY, VMEM, ANY] + [ANY] * len(dmem)
    return run(
        functools.partial(attention_backward_kernel, layer), ins, outs, scratch, 48,
        name, 12 * 10**9, meta, bank, x, mem, gain, cols, info, *saved, dh, *dmem,
    )


def dense_forward(plan, bank, x, gain, sentences, name):
    meta, _, frows, _ = plan
    length, width = x.shape
    wide = ((length, width), bf16)
    hidden = bank.shape[1] // 2 * width
    outs = [(ANY, *wide), (VMEM, (8, length), f32), (VMEM, (1, width), f32)]
    return run(
        functools.partial(dense_forward_kernel, sentences), [SMEM, ANY, VMEM, VMEM, VMEM], outs,
        [wide, ((width, hidden), bf16), ((hidden, width), bf16)], 16,
        name, 4 * 10**9, meta, bank, x, gain, frows,
    )


def dense_backward(plan, bank, x, gain, dh, before, sentences, final, name):
    meta, _, frows, cols = plan
    length, width = x.shape
    wide = ((length, width), bf16)
    hidden = bank.shape[1] // 2 * width
    outs = [(ANY, *wide), (ANY, bank.shape[1:], bf16), (VMEM, (2, width), f32)]
    scratch = [wide, (bank.shape[1:], bf16), ((width, hidden), bf16), ((hidden, width), bf16),
               ((width, hidden), f32), ((hidden, width), f32)]
    if final:
        outs += [(ANY, *wide), (VMEM, (8, length), f32)]
        scratch = [((1, width), f32), wide] + scratch
    return run(
        functools.partial(dense_backward_kernel, sentences, final), [SMEM, ANY] + [VMEM] * 6, outs, scratch, 24,
        name, 8 * 10**9, meta, bank, x, gain, cols, frows, dh, before,
    )


def row_forward_backward(row, core, x, mem, cotangent, bank, gains, ints):
    plan = make_plan(row, core, ints)
    sentences = ints[-1].shape[1]
    *saved0, zero = attention_forward(0, plan, bank, x, mem, gains[0], "attend_zero")
    one, halt, exit0 = dense_forward(plan, bank, zero, gains[1], sentences, "dense_one")
    *saved2, two = attention_forward(1, plan, bank, one, mem, gains[2], "attend_two")
    dtwo, dw3, dgain3, states, halt = dense_backward(
        plan, bank, two, gains[3], cotangent, halt, sentences, True, "dense_three"
    )
    done, dmem, dw2, dgain2 = attention_backward(1, plan, bank, one, mem, gains[2], saved2, dtwo, (), "attend_two_back")
    dzero, dw1, dgain1 = dense_backward(plan, bank, zero, gains[1], done, exit0, sentences, False, "dense_one_back")
    dx, dmem, dw0, dgain0 = attention_backward(
        0, plan, bank, x, mem, gains[0], saved0, dzero, (dmem,), "attend_zero_back"
    )
    return states, halt, dx, dmem, [dw0, dw1, dw2, dw3], [dgain0, dgain1, dgain2, dgain3]


MESH = pl.DeviceIdType.MESH


def neighbours():
    s, d = lax.axis_index("section"), lax.axis_index("dp")
    across = [(s + 1 - 2 * (s % 2), d), ((s + 2) % 4, d), (3 - s, d)]
    layer = d // 2
    along = (s, d + 2 - 4 * (layer % 2))
    sibling = (s, d + 1 - 2 * (d % 2))
    return s, d, across, along, sibling


def greet(devices):
    barrier = pltpu.get_barrier_semaphore()
    for device in devices:
        pl.semaphore_signal(barrier, inc=1, device_id=device, device_id_type=MESH)
    pl.semaphore_wait(barrier, len(devices))


SUBS = 4


def gather_kernel(
    states, memory, cotangent, bank, gains, seg, pad, mseg, mmask, depths,
    x, mem, top, weights, gains_all, seg2, pad2, mseg2, mmask2, depths2,
    staging, send, recv, home,
):
    s, d, across, along, sibling = neighbours()
    core = d % 2
    parity = (d // 2) % 2
    greet(across + [along, sibling])
    started = []
    locals_ = []
    count = [0, 0]

    def push(src, dst, device):
        i = count[0]
        count[0] += 1
        copy = pltpu.make_async_remote_copy(src, dst, send.at[i], recv.at[i], device_id=device, device_id_type=MESH)
        return copy

    def go(src, dst, device):
        copy = push(src, dst, device)
        copy.start()
        started.append(copy)
        return copy

    def keep(src, dst):
        i = count[1]
        count[1] += 1
        copy = pltpu.make_async_copy(src, dst, home.at[i])
        return copy

    shares = states.shape[2]
    chips = [s] + [a[0] for a in across]
    sent_inputs, own_inputs = [], []
    for source, whole in ((states, x), (memory, mem), (cotangent, top)):
        for rel in range(4):
            target = chips[rel]
            mine = target // 2 == core
            dst = whole.at[:, pl.ds(pl.multiple_of(s * shares, shares), shares)]
            src = source.at[target % 2]
            if rel == 0:
                copy = keep(src, dst)
                own_inputs.append(copy)
            else:
                copy = push(src, dst, across[rel - 1])
                sent_inputs.append((copy, whole, rel))
            pl.when(mine)(copy.start)
    small = [go(source, whole.at[core], sibling)
             for source, whole in ((seg, seg2), (pad, pad2), (mseg, mseg2), (mmask, mmask2), (depths, depths2))]
    small += [go(gains, gains_all.at[s], device) for device in across]
    for source, whole in ((seg, seg2), (pad, pad2), (mseg, mseg2), (mmask, mmask2), (depths, depths2)):
        copy = keep(source, whole.at[core])
        copy.start()
        locals_.append(copy)
    copy = keep(gains, gains_all.at[s])
    copy.start()
    locals_.append(copy)

    span = bank.shape[0]
    half = span // 2
    third = half // 3 // (16 * SUBS) * (16 * SUBS)
    first = half - 2 * third
    sub0, sub1 = first // SUBS, third // SUBS

    def rows(section, part, i):
        at = section * span + core * half
        size = sub0 if part == 0 else sub1
        if part == 0:
            at = at + i * size
        elif part == 1:
            at = at + first + parity * third + i * size
        else:
            at = at + first + (1 - parity) * third + i * size
        return weights.at[pl.ds(pl.multiple_of(at, 16), size)]

    def own_rows(part, i):
        size = sub0 if part == 0 else sub1
        at = core * half + (i * size if part == 0 else first + parity * third + i * size)
        return bank.at[pl.ds(pl.multiple_of(at, 16), size)]

    direct = {}
    for part in (1, 0):
        for i in range(SUBS):
            for k in range(2):
                direct[k, part, i] = go(own_rows(part, i), rows(s, part, i), across[k])
    lift = keep(bank, staging)
    lift.start()
    drop = keep(staging, weights.at[pl.ds(pl.multiple_of(s * span, span), span)])

    holder = s // 2 == core
    handed = []
    for n, (source, whole) in enumerate(((states, x), (memory, mem), (cotangent, top))):
        for rel in range(4):
            lanes = whole.at[:, pl.ds(pl.multiple_of(chips[rel] * shares, shares), shares)]
            copy = push(lanes, lanes, sibling)
            handed.append(copy)
            arrived = own_inputs[n] if rel == 0 else sent_inputs[n * 3 + rel - 1][0]

            def hand(copy=copy, arrived=arrived, rel=rel):
                if rel == 0:
                    arrived.wait()
                else:
                    arrived.wait_recv()
                copy.start()

            pl.when(holder)(hand)

    lift.wait()
    drop.start()
    locals_.append(drop)
    far = {}
    lifted = {}
    passed = []

    def arrive(copy, section, part, i):
        copy.wait_recv()
        passed.append(go(rows(section, part, i), rows(section, part, i), sibling))

    for i in range(SUBS):
        arrive(direct[0, 1, i], chips[1], 1, i)
        far[1, i] = go(rows(chips[1], 1, i), rows(chips[1], 1, i), across[1])
        lifted[1, i] = go(rows(chips[1], 1, i), rows(chips[1], 1, i), along)
        arrive(direct[1, 1, i], chips[2], 1, i)
        lifted[2, i] = go(rows(chips[2], 1, i), rows(chips[2], 1, i), along)
    for i in range(SUBS):
        arrive(direct[1, 0, i], chips[2], 0, i)
        far[0, i] = go(rows(chips[2], 0, i), rows(chips[2], 0, i), across[0])
        arrive(direct[0, 0, i], chips[1], 0, i)
    for i in range(SUBS):
        arrive(far[1, i], chips[3], 1, i)
        lifted[3, i] = go(rows(chips[3], 1, i), rows(chips[3], 1, i), along)
    for i in range(SUBS):
        arrive(far[0, i], chips[3], 0, i)
    for k in range(1, 4):
        for i in range(SUBS):
            arrive(lifted[k, i], chips[k], 2, i)
    for copy in passed + small:
        copy.wait_recv()
    for copy in handed:
        pl.when(jnp.logical_not(holder))(copy.wait_recv)
        pl.when(holder)(copy.wait_send)
    for (copy, whole, rel) in sent_inputs:
        pl.when(chips[rel] // 2 == core)(copy.wait_send)
    for copy in started:
        copy.wait_send()
    for copy in locals_:
        copy.wait()


def gather_all(states, memory, cotangent, bank, gains, ints):
    micro, length, shares = states.shape
    sections = lax.axis_size("section")
    width = shares * sections
    wide = jax.ShapeDtypeStruct((length, width), bf16)
    copies = 9 + 12 + 8 + 4 * SUBS + 2 * SUBS + 3 * SUBS + 9 * SUBS
    outs = [wide, wide, wide, jax.ShapeDtypeStruct((sections * bank.shape[0], width), bf16),
            jax.ShapeDtypeStruct((sections,) + gains.shape, f32)]
    outs += [jax.ShapeDtypeStruct((2,) + t.shape, t.dtype) for t in ints]
    return pl.pallas_call(
        gather_kernel,
        out_shape=outs,
        in_specs=[ANY] * 10,
        out_specs=[ANY] * 10,
        scratch_shapes=[pltpu.VMEM(bank.shape, bank.dtype), pltpu.SemaphoreType.DMA((copies,)), pltpu.SemaphoreType.DMA((copies,)),
                        pltpu.SemaphoreType.DMA((12,))],
        compiler_params=pltpu.CompilerParams(collective_id=0, has_side_effects=True, vmem_limit_bytes=16 * 2**20),
        name="gather_all",
    )(states, memory, cotangent, bank, gains, *ints)


GROUPS = 8
AHEAD = 2
RESULTS = 7


def add_rows(target, rows, *others):
    total = target[rows].astype(f32)
    for other, places in others:
        total = total + other[places].astype(f32)
    target[rows] = total.astype(bf16)


def reduce_kernel(
    dw0, dw1, dw2, dw3, gains, states, dx, dmem, halt,
    bank, gains_sum, states_out, dx_out, dmem_out, halt_out,
    own, other, first, second, left, right, total, full, mine, theirs, score, scores,
    gain_parts, send, recv, home,
):
    s, d, across, _, sibling = neighbours()
    core, layer = d % 2, d // 2
    chips = [s] + [a[0] for a in across]
    column = [(s, (layer + k) % 4 * 2 + core) for k in range(1, 4)]
    up, down = (s, d + 2), (s, d - 2)
    pair = (s, d + 2 - 4 * (layer % 2))
    jump = (s, (layer + 2) % 4 * 2 + core)
    holder = s // 2 == core
    greet(across + [sibling] + column)
    count = [0, 0]
    always, ends = [], []

    def push(src, dst, device):
        i = count[0]
        count[0] += 1
        return pltpu.make_async_remote_copy(src, dst, send.at[i], recv.at[i], device_id=device, device_id_type=MESH)

    def go(src, dst, device):
        copy = push(src, dst, device)
        copy.start()
        always.append(copy)
        return copy

    def fetch(src, dst):
        i = count[1]
        count[1] += 1
        copy = pltpu.make_async_copy(src, dst, home.at[i])
        return copy

    span = dw0.shape[0]
    half = span // 2
    quarter = half // 2
    piece = quarter // GROUPS
    grads = (dw0, dw1, dw2, dw3)

    def at(g, side):
        return side * quarter + g * piece

    loads, swaps = {}, {}

    def exchange(g):
        for t in range(4):
            for side in range(2):
                rows = pl.ds(at(g, side), piece)
                there = pl.ds(pl.multiple_of((1 - core) * half + at(g, side), piece), piece)
                here = pl.ds(pl.multiple_of(core * half + at(g, side), piece), piece)
                swaps[g, t, side] = go(grads[t].at[there], other.at[t, rows], sibling)
                loads[g, t, side] = fetch(grads[t].at[here], own.at[t, rows])
                loads[g, t, side].start()

    for g in range(AHEAD):
        exchange(g)
    outs = ((states, states_out), (dx, dx_out), (dmem, dmem_out))
    given, taken = [], []
    for n, (source, _) in enumerate(outs):
        given.append(push(source, theirs.at[n], sibling))
        taken.append(fetch(source, mine.at[n]))
    given.append(push(halt, scores, sibling))
    taken.append(fetch(halt, score))

    def results_begin():
        for copy in given:
            pl.when(jnp.logical_not(holder))(copy.start)
        for copy in taken:
            pl.when(holder)(copy.start)

    gain_steps = [sibling, across[0], across[1], pair, jump]
    gain_parts[0] = gains[...]
    gain_copies = []

    def gain_step(k):
        if k > 0:
            gain_copies[-1].wait_recv()
            gain_parts[2 * k] = gain_parts[2 * k - 2] + gain_parts[2 * k - 1]
        if k < len(gain_steps):
            gain_copies.append(go(gain_parts.at[2 * k], gain_parts.at[2 * k + 1], gain_steps[k]))
        else:
            gains_sum[...] = gain_parts[2 * k]

    step1, step2, rs, ag = {}, {}, {}, {}

    def plane_first(g):
        if g + AHEAD < GROUPS:
            exchange(g + AHEAD)
        for t in range(4):
            for side in range(2):
                swaps[g, t, side].wait_recv()
                loads[g, t, side].wait()
                rows = pl.ds(at(g, side), piece)
                add_rows(own, (t, rows), (other, (t, rows)))
        for side in range(2):
            rows = pl.ds(at(g, side), piece)
            for n, rel in enumerate((3, 1 + side)):
                step1[g, side, n] = go(own.at[chips[rel], rows], first.at[g, side, n], across[side])

    def plane_second(g):
        for side in range(2):
            rows = pl.ds(at(g, side), piece)
            for n, rel in enumerate((2 - side, 0)):
                step1[g, side, n].wait_recv()
                add_rows(own, (chips[rel], rows), (first, (g, side, n)))
                if n == 0:
                    step2[g, side] = go(own.at[chips[rel], rows], second.at[g, side], across[1 - side])

    def plane_third(g):
        for side in range(2):
            step2[g, side].wait_recv()
            rows = pl.ds(at(g, side), piece)
            value = own[s, rows].astype(f32) + second[g, side].astype(f32)
            total[g, pl.ds(side * piece, piece)] = value.astype(bf16)

    wide = 2 * piece
    shard = wide // 4

    def span_of(k0, k1):
        return pl.ds(k0 * shard, (k1 - k0) * shard)

    def share(kind, g, low, high, src, dst, device):
        return push(src.at[g, span_of(low, high)], dst.at[g, span_of(low, high)], device)

    def line_sums(g):
        for z in range(3):
            rs[g, "up", z] = share("up", g, z + 1, 4, total, right, up)
            rs[g, "down", z + 1] = share("down", g, 0, z + 1, total, left, down)
        for k in range(4):
            for z in range(k, 3):
                ag[g, "up", z, k] = push(full.at[g, span_of(k, k + 1)], full.at[g, span_of(k, k + 1)], up)
            for z in range(1, k + 1):
                ag[g, "down", z, k] = push(full.at[g, span_of(k, k + 1)], full.at[g, span_of(k, k + 1)], down)

    def at_layer(z, action):
        pl.when(layer == z)(action)

    def close(g, k, *others):
        value = total[g, span_of(k, k + 1)].astype(f32)
        for other_ in others:
            value = value + other_[g, span_of(k, k + 1)].astype(f32)
        full[g, span_of(k, k + 1)] = value.astype(bf16)

    def line_1(g):
        line_sums(g)
        at_layer(0, lambda: rs[g, "up", 0].start())
        at_layer(3, lambda: rs[g, "down", 3].start())

    def line_2(g):
        def second_layer():
            rs[g, "up", 0].wait_recv()
            add_rows(total, (g, span_of(2, 4)), (right, (g, span_of(2, 4))))
            rs[g, "up", 1].start()

        def third_layer():
            rs[g, "down", 3].wait_recv()
            add_rows(total, (g, span_of(0, 2)), (left, (g, span_of(0, 2))))
            rs[g, "down", 2].start()

        at_layer(1, second_layer)
        at_layer(2, third_layer)

    def line_3(g):
        def third_layer():
            rs[g, "up", 1].wait_recv()
            add_rows(total, (g, span_of(3, 4)), (right, (g, span_of(3, 4))))
            rs[g, "up", 2].start()
            close(g, 2, right, left)
            ag[g, "up", 2, 2].start()
            ag[g, "down", 2, 2].start()

        def second_layer():
            rs[g, "down", 2].wait_recv()
            add_rows(total, (g, span_of(0, 1)), (left, (g, span_of(0, 1))))
            rs[g, "down", 1].start()
            close(g, 1, right, left)
            ag[g, "up", 1, 1].start()
            ag[g, "down", 1, 1].start()

        at_layer(2, third_layer)
        at_layer(1, second_layer)

    def line_4(g):
        def bottom():
            rs[g, "down", 1].wait_recv()
            close(g, 0, left)
            ag[g, "up", 0, 0].start()

        def top():
            rs[g, "up", 2].wait_recv()
            close(g, 3, right)
            ag[g, "down", 3, 3].start()

        def second_layer():
            ag[g, "down", 2, 2].wait_recv()
            ag[g, "down", 1, 2].start()

        def third_layer():
            ag[g, "up", 1, 1].wait_recv()
            ag[g, "up", 2, 1].start()

        at_layer(0, bottom)
        at_layer(3, top)
        at_layer(1, second_layer)
        at_layer(2, third_layer)

    def line_5(g):
        def bottom():
            ag[g, "down", 1, 1].wait_recv()

        def top():
            ag[g, "up", 2, 2].wait_recv()

        def second_layer():
            ag[g, "up", 0, 0].wait_recv()
            ag[g, "up", 1, 0].start()

        def third_layer():
            ag[g, "down", 3, 3].wait_recv()
            ag[g, "down", 2, 3].start()

        at_layer(0, bottom)
        at_layer(3, top)
        at_layer(1, second_layer)
        at_layer(2, third_layer)

    def line_6(g):
        def bottom():
            ag[g, "down", 1, 2].wait_recv()

        def top():
            ag[g, "up", 2, 1].wait_recv()

        def second_layer():
            ag[g, "down", 2, 3].wait_recv()
            ag[g, "down", 1, 3].start()

        def third_layer():
            ag[g, "up", 1, 0].wait_recv()
            ag[g, "up", 2, 0].start()

        at_layer(0, bottom)
        at_layer(3, top)
        at_layer(1, second_layer)
        at_layer(2, third_layer)

    finals = {}

    def line_7(g):
        at_layer(0, lambda: ag[g, "down", 1, 3].wait_recv())
        at_layer(3, lambda: ag[g, "up", 2, 0].wait_recv())
        for side in range(2):
            here = pl.ds(pl.multiple_of(core * half + at(g, side), piece), piece)
            rows = full.at[g, pl.ds(side * piece, piece)]
            finals[g, side] = go(rows, bank.at[here], sibling)
            copy = fetch(rows, bank.at[here])
            copy.start()
            ends.append(copy)

    handed = []

    def results():
        def collect():
            for copy in taken:
                copy.wait()
            for copy in given:
                copy.wait_recv()
            size = mine.shape[1] // 8

            def add(i, _):
                rows = pl.ds(pl.multiple_of(i * size, size), size)
                for n in range(3):
                    add_rows(mine, (n, rows), (theirs, (n, rows)))
                return 0

            lax.fori_loop(0, 8, add, 0)
            score[...] = score[...] + scores[...]

        pl.when(holder)(collect)
        for rel in range(4):
            target = chips[rel]
            for n in range(4):
                out = (states_out, dx_out, dmem_out, halt_out)[n]
                share_ = out.shape[2]
                src = score if n == 3 else mine.at[n]
                src = src.at[:, pl.ds(pl.multiple_of(target * share_, share_), share_)]
                if rel == 0:
                    copy = fetch(src, out.at[s % 2])
                else:
                    copy = push(src, out.at[s % 2], across[rel - 1])
                pl.when(holder)(copy.start)
                handed.append((rel, copy))

    stages = [plane_first, plane_second, plane_third, line_1, line_2, line_3, line_4, line_5, line_6, line_7]
    lags = [0, 1, 2, 2, 3, 3, 4, 4, 5, 5]
    for tick in range(GROUPS + 6):
        for stage, lag in zip(stages, lags):
            if 0 <= tick - lag < GROUPS:
                stage(tick - lag)
        if tick <= len(gain_steps):
            gain_step(tick)
        if tick == RESULTS - 1:
            results_begin()
        if tick == RESULTS:
            results()

    for rel, copy in handed:
        if rel == 0:
            pl.when(holder)(copy.wait)
        else:
            pl.when(chips[rel] // 2 == core)(copy.wait_recv)
            pl.when(holder)(copy.wait_send)
    for copy in given:
        pl.when(jnp.logical_not(holder))(copy.wait_send)
    for copy in finals.values():
        copy.wait_recv()
    for copy in always:
        copy.wait_send()
    for copy in ends:
        copy.wait()
    for (g, way, z), copy in rs.items():
        at_layer(z, copy.wait_send)
    for (g, way, z, k), copy in ag.items():
        at_layer(z, copy.wait_send)


def reduce_all(dw, gains, states, dx, dmem, halt, sections):
    length, width = states.shape
    span = dw[0].shape[0]
    half = span // 2
    piece = half // 2 // GROUPS
    shares = width // sections
    micro = 2
    share = jax.ShapeDtypeStruct((micro, length, shares), bf16)
    outs = [jax.ShapeDtypeStruct((span, width), bf16), jax.ShapeDtypeStruct(gains.shape, f32), share, share, share,
            jax.ShapeDtypeStruct((micro, halt.shape[0], length // sections), f32)]
    copies = 8 * GROUPS + 4 + 5 + (4 + 2 + 6 + 12 + 2) * GROUPS + 12
    scratch = [
        pltpu.VMEM((4, half, width), bf16), pltpu.VMEM((4, half, width), bf16),
        pltpu.VMEM((GROUPS, 2, 2, piece, width), bf16), pltpu.VMEM((GROUPS, 2, piece, width), bf16),
        pltpu.VMEM((GROUPS, 2 * piece, width), bf16), pltpu.VMEM((GROUPS, 2 * piece, width), bf16),
        pltpu.VMEM((GROUPS, 2 * piece, width), bf16), pltpu.VMEM((GROUPS, 2 * piece, width), bf16),
        pltpu.VMEM((3, length, width), bf16), pltpu.VMEM((3, length, width), bf16),
        pltpu.VMEM(halt.shape, f32), pltpu.VMEM(halt.shape, f32),
        pltpu.VMEM((11,) + gains.shape, f32),
        pltpu.SemaphoreType.DMA((copies,)), pltpu.SemaphoreType.DMA((copies,)),
        pltpu.SemaphoreType.DMA((8 * GROUPS + 4 + 2 * GROUPS + 4,)),
    ]
    return pl.pallas_call(
        reduce_kernel,
        out_shape=outs,
        in_specs=[ANY] * 4 + [VMEM] + [ANY] * 4,
        out_specs=[ANY, VMEM, ANY, ANY, ANY, ANY],
        scratch_shapes=scratch,
        compiler_params=pltpu.CompilerParams(collective_id=1, has_side_effects=True, vmem_limit_bytes=52 * 2**20),
        name="reduce_all",
    )(*dw, gains, states, dx, dmem, halt)


def swap_cores(value):
    count = lax.axis_size("dp")
    return lax.ppermute(value, "dp", [(i, i ^ 1) for i in range(count)])


def gather_plain(states, memory, cotangent, bank, gains, ints):
    section, core = lax.axis_index("section"), lax.axis_index("dp") % 2
    micro = states.shape[0]
    holder = section // micro == core

    def pick(rows):
        own = lax.dynamic_index_in_dim(rows, section % micro, 0, keepdims=False)
        return jnp.where(holder, own, swap_cores(own))

    wide = [pick(lax.all_gather(t, "section", axis=2, tiled=True)) for t in (states, memory, cotangent)]
    return wide, lax.all_gather(bank, "section"), lax.all_gather(gains, "section"), [pick(t) for t in ints]


def reduce_plain(dw, dgains, states, dx, dmem, halt):
    section, core = lax.axis_index("section"), lax.axis_index("dp") % 2
    micro = 2
    holder = section // micro == core

    def to_shares(value):
        both = value.astype(f32) + swap_cores(value).astype(f32)
        both = jnp.where(holder, both, 0).astype(value.dtype)
        slots = jnp.stack([jnp.where(section % micro == i, both, 0) for i in range(micro)])
        return lax.psum_scatter(slots, "section", scatter_dimension=2, tiled=True)

    bank = lax.psum_scatter(jnp.stack(dw), "section", scatter_dimension=0, tiled=True)[0]
    bank = lax.psum(bank.astype(f32), "dp")
    gain_sum = lax.psum_scatter(jnp.stack(dgains), "section", scatter_dimension=0, tiled=True)[0]
    gain_sum = lax.psum(gain_sum, "dp")
    return bank, gain_sum, *[to_shares(t) for t in (states, dx, dmem, halt)]


def local(
    states_in, memory, cotangent, weight_bank, gain_bank, segments, pad_mask, memory_segments, memory_mask, exit_depths
):
    section, sections = lax.axis_index("section"), lax.axis_size("section")
    core = lax.axis_index("dp") % 2
    matrices = weight_bank.shape[1:]
    width = matrices[-1]
    ints = (segments, pad_mask, memory_segments, memory_mask, exit_depths)
    near = sections == 4 and lax.axis_size("dp") == 8
    if near:
        x, mem, top, bank, gains, *ints = gather_all(
            states_in, memory, cotangent, weight_bank[0].reshape(-1, width), gain_bank[0], ints
        )
        bank = bank.reshape((sections,) + matrices)
        ints, row = [t.reshape(-1, t.shape[-1]) for t in ints], section
    else:
        (x, mem, top), bank, gains, ints = gather_plain(
            states_in, memory, cotangent, weight_bank[0], gain_bank[0], ints
        )
        ints, row = [t[None] for t in ints], jnp.zeros((), i32)
    states, halt, dx, dmem, dw, dgains = row_forward_backward(
        row, core, x, mem, top, bank, [gains[i] for i in range(sections)], ints
    )
    if near:
        grads = [t.reshape(-1, width) for t in dw]
        bank, gain_sum, states, dx, dmem, halt = reduce_all(
            grads, jnp.concatenate(dgains), states, dx, dmem, halt, sections
        )
        bank = bank.reshape(matrices)
        gain_sum = lax.dynamic_index_in_dim(gain_sum.reshape(sections, 2, width), section, 0, keepdims=False)
    else:
        bank, gain_sum, states, dx, dmem, halt = reduce_plain(dw, dgains, states, dx, dmem, halt)
    return (
        states,
        halt[:, :2],
        dx.astype(f32),
        dmem.astype(f32),
        bank.astype(f32)[None],
        gain_sum[None],
    )


def solution(mesh):
    rows = P("dp", None, "section")
    return jax.shard_map(
        local,
        mesh=mesh,
        in_specs=(
            rows, rows, rows, P("section", None, None, None), P("section", None, None),
            P("dp", None), P("dp", None), P("dp", None), P("dp", None), P("dp", None),
        ),
        out_specs=(rows, rows, rows, rows, P("section", None, None, None), P("section", None, None)),
        check_vma=False,
    )
```

```python
import functools

import jax
import jax.numpy as jnp
from jax import lax
from jax.experimental import pallas as pl
from jax.experimental.pallas import tpu as pltpu
from jax.sharding import PartitionSpec as P

HEADS = 8
EPS = 1e-06
BLOCK = 128
KEYS = 256
STEP = 16
NEG = -1e30

bf16 = jnp.bfloat16
f32 = jnp.float32
i32 = jnp.int32

SELF, CROSS = 0, 2
CORE, FLAG_T, FIRST, LAST, TOP_T = 8, 9, 10, 11, 12
FLAG_M, TOP_M = 13, 14


def dot(left, right):
    return jnp.dot(left, right, preferred_element_type=f32)


def dot_nt(left, right):
    return lax.dot_general(left, right, (((1,), (1,)), ((), ())), preferred_element_type=f32)


def dot_tn(left, right):
    return lax.dot_general(left, right, (((0,), (0,)), ((), ())), preferred_element_type=f32)


def exact_nt(left, right):
    return lax.dot_general(
        left, right, (((1,), (1,)), ((), ())), precision=lax.Precision.HIGHEST, preferred_element_type=f32
    )


def exact(left, right):
    return jnp.dot(left, right, precision=lax.Precision.HIGHEST, preferred_element_type=f32)


def norm(x, gain):
    return x * lax.rsqrt(jnp.mean(x * x, axis=-1, keepdims=True) + EPS) * gain


def norm_back(x, gain, grad):
    rate = lax.rsqrt(jnp.mean(x * x, axis=-1, keepdims=True) + EPS)
    scaled = x * rate
    inner = grad * gain
    grad_x = rate * (inner - scaled * jnp.mean(inner * scaled, axis=-1, keepdims=True))
    return grad_x, jnp.sum(grad * scaled, axis=0, keepdims=True)


GELU_A = 0.7978845608028654
GELU_B = 0.044715


def gelu(z):
    return 0.5 * z * (1.0 + jnp.tanh(GELU_A * (z + GELU_B * z * z * z)))


def gelu_both(z):
    square = z * z
    bend = jnp.tanh(GELU_A * z * (1.0 + GELU_B * square))
    half = 0.5 * (1.0 + bend)
    slope = half + 0.5 * z * (1.0 - bend * bend) * (GELU_A * (1.0 + 3.0 * GELU_B * square))
    return z * half, slope


def windows(meta, length):
    wide = length * 5 // 8
    slim = length - wide
    core = meta[0, CORE]
    return (
        pl.ds(pl.multiple_of(core * slim, BLOCK), wide),
        pl.ds(pl.multiple_of((1 - core) * wide, BLOCK), slim),
    )


def over(meta, flag, length, work):
    main, other = windows(meta, length)
    work(main, True)

    @pl.when(meta[0, flag] == 1)
    def _():
        work(other, False)


class Moves:
    def __init__(self, meta, length, semaphores):
        self.meta, self.semaphores, self.used, self.leaving = meta, semaphores, 0, []
        self.rows = windows(meta, length)

    def copy(self, src, dst):
        self.used += 1
        return pltpu.make_async_copy(src, dst, self.semaphores.at[self.used - 1])

    def whole(self, src, dst):
        copy = self.copy(src, dst)
        copy.start()
        return copy.wait

    def pair(self, src, dst, flag):
        first, second = (self.copy(src.at[rows], dst.at[rows]) for rows in self.rows)
        first.start()
        pl.when(self.meta[0, flag] == 1)(second.start)

        def wait():
            first.wait()
            pl.when(self.meta[0, flag] == 1)(second.wait)

        return wait

    def away(self, src, dst, flag=None):
        self.leaving.append(self.whole(src, dst) if flag is None else self.pair(src, dst, flag))

    def finish(self):
        for wait in self.leaving:
            wait()


def block(i):
    return pl.ds(pl.multiple_of(i * BLOCK, BLOCK), BLOCK)


def lanes_of(at, p):
    return slice(at + p * BLOCK, at + (p + 1) * BLOCK)


def two_heads(tile, lane):
    zero = jnp.zeros_like(tile)
    return jnp.concatenate([jnp.where(lane < 64, tile, zero), jnp.where(lane < 64, zero, tile)], axis=0)


def both_blocks(tile):
    return jnp.concatenate([tile[:64, :BLOCK], tile[64:, BLOCK:]], axis=0)


def key_window(meta, kind, top, i, n, low, high):
    wanted = meta[i, kind] + n * KEYS
    start = pl.multiple_of(jnp.minimum(wanted, meta[0, top]), STEP)
    place = lax.broadcasted_iota(i32, (KEYS, BLOCK), 0) + start
    bias = jnp.where((place >= jnp.maximum(low, wanted)) & (place < high), 0.0, NEG)
    return pl.ds(start, KEYS), jnp.concatenate([bias, bias], axis=1)


def two_rows(rows_ref, p, rows):
    return jnp.concatenate([rows_ref[2 * p : 2 * p + 1, rows], rows_ref[2 * p + 1 : 2 * p + 2, rows]], axis=1)


def attend(meta, kind, top, info, info_row, q, k, v, o, lse, both_q, peaks, totals, sums):
    (q, q_at), (k, k_at), (v, v_at) = q, k, v
    pairs = o.shape[1] // BLOCK

    def one_block(i, _):
        count = (meta[i, kind + 1] - meta[i, kind] + KEYS - 1) // KEYS

        @pl.when(count > 0)
        def _():
            rows = block(i)
            lane = lax.broadcasted_iota(i32, (BLOCK, BLOCK), 1)
            low, high = info[info_row : info_row + 1, rows], info[info_row + 1 : info_row + 2, rows]
            peaks[...] = jnp.full(peaks.shape, -jnp.inf, f32)
            totals[...] = jnp.zeros(totals.shape, f32)
            sums[...] = jnp.zeros(sums.shape, f32)
            for p in range(pairs):
                both_q[p] = two_heads(q[rows, lanes_of(q_at, p)], lane)

            def one_window(n, _):
                keys, bias = key_window(meta, kind, top, i, n, low, high)
                scores = [dot_nt(k[keys, lanes_of(k_at, p)], both_q[p]) for p in range(pairs)]
                weights, fades = [], []
                for p in range(pairs):
                    tile = scores[p] + bias
                    before = peaks[p : p + 1, :]
                    peak = jnp.maximum(before, jnp.max(tile, axis=0, keepdims=True))
                    fade = jnp.exp(before - peak)
                    weight = jnp.exp(tile - peak)
                    peaks[p : p + 1, :] = peak
                    totals[p : p + 1, :] = totals[p : p + 1, :] * fade + jnp.sum(weight, axis=0, keepdims=True)
                    weights.append(weight.astype(bf16))
                    fades.append(fade)
                mixes = [dot_tn(v[keys, lanes_of(v_at, p)], weights[p]) for p in range(pairs)]
                for p in range(pairs):
                    fade = fades[p]
                    faded = jnp.concatenate(
                        [jnp.broadcast_to(fade[:, :BLOCK], (64, BLOCK)), jnp.broadcast_to(fade[:, BLOCK:], (64, BLOCK))]
                    )
                    sums[p] = sums[p] * faded + both_blocks(mixes[p])
                return 0

            lax.fori_loop(0, count, one_window, 0)
            for p in range(pairs):
                total = totals[p : p + 1, :]
                share = 1.0 / total
                shares = jnp.concatenate(
                    [jnp.broadcast_to(share[:, :BLOCK], (64, BLOCK)), jnp.broadcast_to(share[:, BLOCK:], (64, BLOCK))]
                )
                o[rows, lanes_of(0, p)] = (sums[p] * shares).T.astype(bf16)
                log_total = peaks[p : p + 1, :] + jnp.log(total)
                lse[2 * p : 2 * p + 1, rows] = log_total[:, :BLOCK]
                lse[2 * p + 1 : 2 * p + 2, rows] = log_total[:, BLOCK:]

        return 0

    lax.fori_loop(meta[0, FIRST], meta[0, LAST], one_block, 0)


def attend_back(meta, kind, top, info, info_row, q, k, v, lse, delta, do, dq, dk, dv, both_q, both_o, sums):
    (q, q_at), (k, k_at), (v, v_at), (dq, dq_at) = q, k, v, dq
    pairs = do.shape[1] // BLOCK

    def one_block(i, _):
        count = (meta[i, kind + 1] - meta[i, kind] + KEYS - 1) // KEYS

        @pl.when(count > 0)
        def _():
            rows = block(i)
            lane = lax.broadcasted_iota(i32, (BLOCK, BLOCK), 1)
            low, high = info[info_row : info_row + 1, rows], info[info_row + 1 : info_row + 2, rows]
            sums[...] = jnp.zeros(sums.shape, f32)
            for p in range(pairs):
                both_q[p] = two_heads(q[rows, lanes_of(q_at, p)], lane)
                both_o[p] = two_heads(do[rows, lanes_of(0, p)], lane)

            def one_window(n, _):
                keys, bias = key_window(meta, kind, top, i, n, low, high)
                these = [k[keys, lanes_of(k_at, p)] for p in range(pairs)]
                scores = [dot_nt(these[p], both_q[p]) for p in range(pairs)]
                grad_probs = [dot_nt(v[keys, lanes_of(v_at, p)], both_o[p]) for p in range(pairs)]
                probs = [jnp.exp(scores[p] + bias - two_rows(lse, p, rows)) for p in range(pairs)]
                grad_scores = [
                    (probs[p] * (grad_probs[p] - two_rows(delta, p, rows))).astype(bf16) for p in range(pairs)
                ]
                grads_v = [dot(probs[p].astype(bf16), both_o[p]) for p in range(pairs)]
                grads_k = [dot(grad_scores[p], both_q[p]) for p in range(pairs)]
                grads_q = [dot_tn(these[p], grad_scores[p]) for p in range(pairs)]
                for p in range(pairs):
                    dv[keys, lanes_of(0, p)] += grads_v[p]
                    dk[keys, lanes_of(0, p)] += grads_k[p]
                    sums[p] += both_blocks(grads_q[p])
                return 0

            lax.fori_loop(0, count, one_window, 0)
            for p in range(pairs):
                dq[rows, lanes_of(dq_at, p)] = (sums[p] * 0.125).T.astype(bf16)

        return 0

    lax.fori_loop(meta[0, FIRST], meta[0, LAST], one_block, 0)


def attention_forward_kernel(
    layer, meta, bank, x_in, mem_in, gain, go_rows, info,
    qkv_out, o1_out, l1, mid_out, q2_out, kv_out, o2_out, l2, final,
    x, mem, qkv, o1, mid, q2, kv, o2, out, wide, third, fourth, pairw, last, both_q, peaks, totals, sums, semaphores,
):
    length, width = x.shape
    kind, flag_m, top_m = 4 * layer, FLAG_M + 2 * layer, TOP_M + 2 * layer
    moves = Moves(meta, length, semaphores)
    section = 2 * layer
    x_here = moves.pair(x_in, x, FLAG_T)
    self_here = [moves.whole(bank.at[section, j], wide.at[:, j * width : (j + 1) * width]) for j in range(3)]
    mem_here = moves.pair(mem_in, mem, flag_m)
    pair_here = [moves.whole(bank.at[section, 5 + j], pairw.at[:, j * width : (j + 1) * width]) for j in range(2)]
    rest_here = [moves.whole(bank.at[section, j], place) for j, place in ((3, third), (4, fourth), (7, last))]
    go = (lambda rows: go_rows[rows, layer : layer + 1])
    x_here()
    for wait in self_here:
        wait()

    def self_in(rows, _):
        a = norm(x[rows, :].astype(f32), gain[0:1, :]).astype(bf16)
        both = dot(a, wide[...])
        qkv[rows, :width] = (both[:, :width] * 0.125).astype(bf16)
        qkv[rows, width:] = both[:, width:].astype(bf16)
        o1[rows, :] = jnp.zeros((rows.size, width), bf16)
        o2[rows, :] = jnp.zeros((rows.size, width), bf16)

    over(meta, FLAG_T, length, self_in)
    moves.away(qkv, qkv_out, FLAG_T)
    mem_here()
    for wait in pair_here:
        wait()

    def memory_in(rows, _):
        kv[rows, :] = dot(mem[rows, :], pairw[...]).astype(bf16)

    over(meta, flag_m, length, memory_in)
    moves.away(kv, kv_out, flag_m)
    l1[...] = jnp.zeros(l1.shape, f32)
    l2[...] = jnp.zeros(l2.shape, f32)
    attend(
        meta, SELF + kind, TOP_T, info, 0, (qkv, 0), (qkv, width), (qkv, 2 * width), o1, l1,
        both_q, peaks, totals, sums,
    )
    moves.away(o1, o1_out, FLAG_T)
    for wait in rest_here:
        wait()

    def cross_in(rows, _):
        state = x[rows, :].astype(f32) + go(rows) * dot(o1[rows, :], third[...])
        mid[rows, :] = state
        a = norm(state, gain[1:2, :]).astype(bf16)
        q2[rows, :] = (dot(a, fourth[...]) * 0.125).astype(bf16)

    over(meta, FLAG_T, length, cross_in)
    moves.away(mid, mid_out, FLAG_T)
    moves.away(q2, q2_out, FLAG_T)
    attend(
        meta, CROSS + kind, top_m, info, 2, (q2, 0), (kv, 0), (kv, width), o2, l2, both_q, peaks, totals, sums
    )
    moves.away(o2, o2_out, FLAG_T)

    def finish(rows, _):
        out[rows, :] = (mid[rows, :] + go(rows) * dot(o2[rows, :], last[...])).astype(bf16)

    over(meta, FLAG_T, length, finish)
    moves.away(out, final, FLAG_T)
    moves.finish()


def attention_backward_kernel(
    layer, meta, bank, x_in, mem_in, gain, go_rows, info,
    qkv_in, o1_in, l1, mid_in, q2_in, kv_in, o2_in, l2, dh_in, *rest,
):
    entry = layer == 0
    if entry:
        dmem_in, *rest = rest
    (
        dx_out, dmem_out, dw_out, dgain,
        x, mem, qkv, o1, mid, q2, kv, o2, dh, dx, dmem, dw,
        wide, third, fourth, pairw, last,
        dstate, do, dqkv, dk, dv, delta, heads, both_q, both_o, sums, acc, semaphores,
    ) = rest
    length, width = x.shape
    kind, flag_m, top_m = 4 * layer, FLAG_M + 2 * layer, TOP_M + 2 * layer
    moves = Moves(meta, length, semaphores)
    section = 2 * layer
    first_here = [
        moves.pair(dh_in, dh, FLAG_T), moves.whole(bank.at[section, 7], last), moves.pair(o2_in, o2, FLAG_T),
        moves.pair(q2_in, q2, FLAG_T), moves.pair(kv_in, kv, flag_m),
    ]
    if entry:
        first_here.append(moves.whole(dmem_in, dmem))
    second_here = [moves.pair(mem_in, mem, flag_m), moves.pair(mid_in, mid, FLAG_T)]
    second_here += [moves.whole(bank.at[section, 5 + j], pairw.at[:, j * width : (j + 1) * width]) for j in range(2)]
    second_here += [moves.whole(bank.at[section, 4], fourth)]
    third_here = [moves.whole(bank.at[section, 3], third), moves.pair(o1_in, o1, FLAG_T), moves.pair(qkv_in, qkv, FLAG_T)]
    fourth_here = [moves.whole(bank.at[section, j], wide.at[:, j * width : (j + 1) * width]) for j in range(3)]
    fourth_here += [moves.pair(x_in, x, FLAG_T)]
    go = (lambda rows: go_rows[rows, layer : layer + 1])

    row_of = lax.broadcasted_iota(i32, (HEADS, width), 0)
    lane_of = lax.broadcasted_iota(i32, (HEADS, width), 1)
    heads[...] = (lane_of // (width // HEADS) == row_of).astype(bf16)
    dk[...] = jnp.zeros(dk.shape, f32)
    dv[...] = jnp.zeros(dv.shape, f32)
    delta[...] = jnp.zeros(delta.shape, f32)
    if not entry:
        dmem[...] = jnp.zeros(dmem.shape, bf16)
    if entry:
        dx[...] = jnp.zeros(dx.shape, bf16)

    def weight_grad(targets, flag, left, right):
        size = len(targets) * width

        def part(rows, fresh):
            term = dot_tn(left(rows), right(rows))
            acc[:, :size] = term if fresh else acc[:, :size] + term

        over(meta, flag, length, part)
        for n, j in enumerate(targets):
            dw[j] = acc[:, n * width : (n + 1) * width].astype(bf16)
            moves.away(dw.at[j], dw_out.at[j])

    def begin(grad_of, o, out_weight, target):
        def dy(rows):
            return (go(rows) * grad_of(rows)).astype(bf16)

        def part(rows, _):
            grad = dot_nt(dy(rows), out_weight[...]).astype(bf16)
            do[rows, :] = grad
            product = grad.astype(f32) * o[rows, :].astype(f32)
            high = product.astype(bf16)
            rest = (product - high.astype(f32)).astype(bf16)
            delta[:, rows] = dot_nt(heads[...], high) + dot_nt(heads[...], rest)
            dqkv[rows, :width] = jnp.zeros((rows.size, width), bf16)

        over(meta, FLAG_T, length, part)
        weight_grad([target], FLAG_T, lambda rows: o[rows, :], dy)

    def top_grad(rows):
        return dh[rows, :].astype(f32)

    for wait in first_here:
        wait()
    begin(top_grad, o2, last, 7)
    attend_back(
        meta, CROSS + kind, top_m, info, 2, (q2, 0), (kv, 0), (kv, width), l2, delta, do, (dqkv, 0), dk, dv,
        both_q, both_o, sums,
    )
    for wait in second_here:
        wait()

    def memory_out(rows, _):
        dqkv[rows, width : 2 * width] = dk[rows, :].astype(bf16)
        dqkv[rows, 2 * width :] = dv[rows, :].astype(bf16)
        term = dot_nt(dqkv[rows, width:], pairw[...])
        dmem[rows, :] = (dmem[rows, :].astype(f32) + term).astype(bf16)

    over(meta, flag_m, length, memory_out)
    moves.away(dmem, dmem_out)
    weight_grad([5, 6], flag_m, lambda rows: mem[rows, :], lambda rows: dqkv[rows, width:])

    def cross_out(rows, fresh):
        grad_x, grad_gain = norm_back(mid[rows, :], gain[1:2, :], dot_nt(dqkv[rows, :width], fourth[...]))
        dstate[rows, :] = top_grad(rows) + grad_x
        dgain[1:2, :] = grad_gain if fresh else dgain[1:2, :] + grad_gain

    over(meta, FLAG_T, length, cross_out)
    weight_grad(
        [4], FLAG_T, lambda rows: norm(mid[rows, :], gain[1:2, :]).astype(bf16), lambda rows: dqkv[rows, :width]
    )
    for wait in third_here:
        wait()
    dk[...] = jnp.zeros(dk.shape, f32)
    dv[...] = jnp.zeros(dv.shape, f32)
    begin(lambda rows: dstate[rows, :], o1, third, 3)
    attend_back(
        meta, SELF + kind, TOP_T, info, 0, (qkv, 0), (qkv, width), (qkv, 2 * width), l1, delta, do, (dqkv, 0), dk, dv,
        both_q, both_o, sums,
    )
    for wait in fourth_here:
        wait()

    def self_out(rows, fresh):
        dqkv[rows, width : 2 * width] = dk[rows, :].astype(bf16)
        dqkv[rows, 2 * width :] = dv[rows, :].astype(bf16)
        grad_x, grad_gain = norm_back(x[rows, :].astype(f32), gain[0:1, :], dot_nt(dqkv[rows, :], wide[...]))
        value = dstate[rows, :] + grad_x
        if entry:
            value = jnp.where(go_rows[rows, 2:3] > 0.0, value, 0.0)
        dx[rows, :] = value.astype(bf16)
        dgain[0:1, :] = grad_gain if fresh else dgain[0:1, :] + grad_gain

    over(meta, FLAG_T, length, self_out)
    if entry:
        moves.away(dx, dx_out)
    else:
        moves.away(dx, dx_out, FLAG_T)
    weight_grad(
        [0, 1, 2], FLAG_T, lambda rows: norm(x[rows, :].astype(f32), gain[0:1, :]).astype(bf16),
        lambda rows: dqkv[rows, :],
    )
    moves.finish()


def exit_part(layer, vector, frows, rows, target_row, halt, exit_grad, fresh, sentences):
    factor = layer.shape[1] ** (-0.5)
    vectors = jnp.broadcast_to(vector, (8, layer.shape[1]))
    score = jax.nn.sigmoid(exact_nt(vectors, layer) * factor)
    halt[:, rows] = score
    weight = frows[0:1, rows] * (score - frows[target_row : target_row + 1, rows]) / sentences
    term = exact(weight, layer)[0:1] * factor
    exit_grad[...] = term if fresh else exit_grad[...] + term


def dense_weights(moves, bank, section, up, down, width):
    parts = up.shape[1] // width
    here = [moves.whole(bank.at[section, j], up.at[:, j * width : (j + 1) * width]) for j in range(parts)]
    later = [moves.whole(bank.at[section, parts + j], down.at[j * width : (j + 1) * width]) for j in range(parts)]
    return here, later


def dense_forward_kernel(
    sentences, meta, bank, x, gain, frows, final, halt, exit_grad, out, up, down, semaphores
):
    length, width = x.shape
    moves = Moves(meta, length, semaphores)
    here, later = dense_weights(moves, bank, 1, up, down, width)
    for wait in here:
        wait()

    def part(rows, fresh):
        state = x[rows, :].astype(f32)
        a = norm(state, gain[0:1, :]).astype(bf16)
        active = gelu(dot(a, up[...])).astype(bf16)
        if fresh:
            for wait in later:
                wait()
        layer = state + dot(active, down[...])
        out[rows, :] = layer.astype(bf16)
        exit_part(layer, gain[1:2, :], frows, rows, 1, halt, exit_grad, fresh, sentences)

    over(meta, FLAG_T, length, part)
    moves.away(out, final, FLAG_T)
    moves.finish()


def dense_backward_kernel(sentences, final, meta, bank, x, gain, go_rows, frows, dh, before, dx_out, dw_out, dgain, *rest):
    if final:
        states, halt, exit_grad, out, *rest = rest
        out[...] = jnp.zeros(out.shape, bf16)
    else:
        dgain[1:2, :] = before[...]
    dx, dw, up, down, grad_up, grad_down, semaphores = rest
    length, width = x.shape
    moves = Moves(meta, length, semaphores)
    here, later = dense_weights(moves, bank, 3 if final else 1, up, down, width)
    parts = up.shape[1] // width
    for wait in here:
        wait()

    def part(rows, fresh):
        grad_out = dh[rows, :].astype(f32)
        if final:
            grad_out = jnp.where(go_rows[rows, 2:3] > 0.0, grad_out, 0.0)
        go = go_rows[rows, int(final) : int(final) + 1]
        state = x[rows, :].astype(f32)
        a = norm(state, gain[0:1, :]).astype(bf16)
        dy = (go * grad_out).astype(bf16)
        active, slope = gelu_both(dot(a, up[...]))
        active = active.astype(bf16)
        if fresh:
            for wait in later:
                wait()
        dhidden = (slope * dot_nt(dy, down[...])).astype(bf16)
        downs, ups = dot_tn(active, dy), dot_tn(a, dhidden)
        if fresh:
            grad_down[...] = downs
            grad_up[...] = ups
        else:
            grad_down[...] += downs
            grad_up[...] += ups
        if final:
            layer = state + go * dot(active, down[...])
            out[rows, :] = jnp.where(go_rows[rows, 2:3] > 0.0, layer, 0.0).astype(bf16)
            exit_part(layer, gain[1:2, :], frows, rows, 2, halt, exit_grad, fresh, sentences)
        grad_x, grad_gain = norm_back(state, gain[0:1, :], dot_nt(dhidden, up[...]))
        dx[rows, :] = (grad_out + grad_x).astype(bf16)
        dgain[0:1, :] = grad_gain if fresh else dgain[0:1, :] + grad_gain

    over(meta, FLAG_T, length, part)
    moves.away(dx, dx_out, FLAG_T)
    if final:
        moves.away(out, states)
        dgain[1:2, :] = exit_grad[...]
        mine = frows[3:4, :] > 0.0
        halt[1:2, :] = jnp.where(mine, halt[1:2, :], 0.0)
        halt[0:1, :] = jnp.where(mine, before[0:1, :], 0.0)
    for j in range(parts):
        dw[parts + j] = grad_down[j * width : (j + 1) * width, :].astype(bf16)
        dw[j] = grad_up[:, j * width : (j + 1) * width].astype(bf16)
        moves.away(dw.at[j], dw_out.at[j])
        moves.away(dw.at[parts + j], dw_out.at[parts + j])
    moves.finish()


def plan_kernel(sentences, row, core, seg, pad, mseg, mmask, depths, meta, info, frows, cols):
    row, core = row[0], core[0]
    length, slots = seg.shape[1], mseg.shape[1]
    blocks = length // BLOCK
    seg, pad, mseg, mmask = (t[pl.ds(row, 1), :] for t in (seg, pad, mseg, mmask))
    number = lax.broadcasted_iota(i32, (sentences, length), 0)
    place = lax.broadcasted_iota(i32, (1, length), 1)

    def count(marks):
        return jnp.sum(marks.astype(f32), axis=1, keepdims=True).astype(i32)

    square = lax.broadcasted_iota(i32, (sentences, sentences), 0) == lax.broadcasted_iota(
        i32, (sentences, sentences), 1
    )
    depth_row = jnp.broadcast_to(depths[pl.ds(row, 1), :], (sentences, sentences))
    depth_table = jnp.sum(jnp.where(square, depth_row, 0).astype(f32), axis=1, keepdims=True).astype(i32)
    mine = seg == number
    starts = count(seg < number)
    filled = count(pad == 1)
    memory_number = lax.broadcasted_iota(i32, (sentences, slots), 0)
    memory_starts = count(mseg < memory_number)
    memory_stops = jnp.minimum(count(mseg <= memory_number), count(mmask == 1))

    def of_token(table):
        return jnp.sum(jnp.where(mine, table, 0), axis=0, keepdims=True)

    low = of_token(starts)
    high = jnp.where(pad == 1, jnp.minimum(place, filled - 1), place) + 1
    cross_low = jnp.where(pad == 0, 0, of_token(memory_starts))
    cross_high = jnp.where(pad == 0, slots, of_token(memory_stops))
    depth = of_token(depth_table)
    keep = depth == 2

    def by_block(values):
        return jnp.concatenate([values[:, i * BLOCK : (i + 1) * BLOCK] for i in range(blocks)], axis=0)

    def spans(used, lows, highs):
        lows = jnp.min(by_block(jnp.where(used, lows, slots)), axis=1, keepdims=True)
        highs = jnp.max(by_block(jnp.where(used, highs, 0)), axis=1, keepdims=True)
        return jnp.minimum(lows, highs) // STEP * STEP, highs

    work = jnp.zeros((blocks, 1), i32)
    for used in (place >= 0, keep):
        for lows, highs in ((low, high), (cross_low, cross_high)):
            from_, to = spans(used, lows, highs)
            work = work + 2 * ((to - from_ + KEYS - 1) // KEYS) + jnp.where(to > from_, 1, 0)
    start = jnp.sum(jnp.where(square, starts, 0), axis=0, keepdims=True)
    block_at = lax.broadcasted_iota(i32, (blocks, sentences), 0) * BLOCK
    before = jnp.sum(jnp.where(block_at < start, work, 0), axis=0, keepdims=True)
    after = jnp.sum(jnp.where(block_at + BLOCK > start, work, 0), axis=0, keepdims=True)
    after = after + jnp.where(filled < length, 5, 0)
    off = jnp.abs(start - length // 2)
    score = jnp.maximum(before, after) * length + off
    score = score + jnp.where(off > length // 8, length * length, 0)
    score = jnp.where(lax.broadcasted_iota(i32, (1, sentences), 1) > 0, score, 2 * length * length)
    best = jnp.min(score, axis=1, keepdims=True)
    cut = jnp.min(jnp.where(score == best, start, length), axis=1, keepdims=True)

    def by_core(first, second):
        return first * (1 - core) + second * core

    below = jnp.where(place < cut, 1, 0)
    owned = by_core(below, 1 - below) == 1
    begin = by_core(0, cut // BLOCK)
    end = by_core((cut + BLOCK - 1) // BLOCK, blocks)
    wide = length * 5 // 8
    base = by_core(0, length - wide)

    def outside(from_place, to_place):
        return by_core(jnp.where(to_place > wide, 1, 0), jnp.where(from_place < length - wide, 1, 0))

    def top_of(flag):
        return jnp.where(flag == 1, length - KEYS, base + wide - KEYS)

    lane = lax.broadcasted_iota(i32, (blocks, 128), 1)
    table = jnp.zeros((blocks, 128), i32)
    flag_t = outside(begin * BLOCK, end * BLOCK)
    entries = {CORE: jnp.full((1, 1), core, i32), FLAG_T: flag_t, FIRST: begin, LAST: end, TOP_T: top_of(flag_t)}
    for layer in range(2):
        used = owned if layer == 0 else owned & keep
        for kind, lows, highs in ((SELF, low, high), (CROSS, cross_low, cross_high)):
            entries[kind + 4 * layer], entries[kind + 4 * layer + 1] = spans(used, lows, highs)
        flag_m = outside(
            jnp.min(jnp.where(used, cross_low, slots), axis=1, keepdims=True),
            jnp.max(jnp.where(used, cross_high, 0), axis=1, keepdims=True),
        )
        entries[FLAG_M + 2 * layer] = flag_m
        entries[TOP_M + 2 * layer] = top_of(flag_m)
    for column, values in entries.items():
        table = jnp.where(lane == column, values, table)
    meta[...] = table
    info[...] = jnp.concatenate([low, high, cross_low, cross_high, low, low, low, low], axis=0)
    ones = jnp.ones((1, length), f32)
    kept, own = keep.astype(f32), owned.astype(f32)
    counted = jnp.where(pad == 1, own, 0.0)
    frows[...] = jnp.concatenate([counted, (depth == 1).astype(f32), ones, own, ones, ones, ones, ones], axis=0)
    by_row = jnp.concatenate([ones, kept, own, own, own, own, own, own], axis=0)
    for i in range(blocks):
        cols[i * BLOCK : (i + 1) * BLOCK, :] = by_row[:, i * BLOCK : (i + 1) * BLOCK].T


ANY = pl.BlockSpec(memory_space=pltpu.HBM)
VMEM = pl.BlockSpec(memory_space=pltpu.VMEM)
SMEM = pl.BlockSpec(memory_space=pltpu.SMEM)


def make_plan(row, core, ints):
    seg, pad, mseg, mmask, depths = ints
    length, sentences = seg.shape[1], depths.shape[1]
    outs = [((length // BLOCK, 128), i32), ((8, length), i32), ((8, length), f32), ((length, 8), f32)]
    return pl.pallas_call(
        functools.partial(plan_kernel, sentences),
        out_shape=[jax.ShapeDtypeStruct(*out) for out in outs],
        in_specs=[SMEM, SMEM] + [VMEM] * 5,
        out_specs=[VMEM] * 4,
        compiler_params=pltpu.CompilerParams(vmem_limit_bytes=60 * 2**20),
        name="make_plan",
    )(row.astype(i32)[None], core.astype(i32)[None], seg, pad, mseg, mmask, depths)


def run(kernel, ins, outs, scratch, semaphores, name, flops, *args):
    return pl.pallas_call(
        kernel,
        out_shape=[jax.ShapeDtypeStruct(shape, dtype) for _, shape, dtype in outs],
        in_specs=ins,
        out_specs=[spec for spec, _, _ in outs],
        scratch_shapes=[pltpu.VMEM(shape, dtype) for shape, dtype in scratch]
        + [pltpu.SemaphoreType.DMA((semaphores,))],
        compiler_params=pltpu.CompilerParams(vmem_limit_bytes=60 * 2**20),
        cost_estimate=pl.CostEstimate(flops=flops, bytes_accessed=20 * 2**20, transcendentals=0),
        name=name,
    )(*args)


def attention_forward(layer, plan, bank, x, mem, gain, name):
    meta, info, _, cols = plan
    length, width = x.shape
    pairs = width // BLOCK

    def rows(n, dtype=bf16):
        return ((length, n * width), dtype)

    logs = (VMEM, (HEADS, length), f32)
    kept = [rows(3), rows(1), logs[1:], rows(1, f32), rows(1), rows(2), rows(1), logs[1:], rows(1)]
    outs = [(VMEM if shape[0] == HEADS else ANY, shape, dtype) for shape, dtype in kept]
    square = ((width, width), bf16)
    scratch = [
        rows(1), rows(1), rows(3), rows(1), rows(1, f32), rows(1), rows(2), rows(1), rows(1),
        ((width, 3 * width), bf16), square, square, ((width, 2 * width), bf16), square,
        ((pairs, 2 * BLOCK, BLOCK), bf16), ((8, 2 * BLOCK), f32), ((8, 2 * BLOCK), f32), ((pairs, BLOCK, BLOCK), f32),
    ]
    return run(
        functools.partial(attention_forward_kernel, layer), [SMEM, ANY, ANY, ANY, VMEM, VMEM, VMEM], outs, scratch, 32,
        name, 6 * 10**9, meta, bank, x, mem, gain, cols, info,
    )


def attention_backward(layer, plan, bank, x, mem, gain, saved, dh, dmem, name):
    meta, info, _, cols = plan
    length, width = x.shape
    pairs = width // BLOCK

    def rows(n, dtype=bf16):
        return ((length, n * width), dtype)

    square, matrices = ((width, width), bf16), (bank.shape[1:], bf16)
    outs = [(ANY, *rows(1)), (ANY, *rows(1)), (ANY, *matrices), (VMEM, (2, width), f32)]
    both = ((pairs, 2 * BLOCK, BLOCK), bf16)
    scratch = [
        rows(1), rows(1), rows(3), rows(1), rows(1, f32), rows(1), rows(2), rows(1), rows(1), rows(1), rows(1), matrices,
        ((width, 3 * width), bf16), square, square, ((width, 2 * width), bf16), square,
        rows(1, f32), rows(1), rows(3), rows(1, f32), rows(1, f32), ((HEADS, length), f32), ((HEADS, width), bf16),
        both, both, ((pairs, BLOCK, BLOCK), f32), ((width, 3 * width), f32),
    ]
    ins = [SMEM, ANY, ANY, ANY, VMEM, VMEM, VMEM, ANY, ANY, VMEM, ANY, ANY, ANY, ANY, VMEM, ANY] + [ANY] * len(dmem)
    return run(
        functools.partial(attention_backward_kernel, layer), ins, outs, scratch, 48,
        name, 12 * 10**9, meta, bank, x, mem, gain, cols, info, *saved, dh, *dmem,
    )


def dense_forward(plan, bank, x, gain, sentences, name):
    meta, _, frows, _ = plan
    length, width = x.shape
    wide = ((length, width), bf16)
    hidden = bank.shape[1] // 2 * width
    outs = [(ANY, *wide), (VMEM, (8, length), f32), (VMEM, (1, width), f32)]
    return run(
        functools.partial(dense_forward_kernel, sentences), [SMEM, ANY, VMEM, VMEM, VMEM], outs,
        [wide, ((width, hidden), bf16), ((hidden, width), bf16)], 16,
        name, 4 * 10**9, meta, bank, x, gain, frows,
    )


def dense_backward(plan, bank, x, gain, dh, before, sentences, final, name):
    meta, _, frows, cols = plan
    length, width = x.shape
    wide = ((length, width), bf16)
    hidden = bank.shape[1] // 2 * width
    outs = [(ANY, *wide), (ANY, bank.shape[1:], bf16), (VMEM, (2, width), f32)]
    scratch = [wide, (bank.shape[1:], bf16), ((width, hidden), bf16), ((hidden, width), bf16),
               ((width, hidden), f32), ((hidden, width), f32)]
    if final:
        outs += [(ANY, *wide), (VMEM, (8, length), f32)]
        scratch = [((1, width), f32), wide] + scratch
    return run(
        functools.partial(dense_backward_kernel, sentences, final), [SMEM, ANY] + [VMEM] * 6, outs, scratch, 24,
        name, 8 * 10**9, meta, bank, x, gain, cols, frows, dh, before,
    )


def row_forward_backward(row, core, x, mem, cotangent, bank, gains, ints):
    plan = make_plan(row, core, ints)
    sentences = ints[-1].shape[1]
    *saved0, zero = attention_forward(0, plan, bank, x, mem, gains[0], "attend_zero")
    one, halt, exit0 = dense_forward(plan, bank, zero, gains[1], sentences, "dense_one")
    *saved2, two = attention_forward(1, plan, bank, one, mem, gains[2], "attend_two")
    dtwo, dw3, dgain3, states, halt = dense_backward(
        plan, bank, two, gains[3], cotangent, halt, sentences, True, "dense_three"
    )
    done, dmem, dw2, dgain2 = attention_backward(1, plan, bank, one, mem, gains[2], saved2, dtwo, (), "attend_two_back")
    dzero, dw1, dgain1 = dense_backward(plan, bank, zero, gains[1], done, exit0, sentences, False, "dense_one_back")
    dx, dmem, dw0, dgain0 = attention_backward(
        0, plan, bank, x, mem, gains[0], saved0, dzero, (dmem,), "attend_zero_back"
    )
    return states, halt, dx, dmem, [dw0, dw1, dw2, dw3], [dgain0, dgain1, dgain2, dgain3]


MESH = pl.DeviceIdType.MESH


def neighbours():
    s, d = lax.axis_index("section"), lax.axis_index("dp")
    across = [(s + 1 - 2 * (s % 2), d), ((s + 2) % 4, d), (3 - s, d)]
    layer = d // 2
    along = (s, d + 2 - 4 * (layer % 2))
    sibling = (s, d + 1 - 2 * (d % 2))
    return s, d, across, along, sibling


def greet(devices):
    barrier = pltpu.get_barrier_semaphore()
    for device in devices:
        pl.semaphore_signal(barrier, inc=1, device_id=device, device_id_type=MESH)
    pl.semaphore_wait(barrier, len(devices))


SUBS = 4


def gather_kernel(
    states, memory, cotangent, bank, gains, seg, pad, mseg, mmask, depths,
    x, mem, top, weights, gains_all, seg2, pad2, mseg2, mmask2, depths2,
    staging, send, recv, home,
):
    s, d, across, along, sibling = neighbours()
    core = d % 2
    parity = (d // 2) % 2
    greet(across + [along, sibling])
    started = []
    locals_ = []
    count = [0, 0]

    def push(src, dst, device):
        i = count[0]
        count[0] += 1
        copy = pltpu.make_async_remote_copy(src, dst, send.at[i], recv.at[i], device_id=device, device_id_type=MESH)
        return copy

    def go(src, dst, device):
        copy = push(src, dst, device)
        copy.start()
        started.append(copy)
        return copy

    def keep(src, dst):
        i = count[1]
        count[1] += 1
        copy = pltpu.make_async_copy(src, dst, home.at[i])
        return copy

    shares = states.shape[2]
    chips = [s] + [a[0] for a in across]
    sent_inputs, own_inputs = [], []
    for source, whole in ((states, x), (memory, mem), (cotangent, top)):
        for rel in range(4):
            target = chips[rel]
            mine = target // 2 == core
            dst = whole.at[:, pl.ds(pl.multiple_of(s * shares, shares), shares)]
            src = source.at[target % 2]
            if rel == 0:
                copy = keep(src, dst)
                own_inputs.append(copy)
            else:
                copy = push(src, dst, across[rel - 1])
                sent_inputs.append((copy, whole, rel))
            pl.when(mine)(copy.start)
    small = [go(source, whole.at[core], sibling)
             for source, whole in ((seg, seg2), (pad, pad2), (mseg, mseg2), (mmask, mmask2), (depths, depths2))]
    small += [go(gains, gains_all.at[s], device) for device in across]
    for source, whole in ((seg, seg2), (pad, pad2), (mseg, mseg2), (mmask, mmask2), (depths, depths2)):
        copy = keep(source, whole.at[core])
        copy.start()
        locals_.append(copy)
    copy = keep(gains, gains_all.at[s])
    copy.start()
    locals_.append(copy)

    span = bank.shape[0]
    half = span // 2
    third = half // 3 // (16 * SUBS) * (16 * SUBS)
    first = half - 2 * third
    sub0, sub1 = first // SUBS, third // SUBS

    def rows(section, part, i):
        at = section * span + core * half
        size = sub0 if part == 0 else sub1
        if part == 0:
            at = at + i * size
        elif part == 1:
            at = at + first + parity * third + i * size
        else:
            at = at + first + (1 - parity) * third + i * size
        return weights.at[pl.ds(pl.multiple_of(at, 16), size)]

    def own_rows(part, i):
        size = sub0 if part == 0 else sub1
        at = core * half + (i * size if part == 0 else first + parity * third + i * size)
        return bank.at[pl.ds(pl.multiple_of(at, 16), size)]

    direct = {}
    for part in (1, 0):
        for i in range(SUBS):
            for k in range(2):
                direct[k, part, i] = go(own_rows(part, i), rows(s, part, i), across[k])
    lift = keep(bank, staging)
    lift.start()
    drop = keep(staging, weights.at[pl.ds(pl.multiple_of(s * span, span), span)])

    holder = s // 2 == core
    handed = []
    for n, (source, whole) in enumerate(((states, x), (memory, mem), (cotangent, top))):
        for rel in range(4):
            lanes = whole.at[:, pl.ds(pl.multiple_of(chips[rel] * shares, shares), shares)]
            copy = push(lanes, lanes, sibling)
            handed.append(copy)
            arrived = own_inputs[n] if rel == 0 else sent_inputs[n * 3 + rel - 1][0]

            def hand(copy=copy, arrived=arrived, rel=rel):
                if rel == 0:
                    arrived.wait()
                else:
                    arrived.wait_recv()
                copy.start()

            pl.when(holder)(hand)

    lift.wait()
    drop.start()
    locals_.append(drop)
    far = {}
    lifted = {}
    passed = []

    def arrive(copy, section, part, i):
        copy.wait_recv()
        passed.append(go(rows(section, part, i), rows(section, part, i), sibling))

    for i in range(SUBS):
        arrive(direct[0, 1, i], chips[1], 1, i)
        far[1, i] = go(rows(chips[1], 1, i), rows(chips[1], 1, i), across[1])
        lifted[1, i] = go(rows(chips[1], 1, i), rows(chips[1], 1, i), along)
        arrive(direct[1, 1, i], chips[2], 1, i)
        lifted[2, i] = go(rows(chips[2], 1, i), rows(chips[2], 1, i), along)
    for i in range(SUBS):
        arrive(direct[1, 0, i], chips[2], 0, i)
        far[0, i] = go(rows(chips[2], 0, i), rows(chips[2], 0, i), across[0])
        arrive(direct[0, 0, i], chips[1], 0, i)
    for i in range(SUBS):
        arrive(far[1, i], chips[3], 1, i)
        lifted[3, i] = go(rows(chips[3], 1, i), rows(chips[3], 1, i), along)
    for i in range(SUBS):
        arrive(far[0, i], chips[3], 0, i)
    for k in range(1, 4):
        for i in range(SUBS):
            arrive(lifted[k, i], chips[k], 2, i)
    for copy in passed + small:
        copy.wait_recv()
    for copy in handed:
        pl.when(jnp.logical_not(holder))(copy.wait_recv)
        pl.when(holder)(copy.wait_send)
    for (copy, whole, rel) in sent_inputs:
        pl.when(chips[rel] // 2 == core)(copy.wait_send)
    for copy in started:
        copy.wait_send()
    for copy in locals_:
        copy.wait()


def gather_all(states, memory, cotangent, bank, gains, ints):
    micro, length, shares = states.shape
    sections = lax.axis_size("section")
    width = shares * sections
    wide = jax.ShapeDtypeStruct((length, width), bf16)
    copies = 9 + 12 + 8 + 4 * SUBS + 2 * SUBS + 3 * SUBS + 9 * SUBS
    outs = [wide, wide, wide, jax.ShapeDtypeStruct((sections * bank.shape[0], width), bf16),
            jax.ShapeDtypeStruct((sections,) + gains.shape, f32)]
    outs += [jax.ShapeDtypeStruct((2,) + t.shape, t.dtype) for t in ints]
    return pl.pallas_call(
        gather_kernel,
        out_shape=outs,
        in_specs=[ANY] * 10,
        out_specs=[ANY] * 10,
        scratch_shapes=[pltpu.VMEM(bank.shape, bank.dtype), pltpu.SemaphoreType.DMA((copies,)), pltpu.SemaphoreType.DMA((copies,)),
                        pltpu.SemaphoreType.DMA((12,))],
        compiler_params=pltpu.CompilerParams(collective_id=0, has_side_effects=True, vmem_limit_bytes=60 * 2**20),
        name="gather_all",
    )(states, memory, cotangent, bank, gains, *ints)


GROUPS = 8
AHEAD = 2
RESULTS = 7


def add_rows(target, rows, *others):
    total = target[rows].astype(f32)
    for other, places in others:
        total = total + other[places].astype(f32)
    target[rows] = total.astype(bf16)


def reduce_kernel(
    dw0, dw1, dw2, dw3, gains, states, dx, dmem, halt,
    bank, gains_sum, states_out, dx_out, dmem_out, halt_out,
    own, other, first, second, left, right, total, full, mine, theirs, score, scores,
    gain_parts, send, recv, home,
):
    s, d, across, _, sibling = neighbours()
    core, layer = d % 2, d // 2
    chips = [s] + [a[0] for a in across]
    column = [(s, (layer + k) % 4 * 2 + core) for k in range(1, 4)]
    up, down = (s, d + 2), (s, d - 2)
    pair = (s, d + 2 - 4 * (layer % 2))
    jump = (s, (layer + 2) % 4 * 2 + core)
    holder = s // 2 == core
    greet(across + [sibling] + column)
    count = [0, 0]
    always, ends = [], []

    def push(src, dst, device):
        i = count[0]
        count[0] += 1
        return pltpu.make_async_remote_copy(src, dst, send.at[i], recv.at[i], device_id=device, device_id_type=MESH)

    def go(src, dst, device):
        copy = push(src, dst, device)
        copy.start()
        always.append(copy)
        return copy

    def fetch(src, dst):
        i = count[1]
        count[1] += 1
        copy = pltpu.make_async_copy(src, dst, home.at[i])
        return copy

    span = dw0.shape[0]
    half = span // 2
    quarter = half // 2
    piece = quarter // GROUPS
    grads = (dw0, dw1, dw2, dw3)

    def at(g, side):
        return side * quarter + g * piece

    loads, swaps = {}, {}

    def exchange(g):
        for t in range(4):
            for side in range(2):
                rows = pl.ds(at(g, side), piece)
                there = pl.ds(pl.multiple_of((1 - core) * half + at(g, side), piece), piece)
                here = pl.ds(pl.multiple_of(core * half + at(g, side), piece), piece)
                swaps[g, t, side] = go(grads[t].at[there], other.at[t, rows], sibling)
                loads[g, t, side] = fetch(grads[t].at[here], own.at[t, rows])
                loads[g, t, side].start()

    for g in range(AHEAD):
        exchange(g)
    outs = ((states, states_out), (dx, dx_out), (dmem, dmem_out))
    given, taken = [], []
    for n, (source, _) in enumerate(outs):
        given.append(push(source, theirs.at[n], sibling))
        taken.append(fetch(source, mine.at[n]))
    given.append(push(halt, scores, sibling))
    taken.append(fetch(halt, score))

    def results_begin():
        for copy in given:
            pl.when(jnp.logical_not(holder))(copy.start)
        for copy in taken:
            pl.when(holder)(copy.start)

    gain_steps = [sibling, across[0], across[1], pair, jump]
    gain_parts[0] = gains[...]
    gain_copies = []

    def gain_step(k):
        if k > 0:
            gain_copies[-1].wait_recv()
            gain_parts[2 * k] = gain_parts[2 * k - 2] + gain_parts[2 * k - 1]
        if k < len(gain_steps):
            gain_copies.append(go(gain_parts.at[2 * k], gain_parts.at[2 * k + 1], gain_steps[k]))
        else:
            gains_sum[...] = gain_parts[2 * k]

    step1, step2, rs, ag = {}, {}, {}, {}

    def plane_first(g):
        if g + AHEAD < GROUPS:
            exchange(g + AHEAD)
        for t in range(4):
            for side in range(2):
                swaps[g, t, side].wait_recv()
                loads[g, t, side].wait()
                rows = pl.ds(at(g, side), piece)
                add_rows(own, (t, rows), (other, (t, rows)))
        for side in range(2):
            rows = pl.ds(at(g, side), piece)
            for n, rel in enumerate((3, 1 + side)):
                step1[g, side, n] = go(own.at[chips[rel], rows], first.at[g, side, n], across[side])

    def plane_second(g):
        for side in range(2):
            rows = pl.ds(at(g, side), piece)
            for n, rel in enumerate((2 - side, 0)):
                step1[g, side, n].wait_recv()
                add_rows(own, (chips[rel], rows), (first, (g, side, n)))
                if n == 0:
                    step2[g, side] = go(own.at[chips[rel], rows], second.at[g, side], across[1 - side])

    def plane_third(g):
        for side in range(2):
            step2[g, side].wait_recv()
            rows = pl.ds(at(g, side), piece)
            value = own[s, rows].astype(f32) + second[g, side].astype(f32)
            total[g, pl.ds(side * piece, piece)] = value.astype(bf16)

    wide = 2 * piece
    shard = wide // 4

    def span_of(k0, k1):
        return pl.ds(k0 * shard, (k1 - k0) * shard)

    def share(kind, g, low, high, src, dst, device):
        return push(src.at[g, span_of(low, high)], dst.at[g, span_of(low, high)], device)

    def line_sums(g):
        for z in range(3):
            rs[g, "up", z] = share("up", g, z + 1, 4, total, right, up)
            rs[g, "down", z + 1] = share("down", g, 0, z + 1, total, left, down)
        for k in range(4):
            for z in range(k, 3):
                ag[g, "up", z, k] = push(full.at[g, span_of(k, k + 1)], full.at[g, span_of(k, k + 1)], up)
            for z in range(1, k + 1):
                ag[g, "down", z, k] = push(full.at[g, span_of(k, k + 1)], full.at[g, span_of(k, k + 1)], down)

    def at_layer(z, action):
        pl.when(layer == z)(action)

    def close(g, k, *others):
        value = total[g, span_of(k, k + 1)].astype(f32)
        for other_ in others:
            value = value + other_[g, span_of(k, k + 1)].astype(f32)
        full[g, span_of(k, k + 1)] = value.astype(bf16)

    def line_1(g):
        line_sums(g)
        at_layer(0, lambda: rs[g, "up", 0].start())
        at_layer(3, lambda: rs[g, "down", 3].start())

    def line_2(g):
        def second_layer():
            rs[g, "up", 0].wait_recv()
            add_rows(total, (g, span_of(2, 4)), (right, (g, span_of(2, 4))))
            rs[g, "up", 1].start()

        def third_layer():
            rs[g, "down", 3].wait_recv()
            add_rows(total, (g, span_of(0, 2)), (left, (g, span_of(0, 2))))
            rs[g, "down", 2].start()

        at_layer(1, second_layer)
        at_layer(2, third_layer)

    def line_3(g):
        def third_layer():
            rs[g, "up", 1].wait_recv()
            add_rows(total, (g, span_of(3, 4)), (right, (g, span_of(3, 4))))
            rs[g, "up", 2].start()
            close(g, 2, right, left)
            ag[g, "up", 2, 2].start()
            ag[g, "down", 2, 2].start()

        def second_layer():
            rs[g, "down", 2].wait_recv()
            add_rows(total, (g, span_of(0, 1)), (left, (g, span_of(0, 1))))
            rs[g, "down", 1].start()
            close(g, 1, right, left)
            ag[g, "up", 1, 1].start()
            ag[g, "down", 1, 1].start()

        at_layer(2, third_layer)
        at_layer(1, second_layer)

    def line_4(g):
        def bottom():
            rs[g, "down", 1].wait_recv()
            close(g, 0, left)
            ag[g, "up", 0, 0].start()

        def top():
            rs[g, "up", 2].wait_recv()
            close(g, 3, right)
            ag[g, "down", 3, 3].start()

        def second_layer():
            ag[g, "down", 2, 2].wait_recv()
            ag[g, "down", 1, 2].start()

        def third_layer():
            ag[g, "up", 1, 1].wait_recv()
            ag[g, "up", 2, 1].start()

        at_layer(0, bottom)
        at_layer(3, top)
        at_layer(1, second_layer)
        at_layer(2, third_layer)

    def line_5(g):
        def bottom():
            ag[g, "down", 1, 1].wait_recv()

        def top():
            ag[g, "up", 2, 2].wait_recv()

        def second_layer():
            ag[g, "up", 0, 0].wait_recv()
            ag[g, "up", 1, 0].start()

        def third_layer():
            ag[g, "down", 3, 3].wait_recv()
            ag[g, "down", 2, 3].start()

        at_layer(0, bottom)
        at_layer(3, top)
        at_layer(1, second_layer)
        at_layer(2, third_layer)

    def line_6(g):
        def bottom():
            ag[g, "down", 1, 2].wait_recv()

        def top():
            ag[g, "up", 2, 1].wait_recv()

        def second_layer():
            ag[g, "down", 2, 3].wait_recv()
            ag[g, "down", 1, 3].start()

        def third_layer():
            ag[g, "up", 1, 0].wait_recv()
            ag[g, "up", 2, 0].start()

        at_layer(0, bottom)
        at_layer(3, top)
        at_layer(1, second_layer)
        at_layer(2, third_layer)

    finals = {}

    def line_7(g):
        at_layer(0, lambda: ag[g, "down", 1, 3].wait_recv())
        at_layer(3, lambda: ag[g, "up", 2, 0].wait_recv())
        for side in range(2):
            here = pl.ds(pl.multiple_of(core * half + at(g, side), piece), piece)
            rows = full.at[g, pl.ds(side * piece, piece)]
            finals[g, side] = go(rows, bank.at[here], sibling)
            copy = fetch(rows, bank.at[here])
            copy.start()
            ends.append(copy)

    handed = []

    def results():
        def collect():
            for copy in taken:
                copy.wait()
            for copy in given:
                copy.wait_recv()
            size = mine.shape[1] // 8

            def add(i, _):
                rows = pl.ds(pl.multiple_of(i * size, size), size)
                for n in range(3):
                    add_rows(mine, (n, rows), (theirs, (n, rows)))
                return 0

            lax.fori_loop(0, 8, add, 0)
            score[...] = score[...] + scores[...]

        pl.when(holder)(collect)
        for rel in range(4):
            target = chips[rel]
            for n in range(4):
                out = (states_out, dx_out, dmem_out, halt_out)[n]
                share_ = out.shape[2]
                src = score if n == 3 else mine.at[n]
                src = src.at[:, pl.ds(pl.multiple_of(target * share_, share_), share_)]
                if rel == 0:
                    copy = fetch(src, out.at[s % 2])
                else:
                    copy = push(src, out.at[s % 2], across[rel - 1])
                pl.when(holder)(copy.start)
                handed.append((rel, copy))

    stages = [plane_first, plane_second, plane_third, line_1, line_2, line_3, line_4, line_5, line_6, line_7]
    lags = [0, 1, 2, 2, 3, 3, 4, 4, 5, 5]
    for tick in range(GROUPS + 6):
        for stage, lag in zip(stages, lags):
            if 0 <= tick - lag < GROUPS:
                stage(tick - lag)
        if tick <= len(gain_steps):
            gain_step(tick)
        if tick == RESULTS - 1:
            results_begin()
        if tick == RESULTS:
            results()

    for rel, copy in handed:
        if rel == 0:
            pl.when(holder)(copy.wait)
        else:
            pl.when(chips[rel] // 2 == core)(copy.wait_recv)
            pl.when(holder)(copy.wait_send)
    for copy in given:
        pl.when(jnp.logical_not(holder))(copy.wait_send)
    for copy in finals.values():
        copy.wait_recv()
    for copy in always:
        copy.wait_send()
    for copy in ends:
        copy.wait()
    for (g, way, z), copy in rs.items():
        at_layer(z, copy.wait_send)
    for (g, way, z, k), copy in ag.items():
        at_layer(z, copy.wait_send)


def reduce_all(dw, gains, states, dx, dmem, halt, sections):
    length, width = states.shape
    span = dw[0].shape[0]
    half = span // 2
    piece = half // 2 // GROUPS
    shares = width // sections
    micro = 2
    share = jax.ShapeDtypeStruct((micro, length, shares), bf16)
    outs = [jax.ShapeDtypeStruct((span, width), bf16), jax.ShapeDtypeStruct(gains.shape, f32), share, share, share,
            jax.ShapeDtypeStruct((micro, halt.shape[0], length // sections), f32)]
    copies = 8 * GROUPS + 4 + 5 + (4 + 2 + 6 + 12 + 2) * GROUPS + 12
    scratch = [
        pltpu.VMEM((4, half, width), bf16), pltpu.VMEM((4, half, width), bf16),
        pltpu.VMEM((GROUPS, 2, 2, piece, width), bf16), pltpu.VMEM((GROUPS, 2, piece, width), bf16),
        pltpu.VMEM((GROUPS, 2 * piece, width), bf16), pltpu.VMEM((GROUPS, 2 * piece, width), bf16),
        pltpu.VMEM((GROUPS, 2 * piece, width), bf16), pltpu.VMEM((GROUPS, 2 * piece, width), bf16),
        pltpu.VMEM((3, length, width), bf16), pltpu.VMEM((3, length, width), bf16),
        pltpu.VMEM(halt.shape, f32), pltpu.VMEM(halt.shape, f32),
        pltpu.VMEM((11,) + gains.shape, f32),
        pltpu.SemaphoreType.DMA((copies,)), pltpu.SemaphoreType.DMA((copies,)),
        pltpu.SemaphoreType.DMA((8 * GROUPS + 4 + 2 * GROUPS + 4,)),
    ]
    return pl.pallas_call(
        reduce_kernel,
        out_shape=outs,
        in_specs=[ANY] * 4 + [VMEM] + [ANY] * 4,
        out_specs=[ANY, VMEM, ANY, ANY, ANY, ANY],
        scratch_shapes=scratch,
        compiler_params=pltpu.CompilerParams(collective_id=1, has_side_effects=True, vmem_limit_bytes=52 * 2**20),
        name="reduce_all",
    )(*dw, gains, states, dx, dmem, halt)


def swap_cores(value):
    count = lax.axis_size("dp")
    return lax.ppermute(value, "dp", [(i, i ^ 1) for i in range(count)])


def gather_plain(states, memory, cotangent, bank, gains, ints):
    section, core = lax.axis_index("section"), lax.axis_index("dp") % 2
    micro = states.shape[0]
    holder = section // micro == core

    def pick(rows):
        own = lax.dynamic_index_in_dim(rows, section % micro, 0, keepdims=False)
        return jnp.where(holder, own, swap_cores(own))

    wide = [pick(lax.all_gather(t, "section", axis=2, tiled=True)) for t in (states, memory, cotangent)]
    return wide, lax.all_gather(bank, "section"), lax.all_gather(gains, "section"), [pick(t) for t in ints]


def reduce_plain(dw, dgains, states, dx, dmem, halt):
    section, core = lax.axis_index("section"), lax.axis_index("dp") % 2
    micro = 2
    holder = section // micro == core

    def to_shares(value):
        both = value.astype(f32) + swap_cores(value).astype(f32)
        both = jnp.where(holder, both, 0).astype(value.dtype)
        slots = jnp.stack([jnp.where(section % micro == i, both, 0) for i in range(micro)])
        return lax.psum_scatter(slots, "section", scatter_dimension=2, tiled=True)

    bank = lax.psum_scatter(jnp.stack(dw), "section", scatter_dimension=0, tiled=True)[0]
    bank = lax.psum(bank.astype(f32), "dp")
    gain_sum = lax.psum_scatter(jnp.stack(dgains), "section", scatter_dimension=0, tiled=True)[0]
    gain_sum = lax.psum(gain_sum, "dp")
    return bank, gain_sum, *[to_shares(t) for t in (states, dx, dmem, halt)]


def local(
    states_in, memory, cotangent, weight_bank, gain_bank, segments, pad_mask, memory_segments, memory_mask, exit_depths
):
    section, sections = lax.axis_index("section"), lax.axis_size("section")
    core = lax.axis_index("dp") % 2
    matrices = weight_bank.shape[1:]
    width = matrices[-1]
    ints = (segments, pad_mask, memory_segments, memory_mask, exit_depths)
    near = sections == 4 and lax.axis_size("dp") == 8
    if near:
        x, mem, top, bank, gains, *ints = gather_all(
            states_in, memory, cotangent, weight_bank[0].reshape(-1, width), gain_bank[0], ints
        )
        bank = bank.reshape((sections,) + matrices)
        ints, row = [t.reshape(-1, t.shape[-1]) for t in ints], section
    else:
        (x, mem, top), bank, gains, ints = gather_plain(
            states_in, memory, cotangent, weight_bank[0], gain_bank[0], ints
        )
        ints, row = [t[None] for t in ints], jnp.zeros((), i32)
    states, halt, dx, dmem, dw, dgains = row_forward_backward(
        row, core, x, mem, top, bank, [gains[i] for i in range(sections)], ints
    )
    if near:
        grads = [t.reshape(-1, width) for t in dw]
        bank, gain_sum, states, dx, dmem, halt = reduce_all(
            grads, jnp.concatenate(dgains), states, dx, dmem, halt, sections
        )
        bank = bank.reshape(matrices)
        gain_sum = lax.dynamic_index_in_dim(gain_sum.reshape(sections, 2, width), section, 0, keepdims=False)
    else:
        bank, gain_sum, states, dx, dmem, halt = reduce_plain(dw, dgains, states, dx, dmem, halt)
    return (
        states,
        halt[:, :2],
        dx.astype(f32),
        dmem.astype(f32),
        bank.astype(f32)[None],
        gain_sum[None],
    )


def solution(mesh):
    rows = P("dp", None, "section")
    return jax.shard_map(
        local,
        mesh=mesh,
        in_specs=(
            rows, rows, rows, P("section", None, None, None), P("section", None, None),
            P("dp", None), P("dp", None), P("dp", None), P("dp", None), P("dp", None),
        ),
        out_specs=(rows, rows, rows, rows, P("section", None, None, None), P("section", None, None)),
        check_vma=False,
    )
```

```python
import functools

import jax
import jax.numpy as jnp
from jax import lax
from jax.experimental import pallas as pl
from jax.experimental.pallas import tpu as pltpu
from jax.sharding import PartitionSpec as P

HEADS = 8
EPS = 1e-06
BLOCK = 128
KEYS = 256
STEP = 16
NEG = -1e30

bf16 = jnp.bfloat16
f32 = jnp.float32
i32 = jnp.int32

SELF, CROSS = 0, 2
CORE, FLAG_T, FIRST, LAST, TOP_T = 8, 9, 10, 11, 12
FLAG_M, TOP_M = 13, 14


def dot(left, right):
    return jnp.dot(left, right, preferred_element_type=f32)


def dot_nt(left, right):
    return lax.dot_general(left, right, (((1,), (1,)), ((), ())), preferred_element_type=f32)


def dot_tn(left, right):
    return lax.dot_general(left, right, (((0,), (0,)), ((), ())), preferred_element_type=f32)


def norm(x, gain):
    return x * lax.rsqrt(jnp.mean(x * x, axis=-1, keepdims=True) + EPS) * gain


def norm_back(x, gain, grad):
    rate = lax.rsqrt(jnp.mean(x * x, axis=-1, keepdims=True) + EPS)
    scaled = x * rate
    inner = grad * gain
    grad_x = rate * (inner - scaled * jnp.mean(inner * scaled, axis=-1, keepdims=True))
    return grad_x, jnp.sum(grad * scaled, axis=0, keepdims=True)


GELU_A = 0.7978845608028654
GELU_B = 0.044715


def gelu_both(z):
    square = z * z
    bend = jnp.tanh(z * (GELU_A + GELU_A * GELU_B * square))
    half = 0.5 * bend + 0.5
    value = z * half
    return value, half + value * (1.0 - bend) * (GELU_A + 3.0 * GELU_A * GELU_B * square)


def windows(meta, length):
    wide = length * 5 // 8
    slim = length - wide
    core = meta[0, CORE]
    return (
        pl.ds(pl.multiple_of(core * slim, BLOCK), wide),
        pl.ds(pl.multiple_of((1 - core) * wide, BLOCK), slim),
    )


def over(meta, flag, length, work):
    main, other = windows(meta, length)
    work(main, True)

    @pl.when(meta[0, flag] == 1)
    def _():
        work(other, False)


class Moves:
    def __init__(self, meta, length, semaphores):
        self.meta, self.semaphores, self.used, self.leaving = meta, semaphores, 0, []
        self.rows = windows(meta, length)

    def copy(self, src, dst):
        self.used += 1
        return pltpu.make_async_copy(src, dst, self.semaphores.at[self.used - 1])

    def whole(self, src, dst):
        copy = self.copy(src, dst)
        copy.start()
        return copy.wait

    def pair(self, src, dst, flag):
        first, second = (self.copy(src.at[rows], dst.at[rows]) for rows in self.rows)
        first.start()
        pl.when(self.meta[0, flag] == 1)(second.start)

        def wait():
            first.wait()
            pl.when(self.meta[0, flag] == 1)(second.wait)

        return wait

    def away(self, src, dst, flag=None):
        self.leaving.append(self.whole(src, dst) if flag is None else self.pair(src, dst, flag))

    def finish(self):
        for wait in self.leaving:
            wait()


def block(i):
    return pl.ds(pl.multiple_of(i * BLOCK, BLOCK), BLOCK)


def lanes_of(at, p):
    return slice(at + p * BLOCK, at + (p + 1) * BLOCK)


def two_heads(tile, lane):
    zero = jnp.zeros_like(tile)
    return jnp.concatenate([jnp.where(lane < 64, tile, zero), jnp.where(lane < 64, zero, tile)], axis=0)


def both_blocks(tile):
    return jnp.concatenate([tile[:64, :BLOCK], tile[64:, BLOCK:]], axis=0)


def key_window(meta, kind, top, i, n, low, high):
    wanted = meta[i, kind] + n * KEYS
    start = pl.multiple_of(jnp.minimum(wanted, meta[0, top]), STEP)
    place = lax.broadcasted_iota(i32, (KEYS, BLOCK), 0) + start
    bias = jnp.where((place >= jnp.maximum(low, wanted)) & (place < high), 0.0, NEG)
    return pl.ds(start, KEYS), jnp.concatenate([bias, bias], axis=1)


def two_rows(rows_ref, p, rows):
    return jnp.concatenate([rows_ref[2 * p : 2 * p + 1, rows], rows_ref[2 * p + 1 : 2 * p + 2, rows]], axis=1)


def attend(meta, kind, top, info, info_row, q, k, v, o, lse, both_q, peaks, totals, sums):
    (q, q_at), (k, k_at), (v, v_at) = q, k, v
    pairs = o.shape[1] // BLOCK

    def one_block(i, _):
        count = (meta[i, kind + 1] - meta[i, kind] + KEYS - 1) // KEYS

        @pl.when(count > 0)
        def _():
            rows = block(i)
            lane = lax.broadcasted_iota(i32, (BLOCK, BLOCK), 1)
            low, high = info[info_row : info_row + 1, rows], info[info_row + 1 : info_row + 2, rows]
            peaks[...] = jnp.full(peaks.shape, -jnp.inf, f32)
            totals[...] = jnp.zeros(totals.shape, f32)
            sums[...] = jnp.zeros(sums.shape, f32)
            for p in range(pairs):
                both_q[p] = two_heads(q[rows, lanes_of(q_at, p)], lane)

            def one_window(n, _):
                keys, bias = key_window(meta, kind, top, i, n, low, high)
                scores = [dot_nt(k[keys, lanes_of(k_at, p)], both_q[p]) for p in range(pairs)]
                weights, fades = [], []
                for p in range(pairs):
                    tile = scores[p] + bias
                    before = peaks[p : p + 1, :]
                    peak = jnp.maximum(before, jnp.max(tile, axis=0, keepdims=True))
                    fade = jnp.exp(before - peak)
                    weight = jnp.exp(tile - peak)
                    peaks[p : p + 1, :] = peak
                    totals[p : p + 1, :] = totals[p : p + 1, :] * fade + jnp.sum(weight, axis=0, keepdims=True)
                    weights.append(weight.astype(bf16))
                    fades.append(fade)
                mixes = [dot_tn(v[keys, lanes_of(v_at, p)], weights[p]) for p in range(pairs)]
                for p in range(pairs):
                    fade = fades[p]
                    faded = jnp.concatenate(
                        [jnp.broadcast_to(fade[:, :BLOCK], (64, BLOCK)), jnp.broadcast_to(fade[:, BLOCK:], (64, BLOCK))]
                    )
                    sums[p] = sums[p] * faded + both_blocks(mixes[p])
                return 0

            lax.fori_loop(0, count, one_window, 0)
            for p in range(pairs):
                total = totals[p : p + 1, :]
                share = 1.0 / total
                shares = jnp.concatenate(
                    [jnp.broadcast_to(share[:, :BLOCK], (64, BLOCK)), jnp.broadcast_to(share[:, BLOCK:], (64, BLOCK))]
                )
                o[rows, lanes_of(0, p)] = (sums[p] * shares).T.astype(bf16)
                log_total = peaks[p : p + 1, :] + jnp.log(total)
                lse[2 * p : 2 * p + 1, rows] = log_total[:, :BLOCK]
                lse[2 * p + 1 : 2 * p + 2, rows] = log_total[:, BLOCK:]

        return 0

    lax.fori_loop(meta[0, FIRST], meta[0, LAST], one_block, 0)


def attend_back(meta, kind, top, info, info_row, q, k, v, lse, delta, do, dq, dk, dv, both_q, both_o, sums):
    (q, q_at), (k, k_at), (v, v_at), (dq, dq_at) = q, k, v, dq
    pairs = do.shape[1] // BLOCK

    def one_block(i, _):
        count = (meta[i, kind + 1] - meta[i, kind] + KEYS - 1) // KEYS

        @pl.when(count > 0)
        def _():
            rows = block(i)
            lane = lax.broadcasted_iota(i32, (BLOCK, BLOCK), 1)
            low, high = info[info_row : info_row + 1, rows], info[info_row + 1 : info_row + 2, rows]
            sums[...] = jnp.zeros(sums.shape, f32)
            for p in range(pairs):
                both_q[p] = two_heads(q[rows, lanes_of(q_at, p)], lane)
                both_o[p] = two_heads(do[rows, lanes_of(0, p)], lane)

            def one_window(n, _):
                keys, bias = key_window(meta, kind, top, i, n, low, high)
                these = [k[keys, lanes_of(k_at, p)] for p in range(pairs)]
                scores = [dot_nt(these[p], both_q[p]) for p in range(pairs)]
                grad_probs = [dot_nt(v[keys, lanes_of(v_at, p)], both_o[p]) for p in range(pairs)]
                probs = [jnp.exp(scores[p] + bias - two_rows(lse, p, rows)) for p in range(pairs)]
                grad_scores = [
                    (probs[p] * (grad_probs[p] - two_rows(delta, p, rows))).astype(bf16) for p in range(pairs)
                ]
                grads_v = [dot(probs[p].astype(bf16), both_o[p]) for p in range(pairs)]
                grads_k = [dot(grad_scores[p], both_q[p]) for p in range(pairs)]
                grads_q = [dot_tn(these[p], grad_scores[p]) for p in range(pairs)]
                for p in range(pairs):
                    dv[keys, lanes_of(0, p)] += grads_v[p]
                    dk[keys, lanes_of(0, p)] += grads_k[p]
                    sums[p] += both_blocks(grads_q[p])
                return 0

            lax.fori_loop(0, count, one_window, 0)
            for p in range(pairs):
                dq[rows, lanes_of(dq_at, p)] = (sums[p] * 0.125).T.astype(bf16)

        return 0

    lax.fori_loop(meta[0, FIRST], meta[0, LAST], one_block, 0)


def attention_forward_kernel(
    layer, meta, bank, x_in, mem_in, gain, go_rows, info,
    qkv_out, o1_out, l1, mid_out, q2_out, kv_out, o2_out, l2, final,
    x, mem, qkv, o1, mid, q2, kv, o2, out, wide, third, fourth, pairw, last, both_q, peaks, totals, sums, semaphores,
):
    length, width = x.shape
    kind, flag_m, top_m = 4 * layer, FLAG_M + 2 * layer, TOP_M + 2 * layer
    moves = Moves(meta, length, semaphores)
    section = 2 * layer
    x_here = moves.pair(x_in, x, FLAG_T)
    self_here = [moves.whole(bank.at[section, j], wide.at[:, j * width : (j + 1) * width]) for j in range(3)]
    mem_here = moves.pair(mem_in, mem, flag_m)
    pair_here = [moves.whole(bank.at[section, 5 + j], pairw.at[:, j * width : (j + 1) * width]) for j in range(2)]
    rest_here = [moves.whole(bank.at[section, j], place) for j, place in ((3, third), (4, fourth), (7, last))]
    go = (lambda rows: go_rows[rows, layer : layer + 1])
    x_here()
    for wait in self_here:
        wait()

    def self_in(rows, _):
        a = norm(x[rows, :].astype(f32), gain[section, 0:1]).astype(bf16)
        both = dot(a, wide[...])
        qkv[rows, :width] = (both[:, :width] * 0.125).astype(bf16)
        qkv[rows, width:] = both[:, width:].astype(bf16)
        o1[rows, :] = jnp.zeros((rows.size, width), bf16)
        o2[rows, :] = jnp.zeros((rows.size, width), bf16)

    over(meta, FLAG_T, length, self_in)
    moves.away(qkv, qkv_out, FLAG_T)
    mem_here()
    for wait in pair_here:
        wait()

    def memory_in(rows, _):
        kv[rows, :] = dot(mem[rows, :], pairw[...]).astype(bf16)

    over(meta, flag_m, length, memory_in)
    moves.away(kv, kv_out, flag_m)
    l1[...] = jnp.zeros(l1.shape, f32)
    l2[...] = jnp.zeros(l2.shape, f32)
    attend(
        meta, SELF + kind, TOP_T, info, 0, (qkv, 0), (qkv, width), (qkv, 2 * width), o1, l1,
        both_q, peaks, totals, sums,
    )
    moves.away(o1, o1_out, FLAG_T)
    for wait in rest_here:
        wait()

    def cross_in(rows, _):
        state = x[rows, :].astype(f32) + go(rows) * dot(o1[rows, :], third[...])
        mid[rows, :] = state
        a = norm(state, gain[section, 1:2]).astype(bf16)
        q2[rows, :] = (dot(a, fourth[...]) * 0.125).astype(bf16)

    over(meta, FLAG_T, length, cross_in)
    moves.away(mid, mid_out, FLAG_T)
    moves.away(q2, q2_out, FLAG_T)
    attend(
        meta, CROSS + kind, top_m, info, 2, (q2, 0), (kv, 0), (kv, width), o2, l2, both_q, peaks, totals, sums
    )
    moves.away(o2, o2_out, FLAG_T)

    def finish(rows, _):
        out[rows, :] = (mid[rows, :] + go(rows) * dot(o2[rows, :], last[...])).astype(bf16)

    over(meta, FLAG_T, length, finish)
    moves.away(out, final, FLAG_T)
    moves.finish()


def attention_backward_kernel(
    layer, meta, bank, x_in, mem_in, gain, go_rows, info,
    qkv_in, o1_in, l1, mid_in, q2_in, kv_in, o2_in, l2, dh_in, *rest,
):
    entry = layer == 0
    if entry:
        dmem_in, *rest = rest
    (
        dx_out, dmem_out, dw_out, dgain,
        x, mem, qkv, o1, mid, q2, kv, o2, dh, dx, dmem, dw,
        wide, third, fourth, pairw, last,
        dstate, do, dqkv, dk, dv, delta, heads, both_q, both_o, sums, acc, semaphores,
    ) = rest
    length, width = x.shape
    kind, flag_m, top_m = 4 * layer, FLAG_M + 2 * layer, TOP_M + 2 * layer
    moves = Moves(meta, length, semaphores)
    section = 2 * layer
    first_here = [
        moves.pair(dh_in, dh, FLAG_T), moves.whole(bank.at[section, 7], last), moves.pair(o2_in, o2, FLAG_T),
        moves.pair(q2_in, q2, FLAG_T), moves.pair(kv_in, kv, flag_m),
    ]
    if entry:
        first_here.append(moves.whole(dmem_in, dmem))
    second_here = [moves.pair(mem_in, mem, flag_m), moves.pair(mid_in, mid, FLAG_T)]
    second_here += [moves.whole(bank.at[section, 5 + j], pairw.at[:, j * width : (j + 1) * width]) for j in range(2)]
    second_here += [moves.whole(bank.at[section, 4], fourth)]
    third_here = [moves.whole(bank.at[section, 3], third), moves.pair(o1_in, o1, FLAG_T), moves.pair(qkv_in, qkv, FLAG_T)]
    fourth_here = [moves.whole(bank.at[section, j], wide.at[:, j * width : (j + 1) * width]) for j in range(3)]
    fourth_here += [moves.pair(x_in, x, FLAG_T)]
    go = (lambda rows: go_rows[rows, layer : layer + 1])

    row_of = lax.broadcasted_iota(i32, (HEADS, width), 0)
    lane_of = lax.broadcasted_iota(i32, (HEADS, width), 1)
    heads[...] = (lane_of // (width // HEADS) == row_of).astype(bf16)
    dk[...] = jnp.zeros(dk.shape, f32)
    dv[...] = jnp.zeros(dv.shape, f32)
    delta[...] = jnp.zeros(delta.shape, f32)
    if not entry:
        dmem[...] = jnp.zeros(dmem.shape, bf16)
    if entry:
        dx[...] = jnp.zeros(dx.shape, bf16)

    def weight_grad(targets, flag, left, right):
        size = len(targets) * width

        def part(rows, fresh):
            term = dot_tn(left(rows), right(rows))
            acc[:, :size] = term if fresh else acc[:, :size] + term

        over(meta, flag, length, part)
        for n, j in enumerate(targets):
            dw[j] = acc[:, n * width : (n + 1) * width].astype(bf16)
            moves.away(dw.at[j], dw_out.at[j])

    def begin(grad_of, o, out_weight, target):
        def dy(rows):
            return (go(rows) * grad_of(rows)).astype(bf16)

        def part(rows, _):
            grad = dot_nt(dy(rows), out_weight[...]).astype(bf16)
            do[rows, :] = grad
            product = grad.astype(f32) * o[rows, :].astype(f32)
            high = product.astype(bf16)
            rest = (product - high.astype(f32)).astype(bf16)
            delta[:, rows] = dot_nt(heads[...], high) + dot_nt(heads[...], rest)
            dqkv[rows, :width] = jnp.zeros((rows.size, width), bf16)

        over(meta, FLAG_T, length, part)
        weight_grad([target], FLAG_T, lambda rows: o[rows, :], dy)

    def top_grad(rows):
        return dh[rows, :].astype(f32)

    for wait in first_here:
        wait()
    begin(top_grad, o2, last, 7)
    attend_back(
        meta, CROSS + kind, top_m, info, 2, (q2, 0), (kv, 0), (kv, width), l2, delta, do, (dqkv, 0), dk, dv,
        both_q, both_o, sums,
    )
    for wait in second_here:
        wait()

    def memory_out(rows, _):
        dqkv[rows, width : 2 * width] = dk[rows, :].astype(bf16)
        dqkv[rows, 2 * width :] = dv[rows, :].astype(bf16)
        term = dot_nt(dqkv[rows, width:], pairw[...])
        dmem[rows, :] = (dmem[rows, :].astype(f32) + term).astype(bf16)

    over(meta, flag_m, length, memory_out)
    moves.away(dmem, dmem_out)
    weight_grad([5, 6], flag_m, lambda rows: mem[rows, :], lambda rows: dqkv[rows, width:])

    def cross_out(rows, fresh):
        grad_x, grad_gain = norm_back(mid[rows, :], gain[section, 1:2], dot_nt(dqkv[rows, :width], fourth[...]))
        dstate[rows, :] = top_grad(rows) + grad_x
        dgain[1:2, :] = grad_gain if fresh else dgain[1:2, :] + grad_gain

    over(meta, FLAG_T, length, cross_out)
    weight_grad(
        [4], FLAG_T, lambda rows: norm(mid[rows, :], gain[section, 1:2]).astype(bf16), lambda rows: dqkv[rows, :width]
    )
    for wait in third_here:
        wait()
    dk[...] = jnp.zeros(dk.shape, f32)
    dv[...] = jnp.zeros(dv.shape, f32)
    begin(lambda rows: dstate[rows, :], o1, third, 3)
    attend_back(
        meta, SELF + kind, TOP_T, info, 0, (qkv, 0), (qkv, width), (qkv, 2 * width), l1, delta, do, (dqkv, 0), dk, dv,
        both_q, both_o, sums,
    )
    for wait in fourth_here:
        wait()

    def self_out(rows, fresh):
        dqkv[rows, width : 2 * width] = dk[rows, :].astype(bf16)
        dqkv[rows, 2 * width :] = dv[rows, :].astype(bf16)
        grad_x, grad_gain = norm_back(x[rows, :].astype(f32), gain[section, 0:1], dot_nt(dqkv[rows, :], wide[...]))
        value = dstate[rows, :] + grad_x
        if entry:
            value = jnp.where(go_rows[rows, 2:3] > 0.0, value, 0.0)
        dx[rows, :] = value.astype(bf16)
        dgain[0:1, :] = grad_gain if fresh else dgain[0:1, :] + grad_gain

    over(meta, FLAG_T, length, self_out)
    if entry:
        moves.away(dx, dx_out)
    else:
        moves.away(dx, dx_out, FLAG_T)
    weight_grad(
        [0, 1, 2], FLAG_T, lambda rows: norm(x[rows, :].astype(f32), gain[section, 0:1]).astype(bf16),
        lambda rows: dqkv[rows, :],
    )
    moves.finish()


def exit_part(layer, vector, cols, rows, last, score_at, exit_grad, fresh, sentences):
    factor = layer.shape[1] ** (-0.5)
    score = jax.nn.sigmoid(jnp.sum(layer * vector, axis=-1, keepdims=True) * factor)
    score_at[rows, :] = jnp.broadcast_to(score, (rows.size, score_at.shape[1]))
    target = cols[rows, 0:1] if last else cols[rows, 4:5]
    weight = cols[rows, 3:4] * (score - target) * (factor / sentences)
    term = jnp.sum(weight * layer, axis=0, keepdims=True)
    exit_grad[...] = term if fresh else exit_grad[...] + term


def dense_weights(moves, bank, section, up, down, width):
    parts = up.shape[1] // width
    here = [moves.whole(bank.at[section, j], up.at[:, j * width : (j + 1) * width]) for j in range(parts)]
    later = [moves.whole(bank.at[section, parts + j], down.at[j * width : (j + 1) * width]) for j in range(parts)]
    return here, later


def halves(up):
    hidden = up.shape[1]
    return [slice(i * hidden // 2, (i + 1) * hidden // 2) for i in range(2)]


def dense_forward_kernel(
    sentences, meta, bank, x_in, gain, cols, final, active_out, slope_out, scores, exit_grad,
    x, out, active, slope, up, down, semaphores
):
    section = 1
    length, width = x.shape
    moves = Moves(meta, length, semaphores)
    x_here = moves.pair(x_in, x, FLAG_T)
    here, later = dense_weights(moves, bank, section, up, down, width)
    x_here()

    def part(rows, fresh):
        state = x[rows, :].astype(f32)
        a = norm(state, gain[section, 0:1]).astype(bf16)
        if fresh:
            for wait in here:
                wait()
        hidden = [dot(a, up[:, lanes]) for lanes in halves(up)]
        for lanes, z in zip(halves(up), hidden):
            value, gradient = gelu_both(z)
            active[rows, lanes] = value.astype(bf16)
            slope[rows, lanes] = gradient.astype(bf16)
        if fresh:
            for wait in later:
                wait()
        layer = state + dot(active[rows, :], down[...])
        out[rows, :] = layer.astype(bf16)
        exit_part(layer, gain[section, 1:2], cols, rows, False, scores, exit_grad, fresh, sentences)

    over(meta, FLAG_T, length, part)
    moves.away(out, final, FLAG_T)
    moves.away(active, active_out, FLAG_T)
    moves.away(slope, slope_out, FLAG_T)
    moves.finish()


def dense_gradients(moves, dw, dw_out, grad_up, grad_down, width):
    parts = grad_up.shape[1] // width
    for j in range(parts):
        dw[parts + j] = grad_down[j * width : (j + 1) * width, :].astype(bf16)
        moves.away(dw.at[parts + j], dw_out.at[parts + j])
        dw[j] = grad_up[:, j * width : (j + 1) * width].astype(bf16)
        moves.away(dw.at[j], dw_out.at[j])


def accumulate(target, fresh, lanes, value):
    target[lanes] = value if fresh else target[lanes] + value


def dense_last_kernel(
    sentences, meta, bank, x_in, gain, cols, dh_in, before, dx_out, dw_out, dgain, states, halt,
    x, dh, scores, exit_grad, out, dx, dw, active, dhidden, up, down, grad_up, grad_down, semaphores
):
    section = 3
    length, width = x.shape
    moves = Moves(meta, length, semaphores)
    x_here, dh_here = moves.pair(x_in, x, FLAG_T), moves.pair(dh_in, dh, FLAG_T)
    here, later = dense_weights(moves, bank, section, up, down, width)
    out[...] = jnp.zeros(out.shape, bf16)
    scores[...] = jnp.zeros(scores.shape, f32)
    x_here()
    dh_here()

    def part(rows, fresh):
        go, own = cols[rows, 1:2], cols[rows, 2:3] > 0.0
        grad_out = jnp.where(own, dh[rows, :].astype(f32), 0.0)
        state = x[rows, :].astype(f32)
        a = norm(state, gain[section, 0:1]).astype(bf16)
        dy = (go * grad_out).astype(bf16)
        if fresh:
            for wait in here + later:
                wait()
        here_rows = slice(0, rows.size)
        hidden = [dot(a, up[:, lanes]) for lanes in halves(up)]
        for lanes, z in zip(halves(up), hidden):
            grad = dot_nt(dy, down[lanes])
            value, gradient = gelu_both(z)
            active[here_rows, lanes] = value.astype(bf16)
            dhidden[here_rows, lanes] = (gradient * grad).astype(bf16)
        layer = state + go * dot(active[here_rows, :], down[...])
        out[rows, :] = jnp.where(own, layer, 0.0).astype(bf16)
        exit_part(layer, gain[section, 1:2], cols, rows, True, scores, exit_grad, fresh, sentences)
        grad_x, grad_gain = norm_back(state, gain[section, 0:1], dot_nt(dhidden[here_rows, :], up[...]))
        dx[rows, :] = (grad_out + grad_x).astype(bf16)
        dgain[0:1, :] = grad_gain if fresh else dgain[0:1, :] + grad_gain
        accumulate(grad_down, fresh, slice(None), dot_tn(active[here_rows, :], dy))
        accumulate(grad_up, fresh, slice(None), dot_tn(a, dhidden[here_rows, :]))

    over(meta, FLAG_T, length, part)
    moves.away(dx, dx_out, FLAG_T)
    moves.away(out, states)
    dgain[1:2, :] = exit_grad[...]
    lane = lax.broadcasted_iota(i32, (BLOCK, 8), 1)
    for i in range(length // BLOCK):
        rows = slice(i * BLOCK, (i + 1) * BLOCK)
        both = jnp.where(lane == 0, before[rows, :], scores[rows, :])
        halt[:, rows] = jnp.where(cols[rows, 2:3] > 0.0, both, 0.0).T
    dense_gradients(moves, dw, dw_out, grad_up, grad_down, width)
    moves.finish()


def dense_backward_kernel(
    meta, bank, x_in, gain, cols, dh_in, active_in, slope_in, exit_grad, dx_out, dw_out, dgain,
    x, dh, dx, dw, active, slope, dhidden, up, down, grad_up, grad_down, semaphores
):
    section = 1
    length, width = x.shape
    moves = Moves(meta, length, semaphores)
    dh_here = moves.pair(dh_in, dh, FLAG_T)
    later, here = dense_weights(moves, bank, section, up, down, width)
    here.append(moves.pair(slope_in, slope, FLAG_T))
    here += [moves.pair(active_in, active, FLAG_T), moves.pair(x_in, x, FLAG_T)]
    dgain[1:2, :] = exit_grad[...]
    for wait in [dh_here] + here + later:
        wait()

    def part(rows, fresh):
        dy = dh[rows, :]
        grads = [dot_nt(dy, down[lanes]) for lanes in halves(up)]
        for lanes, grad in zip(halves(up), grads):
            dhidden[rows, lanes] = (slope[rows, lanes].astype(f32) * grad).astype(bf16)
        state = x[rows, :].astype(f32)
        a = norm(state, gain[section, 0:1]).astype(bf16)
        grad_x, grad_gain = norm_back(state, gain[section, 0:1], dot_nt(dhidden[rows, :], up[...]))
        dx[rows, :] = (dy.astype(f32) + grad_x).astype(bf16)
        dgain[0:1, :] = grad_gain if fresh else dgain[0:1, :] + grad_gain
        accumulate(grad_down, fresh, slice(None), dot_tn(active[rows, :], dy))
        accumulate(grad_up, fresh, slice(None), dot_tn(a, dhidden[rows, :]))

    over(meta, FLAG_T, length, part)
    moves.away(dx, dx_out, FLAG_T)
    dense_gradients(moves, dw, dw_out, grad_up, grad_down, width)
    moves.finish()


def widen_kernel(bank, dx, dmem, halt, bank_out, dx_out, dmem_out, halt_out):
    bank_out[...] = bank[...].astype(f32)
    dx_out[...] = dx[...].astype(f32)
    dmem_out[...] = dmem[...].astype(f32)
    halt_out[...] = halt[:, : halt_out.shape[1], :]


def widen(bank, dx, dmem, halt):
    steps = 8
    span, width = bank.shape
    micro, length, shares = dx.shape

    def some(shape, *place):
        return pl.BlockSpec(shape, lambda i: tuple(i if p else 0 for p in place))

    rows = some((micro, length // steps, shares), 0, 1, 0)
    whole = some((span // steps, width), 1, 0)
    halting = (micro, 2, halt.shape[2])
    return pl.pallas_call(
        widen_kernel,
        grid=(steps,),
        out_shape=[jax.ShapeDtypeStruct(t.shape, f32) for t in (bank, dx, dmem)]
        + [jax.ShapeDtypeStruct(halting, f32)],
        in_specs=[whole, rows, rows, some(halt.shape, 0, 0, 0)],
        out_specs=[whole, rows, rows, some(halting, 0, 0, 0)],
        compiler_params=pltpu.CompilerParams(vmem_limit_bytes=60 * 2**20),
        name="widen",
    )(bank, dx, dmem, halt)


def plan_kernel(sentences, row, core, seg, pad, mseg, mmask, depths, meta, info, cols):
    row, core = row[0], core[0]
    length, slots = seg.shape[2], mseg.shape[2]
    blocks = length // BLOCK
    micro = seg.shape[1]

    def pick(table):
        return table[row // micro, pl.ds(row % micro, 1), :]

    seg, pad, mseg, mmask, depths = (pick(t) for t in (seg, pad, mseg, mmask, depths))
    number = lax.broadcasted_iota(i32, (sentences, length), 0)
    place = lax.broadcasted_iota(i32, (1, length), 1)

    def count(marks):
        return jnp.sum(marks.astype(f32), axis=1, keepdims=True).astype(i32)

    square = lax.broadcasted_iota(i32, (sentences, sentences), 0) == lax.broadcasted_iota(
        i32, (sentences, sentences), 1
    )
    depth_row = jnp.broadcast_to(depths, (sentences, sentences))
    depth_table = jnp.sum(jnp.where(square, depth_row, 0).astype(f32), axis=1, keepdims=True).astype(i32)
    mine = seg == number
    starts = count(seg < number)
    filled = count(pad == 1)
    memory_number = lax.broadcasted_iota(i32, (sentences, slots), 0)
    memory_starts = count(mseg < memory_number)
    memory_stops = jnp.minimum(count(mseg <= memory_number), count(mmask == 1))

    def of_token(table):
        return jnp.sum(jnp.where(mine, table, 0), axis=0, keepdims=True)

    low = of_token(starts)
    high = jnp.where(pad == 1, jnp.minimum(place, filled - 1), place) + 1
    cross_low = jnp.where(pad == 0, 0, of_token(memory_starts))
    cross_high = jnp.where(pad == 0, slots, of_token(memory_stops))
    depth = of_token(depth_table)
    keep = depth == 2

    def by_block(values):
        return jnp.concatenate([values[:, i * BLOCK : (i + 1) * BLOCK] for i in range(blocks)], axis=0)

    def spans(used, lows, highs):
        lows = jnp.min(by_block(jnp.where(used, lows, slots)), axis=1, keepdims=True)
        highs = jnp.max(by_block(jnp.where(used, highs, 0)), axis=1, keepdims=True)
        return jnp.minimum(lows, highs) // STEP * STEP, highs

    work = jnp.zeros((blocks, 1), i32)
    for used in (place >= 0, keep):
        for lows, highs in ((low, high), (cross_low, cross_high)):
            from_, to = spans(used, lows, highs)
            work = work + 2 * ((to - from_ + KEYS - 1) // KEYS) + jnp.where(to > from_, 1, 0)
    start = jnp.sum(jnp.where(square, starts, 0), axis=0, keepdims=True)
    block_at = lax.broadcasted_iota(i32, (blocks, sentences), 0) * BLOCK
    before = jnp.sum(jnp.where(block_at < start, work, 0), axis=0, keepdims=True)
    after = jnp.sum(jnp.where(block_at + BLOCK > start, work, 0), axis=0, keepdims=True)
    after = after + jnp.where(filled < length, 5, 0)
    off = jnp.abs(start - length // 2)
    score = jnp.maximum(before, after) * length + off
    score = score + jnp.where(off > length // 8, length * length, 0)
    score = jnp.where(lax.broadcasted_iota(i32, (1, sentences), 1) > 0, score, 2 * length * length)
    best = jnp.min(score, axis=1, keepdims=True)
    cut = jnp.min(jnp.where(score == best, start, length), axis=1, keepdims=True)

    def by_core(first, second):
        return first * (1 - core) + second * core

    below = jnp.where(place < cut, 1, 0)
    owned = by_core(below, 1 - below) == 1
    begin = by_core(0, cut // BLOCK)
    end = by_core((cut + BLOCK - 1) // BLOCK, blocks)
    wide = length * 5 // 8
    base = by_core(0, length - wide)

    def outside(from_place, to_place):
        return by_core(jnp.where(to_place > wide, 1, 0), jnp.where(from_place < length - wide, 1, 0))

    def top_of(flag):
        return jnp.where(flag == 1, length - KEYS, base + wide - KEYS)

    lane = lax.broadcasted_iota(i32, (blocks, 128), 1)
    table = jnp.zeros((blocks, 128), i32)
    flag_t = outside(begin * BLOCK, end * BLOCK)
    entries = {CORE: jnp.full((1, 1), core, i32), FLAG_T: flag_t, FIRST: begin, LAST: end, TOP_T: top_of(flag_t)}
    for layer in range(2):
        used = owned if layer == 0 else owned & keep
        for kind, lows, highs in ((SELF, low, high), (CROSS, cross_low, cross_high)):
            entries[kind + 4 * layer], entries[kind + 4 * layer + 1] = spans(used, lows, highs)
        flag_m = outside(
            jnp.min(jnp.where(used, cross_low, slots), axis=1, keepdims=True),
            jnp.max(jnp.where(used, cross_high, 0), axis=1, keepdims=True),
        )
        entries[FLAG_M + 2 * layer] = flag_m
        entries[TOP_M + 2 * layer] = top_of(flag_m)
    for column, values in entries.items():
        table = jnp.where(lane == column, values, table)
    meta[...] = table
    info[...] = jnp.concatenate([low, high, cross_low, cross_high, low, low, low, low], axis=0)
    ones = jnp.ones((1, length), f32)
    kept, own = keep.astype(f32), owned.astype(f32)
    counted = jnp.where(pad == 1, own, 0.0)
    by_row = jnp.concatenate([ones, kept, own, counted, (depth == 1).astype(f32), own, own, own], axis=0)
    for i in range(blocks):
        cols[i * BLOCK : (i + 1) * BLOCK, :] = by_row[:, i * BLOCK : (i + 1) * BLOCK].T


ANY = pl.BlockSpec(memory_space=pltpu.HBM)
VMEM = pl.BlockSpec(memory_space=pltpu.VMEM)
SMEM = pl.BlockSpec(memory_space=pltpu.SMEM)


def make_plan(row, core, ints):
    seg, pad, mseg, mmask, depths = ints
    length, sentences = seg.shape[-1], depths.shape[-1]
    outs = [((length // BLOCK, 128), i32), ((8, length), i32), ((length, 8), f32)]
    return pl.pallas_call(
        functools.partial(plan_kernel, sentences),
        out_shape=[jax.ShapeDtypeStruct(*out) for out in outs],
        in_specs=[SMEM, SMEM] + [VMEM] * 5,
        out_specs=[VMEM] * 3,
        compiler_params=pltpu.CompilerParams(vmem_limit_bytes=60 * 2**20),
        name="make_plan",
    )(row.astype(i32)[None], core.astype(i32)[None], seg, pad, mseg, mmask, depths)


def run(kernel, ins, outs, scratch, semaphores, name, flops, *args):
    return pl.pallas_call(
        kernel,
        out_shape=[jax.ShapeDtypeStruct(shape, dtype) for _, shape, dtype in outs],
        in_specs=ins,
        out_specs=[spec for spec, _, _ in outs],
        scratch_shapes=[pltpu.VMEM(shape, dtype) for shape, dtype in scratch]
        + [pltpu.SemaphoreType.DMA((semaphores,))],
        compiler_params=pltpu.CompilerParams(vmem_limit_bytes=60 * 2**20),
        cost_estimate=pl.CostEstimate(flops=flops, bytes_accessed=20 * 2**20, transcendentals=0),
        name=name,
    )(*args)


def attention_forward(layer, plan, bank, x, mem, gain, name):
    meta, info, cols = plan
    length, width = x.shape
    pairs = width // BLOCK

    def rows(n, dtype=bf16):
        return ((length, n * width), dtype)

    logs = (VMEM, (HEADS, length), f32)
    kept = [rows(3), rows(1), logs[1:], rows(1, f32), rows(1), rows(2), rows(1), logs[1:], rows(1)]
    outs = [(VMEM if shape[0] == HEADS else ANY, shape, dtype) for shape, dtype in kept]
    square = ((width, width), bf16)
    scratch = [
        rows(1), rows(1), rows(3), rows(1), rows(1, f32), rows(1), rows(2), rows(1), rows(1),
        ((width, 3 * width), bf16), square, square, ((width, 2 * width), bf16), square,
        ((pairs, 2 * BLOCK, BLOCK), bf16), ((8, 2 * BLOCK), f32), ((8, 2 * BLOCK), f32), ((pairs, BLOCK, BLOCK), f32),
    ]
    return run(
        functools.partial(attention_forward_kernel, layer), [SMEM, ANY, ANY, ANY, VMEM, VMEM, VMEM], outs, scratch, 32,
        name, 6 * 10**9, meta, bank, x, mem, gain, cols, info,
    )


def attention_backward(layer, plan, bank, x, mem, gain, saved, dh, dmem, name):
    meta, info, cols = plan
    length, width = x.shape
    pairs = width // BLOCK

    def rows(n, dtype=bf16):
        return ((length, n * width), dtype)

    square, matrices = ((width, width), bf16), (bank.shape[1:], bf16)
    outs = [(ANY, *rows(1)), (ANY, *rows(1)), (ANY, *matrices), (VMEM, (2, width), f32)]
    both = ((pairs, 2 * BLOCK, BLOCK), bf16)
    scratch = [
        rows(1), rows(1), rows(3), rows(1), rows(1, f32), rows(1), rows(2), rows(1), rows(1), rows(1), rows(1), matrices,
        ((width, 3 * width), bf16), square, square, ((width, 2 * width), bf16), square,
        rows(1, f32), rows(1), rows(3), rows(1, f32), rows(1, f32), ((HEADS, length), f32), ((HEADS, width), bf16),
        both, both, ((pairs, BLOCK, BLOCK), f32), ((width, 3 * width), f32),
    ]
    ins = [SMEM, ANY, ANY, ANY, VMEM, VMEM, VMEM, ANY, ANY, VMEM, ANY, ANY, ANY, ANY, VMEM, ANY] + [ANY] * len(dmem)
    return run(
        functools.partial(attention_backward_kernel, layer), ins, outs, scratch, 48,
        name, 12 * 10**9, meta, bank, x, mem, gain, cols, info, *saved, dh, *dmem,
    )


def dense_shapes(bank, x):
    length, width = x.shape
    hidden = bank.shape[1] // 2 * width
    return ((length, width), bf16), ((length, hidden), bf16), ((width, hidden), bf16), ((hidden, width), bf16)


def dense_forward(plan, bank, x, gain, sentences, name):
    meta, _, cols = plan
    wide, inner, up, down = dense_shapes(bank, x)
    outs = [(ANY, *wide), (ANY, *inner), (ANY, *inner), (VMEM, cols.shape, f32), (VMEM, (1, x.shape[1]), f32)]
    return run(
        functools.partial(dense_forward_kernel, sentences), [SMEM, ANY, ANY, VMEM, VMEM], outs,
        [wide, wide, inner, inner, up, down], 24,
        name, 4 * 10**9, meta, bank, x, gain, cols,
    )


def dense_last(plan, bank, x, gain, dh, before, sentences, name):
    meta, _, cols = plan
    wide, inner, up, down = dense_shapes(bank, x)
    length, width = x.shape
    matrices = (bank.shape[1:], bf16)
    outs = [(ANY, *wide), (ANY, *matrices), (VMEM, (2, width), f32), (ANY, *wide), (VMEM, (8, length), f32)]
    inner = ((length * 5 // 8, inner[0][1]), bf16)
    scratch = [wide, wide, (cols.shape, f32), ((1, width), f32), wide, wide, matrices, inner, inner, up, down,
               (up[0], f32), (down[0], f32)]
    return run(
        functools.partial(dense_last_kernel, sentences), [SMEM, ANY, ANY, VMEM, VMEM, ANY, VMEM], outs, scratch, 32,
        name, 8 * 10**9, meta, bank, x, gain, cols, dh, before,
    )


def dense_backward(plan, bank, x, gain, dh, active, slope, exit_grad, name):
    meta, _, cols = plan
    wide, inner, up, down = dense_shapes(bank, x)
    matrices = (bank.shape[1:], bf16)
    outs = [(ANY, *wide), (ANY, *matrices), (VMEM, (2, x.shape[1]), f32)]
    scratch = [wide, wide, wide, matrices, inner, inner, inner, up, down, (up[0], f32), (down[0], f32)]
    return run(
        dense_backward_kernel, [SMEM, ANY, ANY, VMEM, VMEM, ANY, ANY, ANY, VMEM], outs, scratch, 32,
        name, 8 * 10**9, meta, bank, x, gain, cols, dh, active, slope, exit_grad,
    )


def row_forward_backward(row, core, x, mem, cotangent, bank, gains, ints):
    plan = make_plan(row, core, ints)
    sentences = ints[-1].shape[-1]
    *saved0, zero = attention_forward(0, plan, bank, x, mem, gains, "attend_zero")
    one, active, slope, scores, exit0 = dense_forward(plan, bank, zero, gains, sentences, "dense_one")
    *saved2, two = attention_forward(1, plan, bank, one, mem, gains, "attend_two")
    dtwo, dw3, dgain3, states, halt = dense_last(plan, bank, two, gains, cotangent, scores, sentences, "dense_three")
    done, dmem, dw2, dgain2 = attention_backward(1, plan, bank, one, mem, gains, saved2, dtwo, (), "attend_two_back")
    dzero, dw1, dgain1 = dense_backward(plan, bank, zero, gains, done, active, slope, exit0, "dense_one_back")
    dx, dmem, dw0, dgain0 = attention_backward(
        0, plan, bank, x, mem, gains, saved0, dzero, (dmem,), "attend_zero_back"
    )
    return states, halt, dx, dmem, [dw0, dw1, dw2, dw3], [dgain0, dgain1, dgain2, dgain3]


MESH = pl.DeviceIdType.MESH


def neighbours():
    s, d = lax.axis_index("section"), lax.axis_index("dp")
    across = [(s + 1 - 2 * (s % 2), d), ((s + 2) % 4, d), (3 - s, d)]
    layer = d // 2
    along = (s, d + 2 - 4 * (layer % 2))
    sibling = (s, d + 1 - 2 * (d % 2))
    return s, d, across, along, sibling


def greet(devices):
    barrier = pltpu.get_barrier_semaphore()
    for device in devices:
        pl.semaphore_signal(barrier, inc=1, device_id=device, device_id_type=MESH)
    pl.semaphore_wait(barrier, len(devices))


SUBS = 4


def gather_kernel(
    states, memory, cotangent, bank, gains, seg, pad, mseg, mmask, depths,
    x, mem, top, weights, gains_all, seg2, pad2, mseg2, mmask2, depths2,
    staging, send, recv, home,
):
    s, d, across, along, sibling = neighbours()
    core = d % 2
    parity = (d // 2) % 2
    greet(across + [along, sibling])
    started = []
    locals_ = []
    count = [0, 0]

    def push(src, dst, device):
        i = count[0]
        count[0] += 1
        copy = pltpu.make_async_remote_copy(src, dst, send.at[i], recv.at[i], device_id=device, device_id_type=MESH)
        return copy

    def go(src, dst, device):
        copy = push(src, dst, device)
        copy.start()
        started.append(copy)
        return copy

    def keep(src, dst):
        i = count[1]
        count[1] += 1
        copy = pltpu.make_async_copy(src, dst, home.at[i])
        return copy

    shares = states.shape[2]
    chips = [s] + [a[0] for a in across]
    sent_inputs, own_inputs = [], []
    for source, whole in ((states, x), (memory, mem), (cotangent, top)):
        for rel in range(4):
            target = chips[rel]
            mine = target // 2 == core
            dst = whole.at[:, pl.ds(pl.multiple_of(s * shares, shares), shares)]
            src = source.at[target % 2]
            if rel == 0:
                copy = keep(src, dst)
                own_inputs.append(copy)
            else:
                copy = push(src, dst, across[rel - 1])
                sent_inputs.append((copy, whole, rel))
            pl.when(mine)(copy.start)
    small = [go(source, whole.at[core], sibling)
             for source, whole in ((seg, seg2), (pad, pad2), (mseg, mseg2), (mmask, mmask2), (depths, depths2))]
    small += [go(gains, gains_all.at[s], device) for device in across]
    for source, whole in ((seg, seg2), (pad, pad2), (mseg, mseg2), (mmask, mmask2), (depths, depths2)):
        copy = keep(source, whole.at[core])
        copy.start()
        locals_.append(copy)
    copy = keep(gains, gains_all.at[s])
    copy.start()
    locals_.append(copy)

    span = bank.shape[0]
    half = span // 2
    third = half // 3 // (16 * SUBS) * (16 * SUBS)
    first = half - 2 * third
    sub0, sub1 = first // SUBS, third // SUBS

    def rows(section, part, i):
        at = section * span + core * half
        size = sub0 if part == 0 else sub1
        if part == 0:
            at = at + i * size
        elif part == 1:
            at = at + first + parity * third + i * size
        else:
            at = at + first + (1 - parity) * third + i * size
        return weights.at[pl.ds(pl.multiple_of(at, 16), size)]

    def own_rows(part, i):
        size = sub0 if part == 0 else sub1
        at = core * half + (i * size if part == 0 else first + parity * third + i * size)
        return bank.at[pl.ds(pl.multiple_of(at, 16), size)]

    direct = {}
    for part in (1, 0):
        for i in range(SUBS):
            for k in range(2):
                direct[k, part, i] = go(own_rows(part, i), rows(s, part, i), across[k])
    lift = keep(bank, staging)
    lift.start()
    drop = keep(staging, weights.at[pl.ds(pl.multiple_of(s * span, span), span)])

    holder = s // 2 == core
    handed = []
    for n, (source, whole) in enumerate(((states, x), (memory, mem), (cotangent, top))):
        for rel in range(4):
            lanes = whole.at[:, pl.ds(pl.multiple_of(chips[rel] * shares, shares), shares)]
            copy = push(lanes, lanes, sibling)
            handed.append(copy)
            arrived = own_inputs[n] if rel == 0 else sent_inputs[n * 3 + rel - 1][0]

            def hand(copy=copy, arrived=arrived, rel=rel):
                if rel == 0:
                    arrived.wait()
                else:
                    arrived.wait_recv()
                copy.start()

            pl.when(holder)(hand)

    lift.wait()
    drop.start()
    locals_.append(drop)
    far = {}
    lifted = {}
    passed = []

    def arrive(copy, section, part, i):
        copy.wait_recv()
        passed.append(go(rows(section, part, i), rows(section, part, i), sibling))

    for i in range(SUBS):
        arrive(direct[0, 1, i], chips[1], 1, i)
        far[1, i] = go(rows(chips[1], 1, i), rows(chips[1], 1, i), across[1])
        lifted[1, i] = go(rows(chips[1], 1, i), rows(chips[1], 1, i), along)
        arrive(direct[1, 1, i], chips[2], 1, i)
        lifted[2, i] = go(rows(chips[2], 1, i), rows(chips[2], 1, i), along)
    for i in range(SUBS):
        arrive(direct[1, 0, i], chips[2], 0, i)
        far[0, i] = go(rows(chips[2], 0, i), rows(chips[2], 0, i), across[0])
        arrive(direct[0, 0, i], chips[1], 0, i)
    for i in range(SUBS):
        arrive(far[1, i], chips[3], 1, i)
        lifted[3, i] = go(rows(chips[3], 1, i), rows(chips[3], 1, i), along)
    for i in range(SUBS):
        arrive(far[0, i], chips[3], 0, i)
    for k in range(1, 4):
        for i in range(SUBS):
            arrive(lifted[k, i], chips[k], 2, i)
    for copy in passed + small:
        copy.wait_recv()
    for copy in handed:
        pl.when(jnp.logical_not(holder))(copy.wait_recv)
        pl.when(holder)(copy.wait_send)
    for (copy, whole, rel) in sent_inputs:
        pl.when(chips[rel] // 2 == core)(copy.wait_send)
    for copy in started:
        copy.wait_send()
    for copy in locals_:
        copy.wait()


def gather_all(states, memory, cotangent, bank, gains, ints):
    micro, length, shares = states.shape
    sections = lax.axis_size("section")
    width = shares * sections
    wide = jax.ShapeDtypeStruct((length, width), bf16)
    copies = 9 + 12 + 8 + 4 * SUBS + 2 * SUBS + 3 * SUBS + 9 * SUBS
    outs = [wide, wide, wide, jax.ShapeDtypeStruct((sections * bank.shape[0], width), bf16),
            jax.ShapeDtypeStruct((sections,) + gains.shape, f32)]
    outs += [jax.ShapeDtypeStruct((2,) + t.shape, t.dtype) for t in ints]
    return pl.pallas_call(
        gather_kernel,
        out_shape=outs,
        in_specs=[ANY] * 10,
        out_specs=[ANY] * 10,
        scratch_shapes=[pltpu.VMEM(bank.shape, bank.dtype), pltpu.SemaphoreType.DMA((copies,)), pltpu.SemaphoreType.DMA((copies,)),
                        pltpu.SemaphoreType.DMA((12,))],
        compiler_params=pltpu.CompilerParams(collective_id=0, has_side_effects=True, vmem_limit_bytes=60 * 2**20),
        name="gather_all",
    )(states, memory, cotangent, bank, gains, *ints)


SIZES = (96,) * 10 + (64,)
GROUPS = len(SIZES)
LAGS = (0, 1, 2, 2, 3, 4, 5, 6, 7, 8)
AHEAD = 2
RESULTS = 11


def add_rows(target, rows, *others):
    total = target[rows].astype(f32)
    for other, places in others:
        total = total + other[places].astype(f32)
    target[rows] = total.astype(bf16)


def reduce_kernel(
    dw0, dw1, dw2, dw3, gains0, gains1, gains2, gains3, states, dx, dmem, halt,
    bank, gains_sum, states_out, dx_out, dmem_out, halt_out,
    own, other, first, second, left, right, total, full, mine, theirs, score, scores,
    gain_parts, send, recv, home,
):
    s, d, across, _, sibling = neighbours()
    core, layer = d % 2, d // 2
    chips = [s] + [a[0] for a in across]
    column = [(s, (layer + k) % 4 * 2 + core) for k in range(1, 4)]
    up, down = (s, d + 2), (s, d - 2)
    pair = (s, d + 2 - 4 * (layer % 2))
    jump = (s, (layer + 2) % 4 * 2 + core)
    holder = s // 2 == core
    greet(across + [sibling] + column)
    count = [0, 0]
    always, ends = [], []

    def push(src, dst, device):
        i = count[0]
        count[0] += 1
        return pltpu.make_async_remote_copy(src, dst, send.at[i], recv.at[i], device_id=device, device_id_type=MESH)

    def go(src, dst, device):
        copy = push(src, dst, device)
        copy.start()
        always.append(copy)
        return copy

    def fetch(src, dst):
        i = count[1]
        count[1] += 1
        copy = pltpu.make_async_copy(src, dst, home.at[i])
        return copy

    span = dw0.shape[0]
    half = span // 2
    offsets = [sum(SIZES[:g]) for g in range(GROUPS)]
    grads = (dw0, dw1, dw2, dw3)

    def at(g, side):
        return 2 * offsets[g] + side * SIZES[g]

    loads, swaps = {}, {}

    def exchange(g):
        size = 2 * SIZES[g]
        rows = pl.ds(at(g, 0), size)
        there = pl.ds(pl.multiple_of((1 - core) * half + at(g, 0), 32), size)
        here = pl.ds(pl.multiple_of(core * half + at(g, 0), 32), size)
        for t in range(4):
            swaps[g, t] = go(grads[t].at[there], other.at[t, rows], sibling)
            loads[g, t] = fetch(grads[t].at[here], own.at[t, rows])
            loads[g, t].start()

    for g in range(AHEAD):
        exchange(g)
    outs = ((states, states_out), (dx, dx_out), (dmem, dmem_out))
    given, taken = [], []
    for n, (source, _) in enumerate(outs):
        given.append(push(source, theirs.at[n], sibling))
        taken.append(fetch(source, mine.at[n]))
    given.append(push(halt, scores, sibling))
    taken.append(fetch(halt, score))

    def results_begin():
        for copy in given:
            pl.when(jnp.logical_not(holder))(copy.start)
        for copy in taken:
            pl.when(holder)(copy.start)

    gain_steps = [sibling, across[0], across[1], pair, jump]
    for t, part in enumerate((gains0, gains1, gains2, gains3)):
        gain_parts[0, 2 * t : 2 * t + 2] = part[...]
    gain_copies = []

    def gain_step(k):
        if k > 0:
            gain_copies[-1].wait_recv()
            gain_parts[2 * k] = gain_parts[2 * k - 2] + gain_parts[2 * k - 1]
        if k < len(gain_steps):
            gain_copies.append(go(gain_parts.at[2 * k], gain_parts.at[2 * k + 1], gain_steps[k]))
        else:
            for j in range(2):
                gains_sum[j : j + 1, :] = gain_parts[2 * k, pl.ds(2 * s + j, 1), :]

    step1, step2, rs, ag = {}, {}, {}, {}

    def plane_first(g):
        if g + AHEAD < GROUPS:
            exchange(g + AHEAD)
        for t in range(4):
            swaps[g, t].wait_recv()
            loads[g, t].wait()
            rows = pl.ds(at(g, 0), 2 * SIZES[g])
            add_rows(own, (t, rows), (other, (t, rows)))
        for side in range(2):
            rows = pl.ds(at(g, side), SIZES[g])
            for n, rel in enumerate((3, 1 + side)):
                step1[g, side, n] = go(own.at[chips[rel], rows], first.at[n, rows], across[side])

    def plane_second(g):
        for side in range(2):
            rows = pl.ds(at(g, side), SIZES[g])
            for n, rel in enumerate((2 - side, 0)):
                step1[g, side, n].wait_recv()
                add_rows(own, (chips[rel], rows), (first, (n, rows)))
                if n == 0:
                    step2[g, side] = go(own.at[chips[rel], rows], second.at[rows], across[1 - side])

    def plane_third(g):
        for side in range(2):
            step2[g, side].wait_recv()
            rows = pl.ds(at(g, side), SIZES[g])
            value = own[s, rows].astype(f32) + second[rows].astype(f32)
            total[pl.ds(2 * offsets[g] + side * SIZES[g], SIZES[g])] = value.astype(bf16)

    def span_of(g, k0, k1):
        shard = SIZES[g] // 2
        return pl.ds(2 * offsets[g] + k0 * shard, (k1 - k0) * shard)

    def share(kind, g, low, high, src, dst, device):
        return push(src.at[span_of(g, low, high)], dst.at[span_of(g, low, high)], device)

    def line_sums(g):
        for z in range(3):
            rs[g, "up", z] = share("up", g, z + 1, 4, total, right, up)
            rs[g, "down", z + 1] = share("down", g, 0, z + 1, total, left, down)
        for k in range(4):
            for z in range(k, 3):
                ag[g, "up", z, k] = push(full.at[span_of(g, k, k + 1)], full.at[span_of(g, k, k + 1)], up)
            for z in range(1, k + 1):
                ag[g, "down", z, k] = push(full.at[span_of(g, k, k + 1)], full.at[span_of(g, k, k + 1)], down)

    def at_layer(z, action):
        pl.when(layer == z)(action)

    def close(g, k, *others):
        value = total[span_of(g, k, k + 1)].astype(f32)
        for other_ in others:
            value = value + other_[span_of(g, k, k + 1)].astype(f32)
        full[span_of(g, k, k + 1)] = value.astype(bf16)

    def line_1(g):
        line_sums(g)
        at_layer(0, lambda: rs[g, "up", 0].start())
        at_layer(3, lambda: rs[g, "down", 3].start())

    def line_2(g):
        def second_layer():
            rs[g, "up", 0].wait_recv()
            add_rows(total, span_of(g, 2, 4), (right, span_of(g, 2, 4)))
            rs[g, "up", 1].start()

        def third_layer():
            rs[g, "down", 3].wait_recv()
            add_rows(total, span_of(g, 0, 2), (left, span_of(g, 0, 2)))
            rs[g, "down", 2].start()

        at_layer(1, second_layer)
        at_layer(2, third_layer)

    def line_3(g):
        def third_layer():
            rs[g, "up", 1].wait_recv()
            add_rows(total, span_of(g, 3, 4), (right, span_of(g, 3, 4)))
            rs[g, "up", 2].start()
            close(g, 2, right, left)
            ag[g, "up", 2, 2].start()
            ag[g, "down", 2, 2].start()

        def second_layer():
            rs[g, "down", 2].wait_recv()
            add_rows(total, span_of(g, 0, 1), (left, span_of(g, 0, 1)))
            rs[g, "down", 1].start()
            close(g, 1, right, left)
            ag[g, "up", 1, 1].start()
            ag[g, "down", 1, 1].start()

        at_layer(2, third_layer)
        at_layer(1, second_layer)

    def line_4(g):
        def bottom():
            rs[g, "down", 1].wait_recv()
            close(g, 0, left)
            ag[g, "up", 0, 0].start()

        def top():
            rs[g, "up", 2].wait_recv()
            close(g, 3, right)
            ag[g, "down", 3, 3].start()

        def second_layer():
            ag[g, "down", 2, 2].wait_recv()
            ag[g, "down", 1, 2].start()

        def third_layer():
            ag[g, "up", 1, 1].wait_recv()
            ag[g, "up", 2, 1].start()

        at_layer(0, bottom)
        at_layer(3, top)
        at_layer(1, second_layer)
        at_layer(2, third_layer)

    def line_5(g):
        def bottom():
            ag[g, "down", 1, 1].wait_recv()

        def top():
            ag[g, "up", 2, 2].wait_recv()

        def second_layer():
            ag[g, "up", 0, 0].wait_recv()
            ag[g, "up", 1, 0].start()

        def third_layer():
            ag[g, "down", 3, 3].wait_recv()
            ag[g, "down", 2, 3].start()

        at_layer(0, bottom)
        at_layer(3, top)
        at_layer(1, second_layer)
        at_layer(2, third_layer)

    def line_6(g):
        def bottom():
            ag[g, "down", 1, 2].wait_recv()

        def top():
            ag[g, "up", 2, 1].wait_recv()

        def second_layer():
            ag[g, "down", 2, 3].wait_recv()
            ag[g, "down", 1, 3].start()

        def third_layer():
            ag[g, "up", 1, 0].wait_recv()
            ag[g, "up", 2, 0].start()

        at_layer(0, bottom)
        at_layer(3, top)
        at_layer(1, second_layer)
        at_layer(2, third_layer)

    finals = {}

    def line_7(g):
        at_layer(0, lambda: ag[g, "down", 1, 3].wait_recv())
        at_layer(3, lambda: ag[g, "up", 2, 0].wait_recv())
        here = pl.ds(pl.multiple_of(core * half + at(g, 0), 32), 2 * SIZES[g])
        rows = full.at[pl.ds(2 * offsets[g], 2 * SIZES[g])]
        finals[g] = go(rows, bank.at[here], sibling)
        copy = fetch(rows, bank.at[here])
        copy.start()
        ends.append(copy)

    handed = []

    def results():
        def collect():
            for copy in taken:
                copy.wait()
            for copy in given:
                copy.wait_recv()
            size = mine.shape[1] // 8

            def add(i, _):
                rows = pl.ds(pl.multiple_of(i * size, size), size)
                for n in range(3):
                    add_rows(mine, (n, rows), (theirs, (n, rows)))
                return 0

            lax.fori_loop(0, 8, add, 0)
            score[...] = score[...] + scores[...]

        pl.when(holder)(collect)
        for rel in range(4):
            target = chips[rel]
            for n in range(4):
                out = (states_out, dx_out, dmem_out, halt_out)[n]
                share_ = out.shape[2]
                src = score if n == 3 else mine.at[n]
                src = src.at[:, pl.ds(pl.multiple_of(target * share_, share_), share_)]
                if rel == 0:
                    copy = fetch(src, out.at[s % 2])
                else:
                    copy = push(src, out.at[s % 2], across[rel - 1])
                pl.when(holder)(copy.start)
                handed.append((rel, copy))

    stages = [plane_first, plane_second, plane_third, line_1, line_2, line_3, line_4, line_5, line_6, line_7]
    for tick in range(GROUPS + LAGS[-1]):
        for stage, lag in zip(stages, LAGS):
            if 0 <= tick - lag < GROUPS:
                stage(tick - lag)
        if tick <= len(gain_steps):
            gain_step(tick)
        if tick == RESULTS - 1:
            results_begin()
        if tick == RESULTS:
            results()

    for rel, copy in handed:
        if rel == 0:
            pl.when(holder)(copy.wait)
        else:
            pl.when(chips[rel] // 2 == core)(copy.wait_recv)
            pl.when(holder)(copy.wait_send)
    for copy in given:
        pl.when(jnp.logical_not(holder))(copy.wait_send)
    for copy in finals.values():
        copy.wait_recv()
    for copy in always:
        copy.wait_send()
    for copy in ends:
        copy.wait()
    for (g, way, z), copy in rs.items():
        at_layer(z, copy.wait_send)
    for (g, way, z, k), copy in ag.items():
        at_layer(z, copy.wait_send)


def reduce_all(dw, gains, states, dx, dmem, halt, sections):
    length, width = states.shape
    span = dw[0].shape[0]
    half = span // 2
    shares = width // sections
    micro = 2
    share = jax.ShapeDtypeStruct((micro, length, shares), bf16)
    outs = [jax.ShapeDtypeStruct((span, width), bf16), jax.ShapeDtypeStruct((2, width), f32), share, share, share,
            jax.ShapeDtypeStruct((micro, halt.shape[0], length // sections), f32)]
    copies = 8 * GROUPS + 4 + 5 + (4 + 2 + 6 + 12 + 2) * GROUPS + 12
    scratch = [
        pltpu.VMEM((4, half, width), bf16), pltpu.VMEM((4, half, width), bf16),
        pltpu.VMEM((2, half, width), bf16), pltpu.VMEM((half, width), bf16),
        pltpu.VMEM((half, width), bf16), pltpu.VMEM((half, width), bf16),
        pltpu.VMEM((half, width), bf16), pltpu.VMEM((half, width), bf16),
        pltpu.VMEM((3, length, width), bf16), pltpu.VMEM((3, length, width), bf16),
        pltpu.VMEM(halt.shape, f32), pltpu.VMEM(halt.shape, f32),
        pltpu.VMEM((11, 2 * sections, width), f32),
        pltpu.SemaphoreType.DMA((copies,)), pltpu.SemaphoreType.DMA((copies,)),
        pltpu.SemaphoreType.DMA((8 * GROUPS + 4 + 2 * GROUPS + 4,)),
    ]
    return pl.pallas_call(
        reduce_kernel,
        out_shape=outs,
        in_specs=[ANY] * 4 + [VMEM] * 4 + [ANY] * 4,
        out_specs=[ANY, VMEM, ANY, ANY, ANY, ANY],
        scratch_shapes=scratch,
        compiler_params=pltpu.CompilerParams(collective_id=1, has_side_effects=True, vmem_limit_bytes=60 * 2**20),
        name="reduce_all",
    )(*dw, *gains, states, dx, dmem, halt)


def swap_cores(value):
    count = lax.axis_size("dp")
    return lax.ppermute(value, "dp", [(i, i ^ 1) for i in range(count)])


def gather_plain(states, memory, cotangent, bank, gains, ints):
    section, core = lax.axis_index("section"), lax.axis_index("dp") % 2
    micro = states.shape[0]
    holder = section // micro == core

    def pick(rows):
        own = lax.dynamic_index_in_dim(rows, section % micro, 0, keepdims=False)
        return jnp.where(holder, own, swap_cores(own))

    wide = [pick(lax.all_gather(t, "section", axis=2, tiled=True)) for t in (states, memory, cotangent)]
    return wide, lax.all_gather(bank, "section"), lax.all_gather(gains, "section"), [pick(t) for t in ints]


def reduce_plain(dw, dgains, states, dx, dmem, halt):
    section, core = lax.axis_index("section"), lax.axis_index("dp") % 2
    micro = 2
    holder = section // micro == core

    def to_shares(value):
        both = value.astype(f32) + swap_cores(value).astype(f32)
        both = jnp.where(holder, both, 0).astype(value.dtype)
        slots = jnp.stack([jnp.where(section % micro == i, both, 0) for i in range(micro)])
        return lax.psum_scatter(slots, "section", scatter_dimension=2, tiled=True)

    bank = lax.psum_scatter(jnp.stack(dw), "section", scatter_dimension=0, tiled=True)[0]
    bank = lax.psum(bank.astype(f32), "dp")
    gain_sum = lax.psum_scatter(jnp.stack(dgains), "section", scatter_dimension=0, tiled=True)[0]
    gain_sum = lax.psum(gain_sum, "dp")
    return bank, gain_sum, *[to_shares(t) for t in (states, dx, dmem, halt)]


def local(
    states_in, memory, cotangent, weight_bank, gain_bank, segments, pad_mask, memory_segments, memory_mask, exit_depths
):
    section, sections = lax.axis_index("section"), lax.axis_size("section")
    core = lax.axis_index("dp") % 2
    matrices = weight_bank.shape[1:]
    width = matrices[-1]
    ints = (segments, pad_mask, memory_segments, memory_mask, exit_depths)
    near = sections == 4 and lax.axis_size("dp") == 8
    if near:
        x, mem, top, bank, gains, *ints = gather_all(
            states_in, memory, cotangent, weight_bank[0].reshape(-1, width), gain_bank[0], ints
        )
        bank = bank.reshape((sections,) + matrices)
        row = section
    else:
        (x, mem, top), bank, gains, ints = gather_plain(
            states_in, memory, cotangent, weight_bank[0], gain_bank[0], ints
        )
        ints, row = [t[None, None] for t in ints], jnp.zeros((), i32)
    states, halt, dx, dmem, dw, dgains = row_forward_backward(
        row, core, x, mem, top, bank, gains, ints
    )
    if near:
        grads = [t.reshape(-1, width) for t in dw]
        bank, gain_sum, states, dx, dmem, halt = reduce_all(
            grads, dgains, states, dx, dmem, halt, sections
        )
    else:
        bank, gain_sum, states, dx, dmem, halt = reduce_plain(dw, dgains, states, dx, dmem, halt)
        bank = bank.reshape(-1, width)
    bank, dx, dmem, halt = widen(bank, dx, dmem, halt)
    return states, halt, dx, dmem, bank.reshape((1,) + matrices), gain_sum[None]


def solution(mesh):
    rows = P("dp", None, "section")
    return jax.shard_map(
        local,
        mesh=mesh,
        in_specs=(
            rows, rows, rows, P("section", None, None, None), P("section", None, None),
            P("dp", None), P("dp", None), P("dp", None), P("dp", None), P("dp", None),
        ),
        out_specs=(rows, rows, rows, rows, P("section", None, None, None), P("section", None, None)),
        check_vma=False,
    )
```

```python
import functools

import jax
import jax.numpy as jnp
from jax import lax
from jax.experimental import pallas as pl
from jax.experimental.pallas import tpu as pltpu
from jax.sharding import PartitionSpec as P

HEADS = 8
EPS = 1e-06
BLOCK = 128
KEYS = 256
STEP = 16
NEG = -1e30

bf16 = jnp.bfloat16
f32 = jnp.float32
i32 = jnp.int32

SELF, CROSS = 0, 2
CORE, FLAG_T, FIRST, LAST, TOP_T = 8, 9, 10, 11, 12
FLAG_M, TOP_M = 13, 14


def dot(left, right):
    return jnp.dot(left, right, preferred_element_type=f32)


def dot_nt(left, right):
    return lax.dot_general(left, right, (((1,), (1,)), ((), ())), preferred_element_type=f32)


def dot_tn(left, right):
    return lax.dot_general(left, right, (((0,), (0,)), ((), ())), preferred_element_type=f32)


def norm(x, gain):
    return x * lax.rsqrt(jnp.mean(x * x, axis=-1, keepdims=True) + EPS) * gain


def norm_back(x, gain, grad):
    rate = lax.rsqrt(jnp.mean(x * x, axis=-1, keepdims=True) + EPS)
    scaled = x * rate
    inner = grad * gain
    grad_x = rate * (inner - scaled * jnp.mean(inner * scaled, axis=-1, keepdims=True))
    return grad_x, jnp.sum(grad * scaled, axis=0, keepdims=True)


GELU_A = 0.7978845608028654
GELU_B = 0.044715


def gelu_both(z):
    square = z * z
    bend = jnp.tanh(z * (GELU_A + GELU_A * GELU_B * square))
    half = 0.5 * bend + 0.5
    value = z * half
    return value, half + value * (1.0 - bend) * (GELU_A + 3.0 * GELU_A * GELU_B * square)


def windows(meta, length):
    wide = length * 5 // 8
    slim = length - wide
    core = meta[0, CORE]
    return (
        pl.ds(pl.multiple_of(core * slim, BLOCK), wide),
        pl.ds(pl.multiple_of((1 - core) * wide, BLOCK), slim),
    )


def over(meta, flag, length, work):
    main, other = windows(meta, length)
    work(main, True)

    @pl.when(meta[0, flag] == 1)
    def _():
        work(other, False)


class Moves:
    def __init__(self, meta, length, semaphores):
        self.meta, self.semaphores, self.used, self.leaving = meta, semaphores, 0, []
        self.rows = windows(meta, length)

    def copy(self, src, dst):
        self.used += 1
        return pltpu.make_async_copy(src, dst, self.semaphores.at[self.used - 1])

    def whole(self, src, dst):
        copy = self.copy(src, dst)
        copy.start()
        return copy.wait

    def pair(self, src, dst, flag):
        start, wait = self.parts(src, dst, flag)
        start(True)
        pl.when(self.meta[0, flag] == 1)(lambda: start(False))
        return wait

    def parts(self, src, dst, flag):
        first, second = (self.copy(src.at[rows], dst.at[rows]) for rows in self.rows)

        def start(fresh):
            (first if fresh else second).start()

        def wait():
            first.wait()
            pl.when(self.meta[0, flag] == 1)(second.wait)

        return start, wait

    def away(self, src, dst, flag=None):
        self.leaving.append(self.whole(src, dst) if flag is None else self.pair(src, dst, flag))

    def away_by_part(self, src, dst, flag):
        start, wait = self.parts(src, dst, flag)
        self.leaving.append(wait)
        return start

    def finish(self):
        all_of(*self.leaving)
        self.leaving = []


def all_of(*waits):
    for wait in waits:
        wait()


def block(i):
    return pl.ds(pl.multiple_of(i * BLOCK, BLOCK), BLOCK)


def lanes_of(at, p):
    return slice(at + p * BLOCK, at + (p + 1) * BLOCK)


def two_heads(tile, lane):
    zero = jnp.zeros_like(tile)
    return jnp.concatenate([jnp.where(lane < 64, tile, zero), jnp.where(lane < 64, zero, tile)], axis=0)


def both_blocks(tile):
    return jnp.concatenate([tile[:64, :BLOCK], tile[64:, BLOCK:]], axis=0)


def key_window(meta, kind, top, i, n, low, high):
    wanted = meta[i, kind] + n * KEYS
    start = pl.multiple_of(jnp.minimum(wanted, meta[0, top]), STEP)
    place = lax.broadcasted_iota(i32, (KEYS, BLOCK), 0) + start
    bias = jnp.where((place >= jnp.maximum(low, wanted)) & (place < high), 0.0, NEG)
    return pl.ds(start, KEYS), jnp.concatenate([bias, bias], axis=1)


def two_rows(rows_ref, p, rows):
    return jnp.concatenate([rows_ref[2 * p : 2 * p + 1, rows], rows_ref[2 * p + 1 : 2 * p + 2, rows]], axis=1)


def attend(meta, kind, top, info, info_row, q, k, v, o, lse, both_q, peaks, totals, sums):
    (q, q_at), (k, k_at), (v, v_at) = q, k, v
    pairs = o.shape[1] // BLOCK

    def one_block(i, _):
        count = (meta[i, kind + 1] - meta[i, kind] + KEYS - 1) // KEYS

        @pl.when(count > 0)
        def _():
            rows = block(i)
            lane = lax.broadcasted_iota(i32, (BLOCK, BLOCK), 1)
            low, high = info[info_row : info_row + 1, rows], info[info_row + 1 : info_row + 2, rows]
            peaks[...] = jnp.full(peaks.shape, -jnp.inf, f32)
            totals[...] = jnp.zeros(totals.shape, f32)
            sums[...] = jnp.zeros(sums.shape, f32)
            for p in range(pairs):
                both_q[p] = two_heads(q[rows, lanes_of(q_at, p)], lane)

            def one_window(n, _):
                keys, bias = key_window(meta, kind, top, i, n, low, high)
                scores = [dot_nt(k[keys, lanes_of(k_at, p)], both_q[p]) for p in range(pairs)]
                weights, fades = [], []
                for p in range(pairs):
                    tile = scores[p] + bias
                    before = peaks[p : p + 1, :]
                    peak = jnp.maximum(before, jnp.max(tile, axis=0, keepdims=True))
                    fade = jnp.exp(before - peak)
                    weight = jnp.exp(tile - peak)
                    peaks[p : p + 1, :] = peak
                    totals[p : p + 1, :] = totals[p : p + 1, :] * fade + jnp.sum(weight, axis=0, keepdims=True)
                    weights.append(weight.astype(bf16))
                    fades.append(fade)
                mixes = [dot_tn(v[keys, lanes_of(v_at, p)], weights[p]) for p in range(pairs)]
                for p in range(pairs):
                    fade = fades[p]
                    faded = jnp.concatenate(
                        [jnp.broadcast_to(fade[:, :BLOCK], (64, BLOCK)), jnp.broadcast_to(fade[:, BLOCK:], (64, BLOCK))]
                    )
                    sums[p] = sums[p] * faded + both_blocks(mixes[p])
                return 0

            lax.fori_loop(0, count, one_window, 0)
            for p in range(pairs):
                total = totals[p : p + 1, :]
                share = 1.0 / total
                shares = jnp.concatenate(
                    [jnp.broadcast_to(share[:, :BLOCK], (64, BLOCK)), jnp.broadcast_to(share[:, BLOCK:], (64, BLOCK))]
                )
                o[rows, lanes_of(0, p)] = (sums[p] * shares).T.astype(bf16)
                log_total = peaks[p : p + 1, :] + jnp.log(total)
                lse[2 * p : 2 * p + 1, rows] = log_total[:, :BLOCK]
                lse[2 * p + 1 : 2 * p + 2, rows] = log_total[:, BLOCK:]

        return 0

    lax.fori_loop(meta[0, FIRST], meta[0, LAST], one_block, 0)


def attend_back(meta, kind, top, info, info_row, q, k, v, lse, delta, do, dq, dk, dv, both_q, both_o, sums):
    (q, q_at), (k, k_at), (v, v_at), (dq, dq_at) = q, k, v, dq
    pairs = do.shape[1] // BLOCK

    def one_block(i, _):
        count = (meta[i, kind + 1] - meta[i, kind] + KEYS - 1) // KEYS

        @pl.when(count > 0)
        def _():
            rows = block(i)
            lane = lax.broadcasted_iota(i32, (BLOCK, BLOCK), 1)
            low, high = info[info_row : info_row + 1, rows], info[info_row + 1 : info_row + 2, rows]
            sums[...] = jnp.zeros(sums.shape, f32)
            for p in range(pairs):
                both_q[p] = two_heads(q[rows, lanes_of(q_at, p)], lane)
                both_o[p] = two_heads(do[rows, lanes_of(0, p)], lane)

            def one_window(n, _):
                keys, bias = key_window(meta, kind, top, i, n, low, high)
                def products(p):
                    return dot_nt(k[keys, lanes_of(k_at, p)], both_q[p]), dot_nt(v[keys, lanes_of(v_at, p)], both_o[p])

                def soften(p, score, grad):
                    prob = jnp.exp(score + bias - two_rows(lse, p, rows))
                    return prob.astype(bf16), (prob * (grad - two_rows(delta, p, rows))).astype(bf16)

                def mix(p, prob, grad_score):
                    dv[keys, lanes_of(0, p)] += dot(prob, both_o[p])
                    dk[keys, lanes_of(0, p)] += dot(grad_score, both_q[p])
                    sums[p] += both_blocks(dot_tn(k[keys, lanes_of(k_at, p)], grad_score))

                tiles = {0: products(0), 1: products(1)}
                soft = {}
                for p in range(pairs):
                    soft[p] = soften(p, *tiles[p])
                    if p + 2 < pairs:
                        tiles[p + 2] = products(p + 2)
                    if p > 0:
                        mix(p - 1, *soft[p - 1])
                mix(pairs - 1, *soft[pairs - 1])
                return 0

            lax.fori_loop(0, count, one_window, 0)
            for p in range(pairs):
                dq[rows, lanes_of(dq_at, p)] = (sums[p] * 0.125).T.astype(bf16)

        return 0

    lax.fori_loop(meta[0, FIRST], meta[0, LAST], one_block, 0)


def side_by_side(moves, bank, section, first, place):
    width = place.shape[0]
    return [
        moves.whole(bank.at[section, first + j], place.at[:, j * width : (j + 1) * width])
        for j in range(place.shape[1] // width)
    ]


def stacked(moves, bank, section, first, place):
    width = place.shape[1]
    return [
        moves.whole(bank.at[section, first + j], place.at[j * width : (j + 1) * width])
        for j in range(place.shape[0] // width)
    ]


def forward_kernel(
    sentences, meta, bank, x_in, mem_in, gain, cols, info,
    qkv_out0, o1_out0, l1_0, mid_out0, q2_out0, kv_out0, o2_out0, l2_0, zero_out,
    one_out, active_out, slope_out, scores, exit_grad,
    qkv_out2, o1_out2, l1_2, mid_out2, q2_out2, kv_out2, o2_out2, l2_2, two_out,
    x, mem, qkv, o1, mid, q2, kv, o2, zero, one, two, active, slope,
    wide, third, fourth, pairw, last, up, down, both_q, peaks, totals, sums, semaphores,
):
    length, width = x.shape
    moves = Moves(meta, length, semaphores)
    here = {"x": [moves.pair(x_in, x, FLAG_T)], "self": side_by_side(moves, bank, 0, 0, wide)}

    def ready(*names):
        for name in names:
            all_of(*here.pop(name))

    def attention(layer, state_in, out, saved, final):
        qkv_out, o1_out, l1, mid_out, q2_out, kv_out, o2_out, l2 = saved
        kind, flag_m, top_m = 4 * layer, FLAG_M + 2 * layer, TOP_M + 2 * layer
        section = 2 * layer

        def go(rows):
            return cols[rows, layer : layer + 1]

        ready("self")

        def self_in(rows, _):
            a = norm(state_in[rows, :].astype(f32), gain[section, 0:1]).astype(bf16)
            both = dot(a, wide[...])
            qkv[rows, :width] = (both[:, :width] * 0.125).astype(bf16)
            qkv[rows, width:] = both[:, width:].astype(bf16)
            o1[rows, :] = jnp.zeros((rows.size, width), bf16)
            o2[rows, :] = jnp.zeros((rows.size, width), bf16)

        over(meta, FLAG_T, length, self_in)
        moves.away(qkv, qkv_out, FLAG_T)
        if layer == 0:
            here["self"] = side_by_side(moves, bank, 2, 0, wide)
        ready("pair")

        def memory_in(rows, _):
            kv[rows, :] = dot(mem[rows, :], pairw[...]).astype(bf16)

        over(meta, flag_m, length, memory_in)
        moves.away(kv, kv_out, flag_m)
        if layer == 0:
            here["pair"] = side_by_side(moves, bank, 2, 5, pairw)
            here["up"] = side_by_side(moves, bank, 1, 0, up)
            here["down"] = stacked(moves, bank, 1, 4, down)
        l1[...] = jnp.zeros(l1.shape, f32)
        l2[...] = jnp.zeros(l2.shape, f32)
        attend(
            meta, SELF + kind, TOP_T, info, 0, (qkv, 0), (qkv, width), (qkv, 2 * width), o1, l1,
            both_q, peaks, totals, sums,
        )
        moves.away(o1, o1_out, FLAG_T)
        ready("middle")

        def cross_in(rows, _):
            state = state_in[rows, :].astype(f32) + go(rows) * dot(o1[rows, :], third[...])
            mid[rows, :] = state
            a = norm(state, gain[section, 1:2]).astype(bf16)
            q2[rows, :] = (dot(a, fourth[...]) * 0.125).astype(bf16)

        over(meta, FLAG_T, length, cross_in)
        moves.away(mid, mid_out, FLAG_T)
        moves.away(q2, q2_out, FLAG_T)
        if layer == 0:
            here["middle"] = [moves.whole(bank.at[2, j], place) for j, place in ((3, third), (4, fourth))]
        attend(
            meta, CROSS + kind, top_m, info, 2, (q2, 0), (kv, 0), (kv, width), o2, l2, both_q, peaks, totals, sums
        )
        moves.away(o2, o2_out, FLAG_T)
        ready("last")

        def finish(rows, _):
            out[rows, :] = (mid[rows, :] + go(rows) * dot(o2[rows, :], last[...])).astype(bf16)

        over(meta, FLAG_T, length, finish)
        moves.away(out, final, FLAG_T)
        if layer == 0:
            here["last"] = [moves.whole(bank.at[2, 7], last)]

    ready("x")
    here["memory"] = [moves.pair(mem_in, mem, FLAG_M)]
    here["pair"] = side_by_side(moves, bank, 0, 5, pairw)
    here["middle"] = [moves.whole(bank.at[0, j], place) for j, place in ((3, third), (4, fourth))]
    here["last"] = [moves.whole(bank.at[0, 7], last)]
    here["pair"] += here.pop("memory")
    attention(
        0, x, zero, (qkv_out0, o1_out0, l1_0, mid_out0, q2_out0, kv_out0, o2_out0, l2_0), zero_out
    )
    kept = [moves.parts(src, dst, FLAG_T) for src, dst in ((active, active_out), (slope, slope_out))]

    def dense(rows, fresh):
        state = zero[rows, :].astype(f32)
        a = norm(state, gain[1, 0:1]).astype(bf16)
        if fresh:
            ready("up")
        hidden = [dot(a, up[:, lanes]) for lanes in halves(up)]
        for lanes, z in zip(halves(up), hidden):
            value, gradient = gelu_both(z)
            active[rows, lanes] = value.astype(bf16)
            slope[rows, lanes] = gradient.astype(bf16)
        for start, _ in kept:
            start(fresh)
        if fresh:
            ready("down")
        layer = state + dot(active[rows, :], down[...])
        one[rows, :] = layer.astype(bf16)
        exit_part(layer, gain[1, 1:2], cols, rows, False, scores, exit_grad, fresh, sentences)

    leaving = moves.leaving
    moves.leaving = [kept_wait for _, kept_wait in kept]
    over(meta, FLAG_T, length, dense)
    moves.away(one, one_out, FLAG_T)
    all_of(*leaving)
    attention(
        1, one, two, (qkv_out2, o1_out2, l1_2, mid_out2, q2_out2, kv_out2, o2_out2, l2_2), two_out
    )
    moves.finish()


def backward_kernel(
    meta, bank, x_in, mem_in, gain, cols, info, dh_in, one_in, zero_in, active_in, slope_in, exit_grad,
    qkv_in0, o1_in0, l1_0, mid_in0, q2_in0, kv_in0, o2_in0, l2_0,
    qkv_in2, o1_in2, l1_2, mid_in2, q2_in2, kv_in2, o2_in2, l2_2,
    dx_out, dmem_out, dw_out0, dw_out1, dw_out2, dgain0, dgain1, dgain2,
    x, mem, qkv, o1, mid, q2, kv, o2, dh, dx, dmem, dw, wide, third, fourth, pairw, last, up, down, active, slope,
    dstate, do, dqkv, dk, dv, delta, heads, both_q, both_o, sums, acc, semaphores,
):
    length, width = x.shape
    moves = Moves(meta, length, semaphores)
    here, sent = {}, {}

    def fetch(name, *waits):
        here.setdefault(name, []).extend(waits)

    def ready(*names):
        for name in names:
            all_of(*here.pop(name))

    def send(j, target, value):
        if j in sent:
            sent.pop(j)()
        dw[j] = value.astype(bf16)
        sent[j] = moves.whole(dw.at[j], target.at[j])

    row_of = lax.broadcasted_iota(i32, (HEADS, width), 0)
    lane_of = lax.broadcasted_iota(i32, (HEADS, width), 1)

    def fetch_cross(layer):
        o2_in, q2_in, kv_in = (o2_in0, q2_in0, kv_in0) if layer == 0 else (o2_in2, q2_in2, kv_in2)
        fetch("cross", moves.whole(bank.at[2 * layer, 7], last), moves.pair(o2_in, o2, FLAG_T))
        fetch("cross tiles", moves.pair(q2_in, q2, FLAG_T), moves.pair(kv_in, kv, FLAG_M + 2 * layer))

    def fetch_middle(layer):
        fetch("memory", *side_by_side(moves, bank, 2 * layer, 5, pairw))
        fetch("middle", moves.whole(bank.at[2 * layer, 4], fourth))
        fetch("middle", moves.pair(mid_in0 if layer == 0 else mid_in2, mid, FLAG_T))

    def fetch_self(layer):
        o1_in, qkv_in = (o1_in0, qkv_in0) if layer == 0 else (o1_in2, qkv_in2)
        fetch("self", moves.whole(bank.at[2 * layer, 3], third), moves.pair(o1_in, o1, FLAG_T))
        fetch("self tiles", moves.pair(qkv_in, qkv, FLAG_T))

    def fetch_entry(layer):
        fetch("entry", *side_by_side(moves, bank, 2 * layer, 0, wide))

    def weight_grad(target, targets, flag, left, right):
        size = len(targets) * width

        def part(rows, fresh):
            term = dot_tn(left(rows), right(rows))
            for n in range(len(targets)):
                place = slice(n * width, (n + 1) * width)
                acc[place] = term[:, place] if fresh else acc[place] + term[:, place]

        over(meta, flag, length, part)
        for n, j in enumerate(targets):
            send(j, target, acc[n * width : (n + 1) * width])

    def attention(layer, grad_in, grad_out, dw_out, dgain, l1, l2, after):
        kind, flag_m, top_m = 4 * layer, FLAG_M + 2 * layer, TOP_M + 2 * layer
        section = 2 * layer

        def go(rows):
            return cols[rows, layer : layer + 1]

        def clear(rows, _):
            dk[rows, :] = jnp.zeros((rows.size, width), f32)
            dv[rows, :] = jnp.zeros((rows.size, width), f32)

        def begin(grad_of, o, out_weight, target):
            def dy(rows):
                return (go(rows) * grad_of(rows)).astype(bf16)

            def part(rows, _):
                grad = dot_nt(dy(rows), out_weight[...]).astype(bf16)
                do[rows, :] = grad
                product = grad.astype(f32) * o[rows, :].astype(f32)
                high = product.astype(bf16)
                rest = (product - high.astype(f32)).astype(bf16)
                delta[:, rows] = dot_nt(heads[...], high) + dot_nt(heads[...], rest)
                dqkv[rows, :width] = jnp.zeros((rows.size, width), bf16)

            over(meta, FLAG_T, length, part)
            weight_grad(dw_out, [target], FLAG_T, lambda rows: o[rows, :], dy)

        def top_grad(rows):
            return grad_in[rows, :].astype(f32)

        over(meta, flag_m, length, clear)
        ready("cross")
        begin(top_grad, o2, last, 7)
        ready("cross tiles")
        attend_back(
            meta, CROSS + kind, top_m, info, 2, (q2, 0), (kv, 0), (kv, width), l2, delta, do, (dqkv, 0), dk, dv,
            both_q, both_o, sums,
        )
        after("cross")
        ready("memory")

        def memory_out(rows, _):
            dqkv[rows, width : 2 * width] = dk[rows, :].astype(bf16)
            dqkv[rows, 2 * width :] = dv[rows, :].astype(bf16)
            term = dot_nt(dqkv[rows, width:], pairw[...])
            dmem[rows, :] = (dmem[rows, :].astype(f32) + term).astype(bf16)

        over(meta, flag_m, length, memory_out)
        if layer == 0:
            moves.away(dmem, dmem_out)
        weight_grad(dw_out, [5, 6], flag_m, lambda rows: mem[rows, :], lambda rows: dqkv[rows, width:])
        ready("middle")

        def cross_out(rows, fresh):
            grad_normed = dot_nt(dqkv[rows, :width], fourth[...])
            grad_x, grad_gain = norm_back(mid[rows, :], gain[section, 1:2], grad_normed)
            dstate[rows, :] = top_grad(rows) + grad_x
            dgain[1:2, :] = grad_gain if fresh else dgain[1:2, :] + grad_gain

        over(meta, FLAG_T, length, cross_out)
        weight_grad(
            dw_out, [4], FLAG_T, lambda rows: norm(mid[rows, :], gain[section, 1:2]).astype(bf16),
            lambda rows: dqkv[rows, :width],
        )
        after("middle")
        over(meta, FLAG_T, length, clear)
        ready("self")
        begin(lambda rows: dstate[rows, :], o1, third, 3)
        ready("self tiles")
        attend_back(
            meta, SELF + kind, TOP_T, info, 0, (qkv, 0), (qkv, width), (qkv, 2 * width), l1, delta, do, (dqkv, 0),
            dk, dv, both_q, both_o, sums,
        )
        after("self")
        ready("entry", "x")
        if layer == 0:
            grad_out[...] = jnp.zeros(grad_out.shape, bf16)

        def self_out(rows, fresh):
            dqkv[rows, width : 2 * width] = dk[rows, :].astype(bf16)
            dqkv[rows, 2 * width :] = dv[rows, :].astype(bf16)
            grad_normed = dot_nt(dqkv[rows, :], wide[...])
            grad_x, grad_gain = norm_back(x[rows, :].astype(f32), gain[section, 0:1], grad_normed)
            value = dstate[rows, :] + grad_x
            if layer == 0:
                value = jnp.where(cols[rows, 2:3] > 0.0, value, 0.0)
            grad_out[rows, :] = value.astype(bf16)
            dgain[0:1, :] = grad_gain if fresh else dgain[0:1, :] + grad_gain

        over(meta, FLAG_T, length, self_out)
        if layer == 0:
            moves.away(grad_out, dx_out)
        weight_grad(
            dw_out, [0, 1, 2], FLAG_T, lambda rows: norm(x[rows, :].astype(f32), gain[section, 0:1]).astype(bf16),
            lambda rows: dqkv[rows, :],
        )
        after("end")

    def after_two(stage):
        if stage == "cross":
            fetch_cross(0)
            fetch("down", *stacked(moves, bank, 1, 4, down))
        if stage == "middle":
            fetch_middle(0)
            fetch("slope", moves.pair(slope_in, slope, FLAG_T))
            fetch("active", moves.pair(active_in, active, FLAG_T))
        if stage == "self":
            fetch_self(0)
            fetch("up", *side_by_side(moves, bank, 1, 0, up))
        if stage == "end":
            fetch("x", moves.pair(zero_in, x, FLAG_T))
            fetch_entry(0)

    fetch("dh", moves.pair(dh_in, dh, FLAG_T))
    fetch_cross(1)
    heads[...] = (lane_of // (width // HEADS) == row_of).astype(bf16)
    delta[...] = jnp.zeros(delta.shape, f32)
    dmem[...] = jnp.zeros(dmem.shape, bf16)
    ready("dh")
    fetch_middle(1)
    fetch("memory", moves.pair(mem_in, mem, FLAG_M))
    fetch_self(1)
    fetch_entry(1)
    fetch("x", moves.pair(one_in, x, FLAG_T))
    attention(1, dh, dx, dw_out2, dgain2, l1_2, l2_2, after_two)

    ready("down", "slope")

    def hidden(rows, fresh):
        for lanes in halves(up):
            grad = dot_nt(dx[rows, :], down[lanes])
            slope[rows, lanes] = (slope[rows, lanes].astype(f32) * grad).astype(bf16)

    over(meta, FLAG_T, length, hidden)
    ready("active")

    def down_part(rows, fresh):
        term = dot_tn(active[rows, :], dx[rows, :])
        acc[...] = term if fresh else acc[...] + term

    over(meta, FLAG_T, length, down_part)
    parts = acc.shape[0] // width
    for j in range(parts):
        send(parts + j, dw_out1, acc[j * width : (j + 1) * width])
    ready("x", "up")

    def normalise(rows, _):
        do[rows, :] = norm(x[rows, :].astype(f32), gain[1, 0:1]).astype(bf16)

    over(meta, FLAG_T, length, normalise)

    def up_part(rows, fresh):
        term = dot_tn(do[rows, :], slope[rows, :])
        for j in range(parts):
            place = slice(j * width, (j + 1) * width)
            acc[place] = term[:, place] if fresh else acc[place] + term[:, place]

    over(meta, FLAG_T, length, up_part)
    for j in range(parts):
        send(j, dw_out1, acc[j * width : (j + 1) * width])

    def back(rows, fresh):
        grad_normed = dot_nt(slope[rows, :], up[...])
        grad_x, grad_gain = norm_back(x[rows, :].astype(f32), gain[1, 0:1], grad_normed)
        dh[rows, :] = (dx[rows, :].astype(f32) + grad_x).astype(bf16)
        dgain1[0:1, :] = grad_gain if fresh else dgain1[0:1, :] + grad_gain

    over(meta, FLAG_T, length, back)
    dgain1[1:2, :] = exit_grad[...]
    fetch("x", moves.pair(x_in, x, FLAG_T))
    attention(0, dh, dx, dw_out0, dgain0, l1_0, l2_0, lambda stage: None)
    all_of(*sent.values())
    moves.finish()


def exit_part(layer, vector, cols, rows, last, score_at, exit_grad, fresh, sentences):
    factor = layer.shape[1] ** (-0.5)
    score = jax.nn.sigmoid(jnp.sum(layer * vector, axis=-1, keepdims=True) * factor)
    score_at[rows, :] = jnp.broadcast_to(score, (rows.size, score_at.shape[1]))
    target = cols[rows, 0:1] if last else cols[rows, 4:5]
    weight = cols[rows, 3:4] * (score - target) * (factor / sentences)
    term = jnp.sum(weight * layer, axis=0, keepdims=True)
    exit_grad[...] = term if fresh else exit_grad[...] + term


def up_weights(moves, bank, section, up, width):
    parts = up.shape[1] // width
    return [moves.whole(bank.at[section, j], up.at[:, j * width : (j + 1) * width]) for j in range(parts)]


def down_weights(moves, bank, section, down, width):
    parts = down.shape[0] // width
    return [moves.whole(bank.at[section, parts + j], down.at[j * width : (j + 1) * width]) for j in range(parts)]


def halves(up):
    hidden = up.shape[1]
    return [slice(i * hidden // 2, (i + 1) * hidden // 2) for i in range(2)]


def dense_gradient(meta, moves, length, acc, left, right, pieces):
    def part(rows, fresh):
        term = dot_tn(left[rows, :], right[rows, :])
        rows_, lanes_ = term.shape
        acc[:rows_, :lanes_] = term if fresh else acc[:rows_, :lanes_] + term

    over(meta, FLAG_T, length, part)
    for block_, place, target in pieces:
        place[...] = block_().astype(bf16)
        moves.away(place, target)


def down_pieces(acc, dw, dw_out, width):
    parts = dw.shape[0] // 2
    return [
        (lambda j=j: acc[j * width : (j + 1) * width, :], dw.at[parts + j], dw_out.at[parts + j]) for j in range(parts)
    ]


def up_pieces(acc, dw, dw_out, width):
    return [
        (lambda j=j: acc[:, j * width : (j + 1) * width], dw.at[j], dw_out.at[j]) for j in range(dw.shape[0] // 2)
    ]


def dense_last_kernel(
    sentences, meta, bank, x_in, gain, cols, dh_in, before, dx_out, dw_out, dgain, states, halt,
    x, dh, dy, normed, scores, exit_grad, out, dx, dw, active, dhidden, up, down, acc_up, acc_down, semaphores
):
    section = 3
    length, width = x.shape
    moves = Moves(meta, length, semaphores)
    x_here = moves.pair(x_in, x, FLAG_T)
    up_here = up_weights(moves, bank, section, up, width)
    out[...] = jnp.zeros(out.shape, bf16)
    scores[...] = jnp.zeros(scores.shape, f32)
    x_here()

    def forward(rows, fresh):
        own = cols[rows, 2:3] > 0.0
        state = x[rows, :].astype(f32)
        a = norm(state, gain[section, 0:1]).astype(bf16)
        normed[rows, :] = a
        if fresh:
            all_of(*up_here)
            down_here = down_weights(moves, bank, section, down, width) + [moves.pair(dh_in, dh, FLAG_T)]
        hidden = [dot(a, up[:, lanes]) for lanes in halves(up)]
        if fresh:
            all_of(*down_here)
        go = cols[rows, 1:2]
        dy[rows, :] = (go * jnp.where(own, dh[rows, :].astype(f32), 0.0)).astype(bf16)
        for lanes, z in zip(halves(up), hidden):
            grad = dot_nt(dy[rows, :], down[lanes])
            value, gradient = gelu_both(z)
            active[rows, lanes] = value.astype(bf16)
            dhidden[rows, lanes] = (gradient * grad).astype(bf16)
        layer = state + go * dot(active[rows, :], down[...])
        out[rows, :] = jnp.where(own, layer, 0.0).astype(bf16)
        exit_part(layer, gain[section, 1:2], cols, rows, True, scores, exit_grad, fresh, sentences)

    over(meta, FLAG_T, length, forward)
    moves.away(out, states)
    dense_gradient(meta, moves, length, acc_down, active, dy, down_pieces(acc_down, dw, dw_out, width))
    dense_gradient(meta, moves, length, acc_up, normed, dhidden, up_pieces(acc_up, dw, dw_out, width))
    dgain[1:2, :] = exit_grad[...]
    lane = lax.broadcasted_iota(i32, (BLOCK, 8), 1)
    for i in range(length // BLOCK):
        rows = slice(i * BLOCK, (i + 1) * BLOCK)
        both = jnp.where(lane == 0, before[rows, :], scores[rows, :])
        halt[:, rows] = jnp.where(cols[rows, 2:3] > 0.0, both, 0.0).T

    def back(rows, fresh):
        grad_out = jnp.where(cols[rows, 2:3] > 0.0, dh[rows, :].astype(f32), 0.0)
        grad_normed = dot_nt(dhidden[rows, :], up[...])
        grad_x, grad_gain = norm_back(x[rows, :].astype(f32), gain[section, 0:1], grad_normed)
        dx[rows, :] = (grad_out + grad_x).astype(bf16)
        dgain[0:1, :] = grad_gain if fresh else dgain[0:1, :] + grad_gain

    over(meta, FLAG_T, length, back)
    moves.away(dx, dx_out, FLAG_T)
    moves.finish()


def widen_kernel(bank, dx, dmem, halt, bank_out, dx_out, dmem_out, halt_out):
    bank_out[...] = bank[...].astype(f32)
    dx_out[...] = dx[...].astype(f32)
    dmem_out[...] = dmem[...].astype(f32)
    halt_out[...] = halt[:, : halt_out.shape[1], :]


def widen(bank, dx, dmem, halt):
    steps = 8
    span, width = bank.shape
    micro, length, shares = dx.shape

    def some(shape, *place):
        return pl.BlockSpec(shape, lambda i: tuple(i if p else 0 for p in place))

    rows = some((micro, length // steps, shares), 0, 1, 0)
    whole = some((span // steps, width), 1, 0)
    halting = (micro, 2, halt.shape[2])
    return pl.pallas_call(
        widen_kernel,
        grid=(steps,),
        out_shape=[jax.ShapeDtypeStruct(t.shape, f32) for t in (bank, dx, dmem)]
        + [jax.ShapeDtypeStruct(halting, f32)],
        in_specs=[whole, rows, rows, some(halt.shape, 0, 0, 0)],
        out_specs=[whole, rows, rows, some(halting, 0, 0, 0)],
        compiler_params=pltpu.CompilerParams(vmem_limit_bytes=60 * 2**20),
        name="widen",
    )(bank, dx, dmem, halt)


def plan_kernel(sentences, row, core, seg, pad, mseg, mmask, depths, meta, info, cols):
    row, core = row[0], core[0]
    length, slots = seg.shape[2], mseg.shape[2]
    blocks = length // BLOCK
    micro = seg.shape[1]

    def pick(table):
        return table[row // micro, pl.ds(row % micro, 1), :]

    seg, pad, mseg, mmask, depths = (pick(t) for t in (seg, pad, mseg, mmask, depths))
    number = lax.broadcasted_iota(i32, (sentences, length), 0)
    place = lax.broadcasted_iota(i32, (1, length), 1)

    def count(marks):
        return jnp.sum(marks.astype(f32), axis=1, keepdims=True).astype(i32)

    square = lax.broadcasted_iota(i32, (sentences, sentences), 0) == lax.broadcasted_iota(
        i32, (sentences, sentences), 1
    )
    depth_row = jnp.broadcast_to(depths, (sentences, sentences))
    depth_table = jnp.sum(jnp.where(square, depth_row, 0).astype(f32), axis=1, keepdims=True).astype(i32)
    mine = seg == number
    starts = count(seg < number)
    filled = count(pad == 1)
    memory_number = lax.broadcasted_iota(i32, (sentences, slots), 0)
    memory_starts = count(mseg < memory_number)
    memory_stops = jnp.minimum(count(mseg <= memory_number), count(mmask == 1))

    def of_token(table):
        return jnp.sum(jnp.where(mine, table, 0), axis=0, keepdims=True)

    low = of_token(starts)
    high = jnp.where(pad == 1, jnp.minimum(place, filled - 1), place) + 1
    cross_low = jnp.where(pad == 0, 0, of_token(memory_starts))
    cross_high = jnp.where(pad == 0, slots, of_token(memory_stops))
    depth = of_token(depth_table)
    keep = depth == 2

    def by_block(values):
        return jnp.concatenate([values[:, i * BLOCK : (i + 1) * BLOCK] for i in range(blocks)], axis=0)

    def spans(used, lows, highs):
        lows = jnp.min(by_block(jnp.where(used, lows, slots)), axis=1, keepdims=True)
        highs = jnp.max(by_block(jnp.where(used, highs, 0)), axis=1, keepdims=True)
        return jnp.minimum(lows, highs) // STEP * STEP, highs

    work = jnp.zeros((blocks, 1), i32)
    for used in (place >= 0, keep):
        for lows, highs in ((low, high), (cross_low, cross_high)):
            from_, to = spans(used, lows, highs)
            work = work + 2 * ((to - from_ + KEYS - 1) // KEYS) + jnp.where(to > from_, 1, 0)
    start = jnp.sum(jnp.where(square, starts, 0), axis=0, keepdims=True)
    block_at = lax.broadcasted_iota(i32, (blocks, sentences), 0) * BLOCK
    before = jnp.sum(jnp.where(block_at < start, work, 0), axis=0, keepdims=True)
    after = jnp.sum(jnp.where(block_at + BLOCK > start, work, 0), axis=0, keepdims=True)
    after = after + jnp.where(filled < length, 5, 0)
    off = jnp.abs(start - length // 2)
    score = jnp.maximum(before, after) * length + off
    score = score + jnp.where(off > length // 8, length * length, 0)
    score = jnp.where(lax.broadcasted_iota(i32, (1, sentences), 1) > 0, score, 2 * length * length)
    best = jnp.min(score, axis=1, keepdims=True)
    cut = jnp.min(jnp.where(score == best, start, length), axis=1, keepdims=True)

    def by_core(first, second):
        return first * (1 - core) + second * core

    below = jnp.where(place < cut, 1, 0)
    owned = by_core(below, 1 - below) == 1
    begin = by_core(0, cut // BLOCK)
    end = by_core((cut + BLOCK - 1) // BLOCK, blocks)
    wide = length * 5 // 8
    base = by_core(0, length - wide)

    def outside(from_place, to_place):
        return by_core(jnp.where(to_place > wide, 1, 0), jnp.where(from_place < length - wide, 1, 0))

    def top_of(flag):
        return jnp.where(flag == 1, length - KEYS, base + wide - KEYS)

    lane = lax.broadcasted_iota(i32, (blocks, 128), 1)
    table = jnp.zeros((blocks, 128), i32)
    flag_t = outside(begin * BLOCK, end * BLOCK)
    entries = {CORE: jnp.full((1, 1), core, i32), FLAG_T: flag_t, FIRST: begin, LAST: end, TOP_T: top_of(flag_t)}
    for layer in range(2):
        used = owned if layer == 0 else owned & keep
        for kind, lows, highs in ((SELF, low, high), (CROSS, cross_low, cross_high)):
            entries[kind + 4 * layer], entries[kind + 4 * layer + 1] = spans(used, lows, highs)
        flag_m = outside(
            jnp.min(jnp.where(used, cross_low, slots), axis=1, keepdims=True),
            jnp.max(jnp.where(used, cross_high, 0), axis=1, keepdims=True),
        )
        entries[FLAG_M + 2 * layer] = flag_m
        entries[TOP_M + 2 * layer] = top_of(flag_m)
    for column, values in entries.items():
        table = jnp.where(lane == column, values, table)
    meta[...] = table
    info[...] = jnp.concatenate([low, high, cross_low, cross_high, low, low, low, low], axis=0)
    ones = jnp.ones((1, length), f32)
    kept, own = keep.astype(f32), owned.astype(f32)
    counted = jnp.where(pad == 1, own, 0.0)
    by_row = jnp.concatenate([ones, kept, own, counted, (depth == 1).astype(f32), own, own, own], axis=0)
    for i in range(blocks):
        cols[i * BLOCK : (i + 1) * BLOCK, :] = by_row[:, i * BLOCK : (i + 1) * BLOCK].T


ANY = pl.BlockSpec(memory_space=pltpu.HBM)
VMEM = pl.BlockSpec(memory_space=pltpu.VMEM)
SMEM = pl.BlockSpec(memory_space=pltpu.SMEM)


def make_plan(row, core, ints):
    seg, pad, mseg, mmask, depths = ints
    length, sentences = seg.shape[-1], depths.shape[-1]
    outs = [((length // BLOCK, 128), i32), ((8, length), i32), ((length, 8), f32)]
    return pl.pallas_call(
        functools.partial(plan_kernel, sentences),
        out_shape=[jax.ShapeDtypeStruct(*out) for out in outs],
        in_specs=[SMEM, SMEM] + [VMEM] * 5,
        out_specs=[VMEM] * 3,
        compiler_params=pltpu.CompilerParams(vmem_limit_bytes=60 * 2**20),
        name="make_plan",
    )(row.astype(i32)[None], core.astype(i32)[None], seg, pad, mseg, mmask, depths)


def run(kernel, ins, outs, scratch, semaphores, name, flops, *args):
    return pl.pallas_call(
        kernel,
        out_shape=[jax.ShapeDtypeStruct(shape, dtype) for _, shape, dtype in outs],
        in_specs=ins,
        out_specs=[spec for spec, _, _ in outs],
        scratch_shapes=[pltpu.VMEM(shape, dtype) for shape, dtype in scratch]
        + [pltpu.SemaphoreType.DMA((semaphores,))],
        compiler_params=pltpu.CompilerParams(vmem_limit_bytes=63 * 2**20),
        cost_estimate=pl.CostEstimate(flops=flops, bytes_accessed=20 * 2**20, transcendentals=0),
        name=name,
    )(*args)


def forward(plan, bank, x, mem, gain, sentences):
    meta, info, cols = plan
    length, width = x.shape
    pairs = width // BLOCK
    hidden = bank.shape[1] // 2 * width

    def rows(n, dtype=bf16):
        return ((length, n * width), dtype)

    def put(shape, dtype):
        return (ANY, shape, dtype)

    logs = (VMEM, (HEADS, length), f32)
    inner = ((length, hidden), bf16)
    saved = [put(*rows(3)), put(*rows(1)), logs, put(*rows(1, f32)), put(*rows(1)), put(*rows(2)), put(*rows(1)), logs,
             put(*rows(1))]
    outs = saved + [put(*rows(1)), put(*inner), put(*inner), (VMEM, cols.shape, f32), (VMEM, (1, width), f32)] + saved
    square = ((width, width), bf16)
    scratch = [
        rows(1), rows(1), rows(3), rows(1), rows(1, f32), rows(1), rows(2), rows(1), rows(1), rows(1), rows(1), inner, inner,
        ((width, 3 * width), bf16), square, square, ((width, 2 * width), bf16), square,
        ((width, hidden), bf16), ((hidden, width), bf16),
        ((pairs, 2 * BLOCK, BLOCK), bf16), ((8, 2 * BLOCK), f32), ((8, 2 * BLOCK), f32), ((pairs, BLOCK, BLOCK), f32),
    ]
    results = run(
        functools.partial(forward_kernel, sentences), [SMEM, ANY, ANY, ANY, VMEM, VMEM, VMEM], outs, scratch, 96,
        "forward", 16 * 10**9, meta, bank, x, mem, gain, cols, info,
    )
    return results[:8], results[8], results[9:14], results[14:22], results[22]


def backward(plan, bank, x, mem, gain, dh, one, zero, active, slope, exit_grad, saved0, saved2):
    meta, info, cols = plan
    length, width = x.shape
    pairs = width // BLOCK
    hidden = bank.shape[1] // 2 * width

    def rows(n, dtype=bf16):
        return ((length, n * width), dtype)

    square, matrices = ((width, width), bf16), (bank.shape[1:], bf16)
    gains = [(VMEM, (2, width), f32)] * 3
    outs = [(ANY, *rows(1)), (ANY, *rows(1))] + [(ANY, *matrices)] * 3 + gains
    both = ((pairs, 2 * BLOCK, BLOCK), bf16)
    inner = ((length, hidden), bf16)
    scratch = [
        rows(1), rows(1), rows(3), rows(1), rows(1, f32), rows(1), rows(2), rows(1), rows(1), rows(1), rows(1), matrices,
        ((width, 3 * width), bf16), square, square, ((width, 2 * width), bf16), square,
        ((width, hidden), bf16), ((hidden, width), bf16), inner, inner,
        rows(1, f32), rows(1), rows(3), rows(1, f32), rows(1, f32), ((HEADS, length), f32), ((HEADS, width), bf16),
        both, both, ((pairs, BLOCK, BLOCK), f32), ((hidden, width), f32),
    ]
    kept = [ANY, ANY, VMEM, ANY, ANY, ANY, ANY, VMEM]
    ins = [SMEM, ANY, ANY, ANY, VMEM, VMEM, VMEM] + [ANY] * 5 + [VMEM] + kept + kept
    return run(
        backward_kernel, ins, outs, scratch, 160, "backward", 30 * 10**9,
        meta, bank, x, mem, gain, cols, info, dh, one, zero, active, slope, exit_grad, *saved0, *saved2,
    )


def dense_shapes(bank, x):
    length, width = x.shape
    hidden = bank.shape[1] // 2 * width
    return ((length, width), bf16), ((length, hidden), bf16), ((width, hidden), bf16), ((hidden, width), bf16)


def dense_last(plan, bank, x, gain, dh, before, sentences, name):
    meta, _, cols = plan
    wide, inner, up, down = dense_shapes(bank, x)
    length, width = x.shape
    matrices = (bank.shape[1:], bf16)
    outs = [(ANY, *wide), (ANY, *matrices), (VMEM, (2, width), f32), (ANY, *wide), (VMEM, (8, length), f32)]
    scratch = [wide, wide, wide, wide, (cols.shape, f32), ((1, width), f32), wide, wide, matrices, inner, inner, up, down,
               (up[0], f32), (down[0], f32)]
    return run(
        functools.partial(dense_last_kernel, sentences), [SMEM, ANY, ANY, VMEM, VMEM, ANY, VMEM], outs, scratch, 32,
        name, 8 * 10**9, meta, bank, x, gain, cols, dh, before,
    )


def row_forward_backward(row, core, x, mem, cotangent, bank, gains, ints):
    plan = make_plan(row, core, ints)
    sentences = ints[-1].shape[-1]
    saved0, zero, (one, active, slope, scores, exit0), saved2, two = forward(plan, bank, x, mem, gains, sentences)
    dtwo, dw3, dgain3, states, halt = dense_last(plan, bank, two, gains, cotangent, scores, sentences, "dense_three")
    dx, dmem, dw0, dw1, dw2, dgain0, dgain1, dgain2 = backward(
        plan, bank, x, mem, gains, dtwo, one, zero, active, slope, exit0, saved0, saved2
    )
    return states, halt, dx, dmem, [dw0, dw1, dw2, dw3], [dgain0, dgain1, dgain2, dgain3]


MESH = pl.DeviceIdType.MESH


def neighbours():
    s, d = lax.axis_index("section"), lax.axis_index("dp")
    across = [(s + 1 - 2 * (s % 2), d), ((s + 2) % 4, d), (3 - s, d)]
    layer = d // 2
    along = (s, d + 2 - 4 * (layer % 2))
    sibling = (s, d + 1 - 2 * (d % 2))
    return s, d, across, along, sibling


def greet(devices):
    barrier = pltpu.get_barrier_semaphore()
    for device in devices:
        pl.semaphore_signal(barrier, inc=1, device_id=device, device_id_type=MESH)
    pl.semaphore_wait(barrier, len(devices))


SUBS = 4


def gather_kernel(
    states, memory, cotangent, bank, gains, seg, pad, mseg, mmask, depths,
    x, mem, top, weights, gains_all, seg2, pad2, mseg2, mmask2, depths2,
    staging, send, recv, home,
):
    s, d, across, along, sibling = neighbours()
    core = d % 2
    parity = (d // 2) % 2
    greet(across + [along, sibling])
    started = []
    locals_ = []
    count = [0, 0]

    def push(src, dst, device):
        i = count[0]
        count[0] += 1
        copy = pltpu.make_async_remote_copy(src, dst, send.at[i], recv.at[i], device_id=device, device_id_type=MESH)
        return copy

    def go(src, dst, device):
        copy = push(src, dst, device)
        copy.start()
        started.append(copy)
        return copy

    def keep(src, dst):
        i = count[1]
        count[1] += 1
        copy = pltpu.make_async_copy(src, dst, home.at[i])
        return copy

    shares = states.shape[2]
    chips = [s] + [a[0] for a in across]
    sent_inputs, own_inputs = [], []
    for source, whole in ((states, x), (memory, mem), (cotangent, top)):
        for rel in range(4):
            target = chips[rel]
            mine = target // 2 == core
            dst = whole.at[:, pl.ds(pl.multiple_of(s * shares, shares), shares)]
            src = source.at[target % 2]
            if rel == 0:
                copy = keep(src, dst)
                own_inputs.append(copy)
            else:
                copy = push(src, dst, across[rel - 1])
                sent_inputs.append((copy, whole, rel))
            pl.when(mine)(copy.start)
    small = [go(source, whole.at[core], sibling)
             for source, whole in ((seg, seg2), (pad, pad2), (mseg, mseg2), (mmask, mmask2), (depths, depths2))]
    small += [go(gains, gains_all.at[s], device) for device in across]
    for source, whole in ((seg, seg2), (pad, pad2), (mseg, mseg2), (mmask, mmask2), (depths, depths2)):
        copy = keep(source, whole.at[core])
        copy.start()
        locals_.append(copy)
    copy = keep(gains, gains_all.at[s])
    copy.start()
    locals_.append(copy)

    span = bank.shape[0]
    half = span // 2
    third = half // 3 // (16 * SUBS) * (16 * SUBS)
    first = half - 2 * third
    sub0, sub1 = first // SUBS, third // SUBS

    def rows(section, part, i):
        at = section * span + core * half
        size = sub0 if part == 0 else sub1
        if part == 0:
            at = at + i * size
        elif part == 1:
            at = at + first + parity * third + i * size
        else:
            at = at + first + (1 - parity) * third + i * size
        return weights.at[pl.ds(pl.multiple_of(at, 16), size)]

    def own_rows(part, i):
        size = sub0 if part == 0 else sub1
        at = core * half + (i * size if part == 0 else first + parity * third + i * size)
        return bank.at[pl.ds(pl.multiple_of(at, 16), size)]

    direct = {}
    for part in (1, 0):
        for i in range(SUBS):
            for k in range(2):
                direct[k, part, i] = go(own_rows(part, i), rows(s, part, i), across[k])
    lift = keep(bank, staging)
    lift.start()
    drop = keep(staging, weights.at[pl.ds(pl.multiple_of(s * span, span), span)])

    holder = s // 2 == core
    handed = []
    for n, (source, whole) in enumerate(((states, x), (memory, mem), (cotangent, top))):
        for rel in range(4):
            lanes = whole.at[:, pl.ds(pl.multiple_of(chips[rel] * shares, shares), shares)]
            copy = push(lanes, lanes, sibling)
            handed.append(copy)
            arrived = own_inputs[n] if rel == 0 else sent_inputs[n * 3 + rel - 1][0]

            def hand(copy=copy, arrived=arrived, rel=rel):
                if rel == 0:
                    arrived.wait()
                else:
                    arrived.wait_recv()
                copy.start()

            pl.when(holder)(hand)

    lift.wait()
    drop.start()
    locals_.append(drop)
    far = {}
    lifted = {}
    passed = []

    def arrive(copy, section, part, i):
        copy.wait_recv()
        passed.append(go(rows(section, part, i), rows(section, part, i), sibling))

    for i in range(SUBS):
        arrive(direct[0, 1, i], chips[1], 1, i)
        far[1, i] = go(rows(chips[1], 1, i), rows(chips[1], 1, i), across[1])
        lifted[1, i] = go(rows(chips[1], 1, i), rows(chips[1], 1, i), along)
        arrive(direct[1, 1, i], chips[2], 1, i)
        lifted[2, i] = go(rows(chips[2], 1, i), rows(chips[2], 1, i), along)
    for i in range(SUBS):
        arrive(direct[1, 0, i], chips[2], 0, i)
        far[0, i] = go(rows(chips[2], 0, i), rows(chips[2], 0, i), across[0])
        arrive(direct[0, 0, i], chips[1], 0, i)
    for i in range(SUBS):
        arrive(far[1, i], chips[3], 1, i)
        lifted[3, i] = go(rows(chips[3], 1, i), rows(chips[3], 1, i), along)
    for i in range(SUBS):
        arrive(far[0, i], chips[3], 0, i)
    for k in range(1, 4):
        for i in range(SUBS):
            arrive(lifted[k, i], chips[k], 2, i)
    for copy in passed + small:
        copy.wait_recv()
    for copy in handed:
        pl.when(jnp.logical_not(holder))(copy.wait_recv)
        pl.when(holder)(copy.wait_send)
    for (copy, whole, rel) in sent_inputs:
        pl.when(chips[rel] // 2 == core)(copy.wait_send)
    for copy in started:
        copy.wait_send()
    for copy in locals_:
        copy.wait()


def gather_all(states, memory, cotangent, bank, gains, ints):
    micro, length, shares = states.shape
    sections = lax.axis_size("section")
    width = shares * sections
    wide = jax.ShapeDtypeStruct((length, width), bf16)
    copies = 9 + 12 + 8 + 4 * SUBS + 2 * SUBS + 3 * SUBS + 9 * SUBS
    outs = [wide, wide, wide, jax.ShapeDtypeStruct((sections * bank.shape[0], width), bf16),
            jax.ShapeDtypeStruct((sections,) + gains.shape, f32)]
    outs += [jax.ShapeDtypeStruct((2,) + t.shape, t.dtype) for t in ints]
    return pl.pallas_call(
        gather_kernel,
        out_shape=outs,
        in_specs=[ANY] * 10,
        out_specs=[ANY] * 10,
        scratch_shapes=[pltpu.VMEM(bank.shape, bank.dtype), pltpu.SemaphoreType.DMA((copies,)), pltpu.SemaphoreType.DMA((copies,)),
                        pltpu.SemaphoreType.DMA((12,))],
        compiler_params=pltpu.CompilerParams(collective_id=0, has_side_effects=True, vmem_limit_bytes=60 * 2**20),
        name="gather_all",
    )(states, memory, cotangent, bank, gains, *ints)


SIZES = (96,) * 10 + (64,)
GROUPS = len(SIZES)
LAGS = (0, 1, 2, 2, 3, 4, 5, 6, 7, 8)
AHEAD = 2
RESULTS = 11


def add_rows(target, rows, *others):
    total = target[rows].astype(f32)
    for other, places in others:
        total = total + other[places].astype(f32)
    target[rows] = total.astype(bf16)


def reduce_kernel(
    dw0, dw1, dw2, dw3, gains0, gains1, gains2, gains3, states, dx, dmem, halt,
    bank, gains_sum, states_out, dx_out, dmem_out, halt_out,
    own, other, first, second, left, right, total, full, mine, theirs, score, scores,
    gain_parts, send, recv, home,
):
    s, d, across, _, sibling = neighbours()
    core, layer = d % 2, d // 2
    chips = [s] + [a[0] for a in across]
    column = [(s, (layer + k) % 4 * 2 + core) for k in range(1, 4)]
    up, down = (s, d + 2), (s, d - 2)
    pair = (s, d + 2 - 4 * (layer % 2))
    jump = (s, (layer + 2) % 4 * 2 + core)
    holder = s // 2 == core
    greet(across + [sibling] + column)
    count = [0, 0]
    always, ends = [], []

    def push(src, dst, device):
        i = count[0]
        count[0] += 1
        return pltpu.make_async_remote_copy(src, dst, send.at[i], recv.at[i], device_id=device, device_id_type=MESH)

    def go(src, dst, device):
        copy = push(src, dst, device)
        copy.start()
        always.append(copy)
        return copy

    def fetch(src, dst):
        i = count[1]
        count[1] += 1
        copy = pltpu.make_async_copy(src, dst, home.at[i])
        return copy

    span = dw0.shape[0]
    half = span // 2
    offsets = [sum(SIZES[:g]) for g in range(GROUPS)]
    grads = (dw0, dw1, dw2, dw3)

    def at(g, side):
        return 2 * offsets[g] + side * SIZES[g]

    loads, swaps = {}, {}

    def exchange(g):
        size = 2 * SIZES[g]
        rows = pl.ds(at(g, 0), size)
        there = pl.ds(pl.multiple_of((1 - core) * half + at(g, 0), 32), size)
        here = pl.ds(pl.multiple_of(core * half + at(g, 0), 32), size)
        for t in range(4):
            swaps[g, t] = go(grads[t].at[there], other.at[t, rows], sibling)
            loads[g, t] = fetch(grads[t].at[here], own.at[t, rows])
            loads[g, t].start()

    for g in range(AHEAD):
        exchange(g)
    outs = ((states, states_out), (dx, dx_out), (dmem, dmem_out))
    given, taken = [], []
    for n, (source, _) in enumerate(outs):
        given.append(push(source, theirs.at[n], sibling))
        taken.append(fetch(source, mine.at[n]))
    given.append(push(halt, scores, sibling))
    taken.append(fetch(halt, score))

    def results_begin():
        for copy in given:
            pl.when(jnp.logical_not(holder))(copy.start)
        for copy in taken:
            pl.when(holder)(copy.start)

    gain_steps = [sibling, across[0], across[1], pair, jump]
    for t, part in enumerate((gains0, gains1, gains2, gains3)):
        gain_parts[0, 2 * t : 2 * t + 2] = part[...]
    gain_copies = []

    def gain_step(k):
        if k > 0:
            gain_copies[-1].wait_recv()
            gain_parts[2 * k] = gain_parts[2 * k - 2] + gain_parts[2 * k - 1]
        if k < len(gain_steps):
            gain_copies.append(go(gain_parts.at[2 * k], gain_parts.at[2 * k + 1], gain_steps[k]))
        else:
            for j in range(2):
                gains_sum[j : j + 1, :] = gain_parts[2 * k, pl.ds(2 * s + j, 1), :]

    step1, step2, rs, ag = {}, {}, {}, {}

    def plane_first(g):
        if g + AHEAD < GROUPS:
            exchange(g + AHEAD)
        for t in range(4):
            swaps[g, t].wait_recv()
            loads[g, t].wait()
            rows = pl.ds(at(g, 0), 2 * SIZES[g])
            add_rows(own, (t, rows), (other, (t, rows)))
        for side in range(2):
            rows = pl.ds(at(g, side), SIZES[g])
            for n, rel in enumerate((3, 1 + side)):
                step1[g, side, n] = go(own.at[chips[rel], rows], first.at[n, rows], across[side])

    def plane_second(g):
        for side in range(2):
            rows = pl.ds(at(g, side), SIZES[g])
            for n, rel in enumerate((2 - side, 0)):
                step1[g, side, n].wait_recv()
                add_rows(own, (chips[rel], rows), (first, (n, rows)))
                if n == 0:
                    step2[g, side] = go(own.at[chips[rel], rows], second.at[rows], across[1 - side])

    def plane_third(g):
        for side in range(2):
            step2[g, side].wait_recv()
            rows = pl.ds(at(g, side), SIZES[g])
            value = own[s, rows].astype(f32) + second[rows].astype(f32)
            total[pl.ds(2 * offsets[g] + side * SIZES[g], SIZES[g])] = value.astype(bf16)

    def span_of(g, k0, k1):
        shard = SIZES[g] // 2
        return pl.ds(2 * offsets[g] + k0 * shard, (k1 - k0) * shard)

    def share(kind, g, low, high, src, dst, device):
        return push(src.at[span_of(g, low, high)], dst.at[span_of(g, low, high)], device)

    def line_sums(g):
        for z in range(3):
            rs[g, "up", z] = share("up", g, z + 1, 4, total, right, up)
            rs[g, "down", z + 1] = share("down", g, 0, z + 1, total, left, down)
        for k in range(4):
            for z in range(k, 3):
                ag[g, "up", z, k] = push(full.at[span_of(g, k, k + 1)], full.at[span_of(g, k, k + 1)], up)
            for z in range(1, k + 1):
                ag[g, "down", z, k] = push(full.at[span_of(g, k, k + 1)], full.at[span_of(g, k, k + 1)], down)

    def at_layer(z, action):
        pl.when(layer == z)(action)

    def close(g, k, *others):
        value = total[span_of(g, k, k + 1)].astype(f32)
        for other_ in others:
            value = value + other_[span_of(g, k, k + 1)].astype(f32)
        full[span_of(g, k, k + 1)] = value.astype(bf16)

    def line_1(g):
        line_sums(g)
        at_layer(0, lambda: rs[g, "up", 0].start())
        at_layer(3, lambda: rs[g, "down", 3].start())

    def line_2(g):
        def second_layer():
            rs[g, "up", 0].wait_recv()
            add_rows(total, span_of(g, 2, 4), (right, span_of(g, 2, 4)))
            rs[g, "up", 1].start()

        def third_layer():
            rs[g, "down", 3].wait_recv()
            add_rows(total, span_of(g, 0, 2), (left, span_of(g, 0, 2)))
            rs[g, "down", 2].start()

        at_layer(1, second_layer)
        at_layer(2, third_layer)

    def line_3(g):
        def third_layer():
            rs[g, "up", 1].wait_recv()
            add_rows(total, span_of(g, 3, 4), (right, span_of(g, 3, 4)))
            rs[g, "up", 2].start()
            close(g, 2, right, left)
            ag[g, "up", 2, 2].start()
            ag[g, "down", 2, 2].start()

        def second_layer():
            rs[g, "down", 2].wait_recv()
            add_rows(total, span_of(g, 0, 1), (left, span_of(g, 0, 1)))
            rs[g, "down", 1].start()
            close(g, 1, right, left)
            ag[g, "up", 1, 1].start()
            ag[g, "down", 1, 1].start()

        at_layer(2, third_layer)
        at_layer(1, second_layer)

    def line_4(g):
        def bottom():
            rs[g, "down", 1].wait_recv()
            close(g, 0, left)
            ag[g, "up", 0, 0].start()

        def top():
            rs[g, "up", 2].wait_recv()
            close(g, 3, right)
            ag[g, "down", 3, 3].start()

        def second_layer():
            ag[g, "down", 2, 2].wait_recv()
            ag[g, "down", 1, 2].start()

        def third_layer():
            ag[g, "up", 1, 1].wait_recv()
            ag[g, "up", 2, 1].start()

        at_layer(0, bottom)
        at_layer(3, top)
        at_layer(1, second_layer)
        at_layer(2, third_layer)

    def line_5(g):
        def bottom():
            ag[g, "down", 1, 1].wait_recv()

        def top():
            ag[g, "up", 2, 2].wait_recv()

        def second_layer():
            ag[g, "up", 0, 0].wait_recv()
            ag[g, "up", 1, 0].start()

        def third_layer():
            ag[g, "down", 3, 3].wait_recv()
            ag[g, "down", 2, 3].start()

        at_layer(0, bottom)
        at_layer(3, top)
        at_layer(1, second_layer)
        at_layer(2, third_layer)

    def line_6(g):
        def bottom():
            ag[g, "down", 1, 2].wait_recv()

        def top():
            ag[g, "up", 2, 1].wait_recv()

        def second_layer():
            ag[g, "down", 2, 3].wait_recv()
            ag[g, "down", 1, 3].start()

        def third_layer():
            ag[g, "up", 1, 0].wait_recv()
            ag[g, "up", 2, 0].start()

        at_layer(0, bottom)
        at_layer(3, top)
        at_layer(1, second_layer)
        at_layer(2, third_layer)

    finals = {}

    def line_7(g):
        at_layer(0, lambda: ag[g, "down", 1, 3].wait_recv())
        at_layer(3, lambda: ag[g, "up", 2, 0].wait_recv())
        here = pl.ds(pl.multiple_of(core * half + at(g, 0), 32), 2 * SIZES[g])
        rows = full.at[pl.ds(2 * offsets[g], 2 * SIZES[g])]
        finals[g] = go(rows, bank.at[here], sibling)
        copy = fetch(rows, bank.at[here])
        copy.start()
        ends.append(copy)

    handed = []

    def results():
        def collect():
            for copy in taken:
                copy.wait()
            for copy in given:
                copy.wait_recv()
            size = mine.shape[1] // 8

            def add(i, _):
                rows = pl.ds(pl.multiple_of(i * size, size), size)
                for n in range(3):
                    add_rows(mine, (n, rows), (theirs, (n, rows)))
                return 0

            lax.fori_loop(0, 8, add, 0)
            score[...] = score[...] + scores[...]

        pl.when(holder)(collect)
        for rel in range(4):
            target = chips[rel]
            for n in range(4):
                out = (states_out, dx_out, dmem_out, halt_out)[n]
                share_ = out.shape[2]
                src = score if n == 3 else mine.at[n]
                src = src.at[:, pl.ds(pl.multiple_of(target * share_, share_), share_)]
                if rel == 0:
                    copy = fetch(src, out.at[s % 2])
                else:
                    copy = push(src, out.at[s % 2], across[rel - 1])
                pl.when(holder)(copy.start)
                handed.append((rel, copy))

    stages = [plane_first, plane_second, plane_third, line_1, line_2, line_3, line_4, line_5, line_6, line_7]
    for tick in range(GROUPS + LAGS[-1]):
        for stage, lag in zip(stages, LAGS):
            if 0 <= tick - lag < GROUPS:
                stage(tick - lag)
        if tick <= len(gain_steps):
            gain_step(tick)
        if tick == RESULTS - 1:
            results_begin()
        if tick == RESULTS:
            results()

    for rel, copy in handed:
        if rel == 0:
            pl.when(holder)(copy.wait)
        else:
            pl.when(chips[rel] // 2 == core)(copy.wait_recv)
            pl.when(holder)(copy.wait_send)
    for copy in given:
        pl.when(jnp.logical_not(holder))(copy.wait_send)
    for copy in finals.values():
        copy.wait_recv()
    for copy in always:
        copy.wait_send()
    for copy in ends:
        copy.wait()
    for (g, way, z), copy in rs.items():
        at_layer(z, copy.wait_send)
    for (g, way, z, k), copy in ag.items():
        at_layer(z, copy.wait_send)


def reduce_all(dw, gains, states, dx, dmem, halt, sections):
    length, width = states.shape
    span = dw[0].shape[0]
    half = span // 2
    shares = width // sections
    micro = 2
    share = jax.ShapeDtypeStruct((micro, length, shares), bf16)
    outs = [jax.ShapeDtypeStruct((span, width), bf16), jax.ShapeDtypeStruct((2, width), f32), share, share, share,
            jax.ShapeDtypeStruct((micro, halt.shape[0], length // sections), f32)]
    copies = 8 * GROUPS + 4 + 5 + (4 + 2 + 6 + 12 + 2) * GROUPS + 12
    scratch = [
        pltpu.VMEM((4, half, width), bf16), pltpu.VMEM((4, half, width), bf16),
        pltpu.VMEM((2, half, width), bf16), pltpu.VMEM((half, width), bf16),
        pltpu.VMEM((half, width), bf16), pltpu.VMEM((half, width), bf16),
        pltpu.VMEM((half, width), bf16), pltpu.VMEM((half, width), bf16),
        pltpu.VMEM((3, length, width), bf16), pltpu.VMEM((3, length, width), bf16),
        pltpu.VMEM(halt.shape, f32), pltpu.VMEM(halt.shape, f32),
        pltpu.VMEM((11, 2 * sections, width), f32),
        pltpu.SemaphoreType.DMA((copies,)), pltpu.SemaphoreType.DMA((copies,)),
        pltpu.SemaphoreType.DMA((8 * GROUPS + 4 + 2 * GROUPS + 4,)),
    ]
    return pl.pallas_call(
        reduce_kernel,
        out_shape=outs,
        in_specs=[ANY] * 4 + [VMEM] * 4 + [ANY] * 4,
        out_specs=[ANY, VMEM, ANY, ANY, ANY, ANY],
        scratch_shapes=scratch,
        compiler_params=pltpu.CompilerParams(collective_id=1, has_side_effects=True, vmem_limit_bytes=60 * 2**20),
        name="reduce_all",
    )(*dw, *gains, states, dx, dmem, halt)


def swap_cores(value):
    count = lax.axis_size("dp")
    return lax.ppermute(value, "dp", [(i, i ^ 1) for i in range(count)])


def gather_plain(states, memory, cotangent, bank, gains, ints):
    section, core = lax.axis_index("section"), lax.axis_index("dp") % 2
    micro = states.shape[0]
    holder = section // micro == core

    def pick(rows):
        own = lax.dynamic_index_in_dim(rows, section % micro, 0, keepdims=False)
        return jnp.where(holder, own, swap_cores(own))

    wide = [pick(lax.all_gather(t, "section", axis=2, tiled=True)) for t in (states, memory, cotangent)]
    return wide, lax.all_gather(bank, "section"), lax.all_gather(gains, "section"), [pick(t) for t in ints]


def reduce_plain(dw, dgains, states, dx, dmem, halt):
    section, core = lax.axis_index("section"), lax.axis_index("dp") % 2
    micro = 2
    holder = section // micro == core

    def to_shares(value):
        both = value.astype(f32) + swap_cores(value).astype(f32)
        both = jnp.where(holder, both, 0).astype(value.dtype)
        slots = jnp.stack([jnp.where(section % micro == i, both, 0) for i in range(micro)])
        return lax.psum_scatter(slots, "section", scatter_dimension=2, tiled=True)

    bank = lax.psum_scatter(jnp.stack(dw), "section", scatter_dimension=0, tiled=True)[0]
    bank = lax.psum(bank.astype(f32), "dp")
    gain_sum = lax.psum_scatter(jnp.stack(dgains), "section", scatter_dimension=0, tiled=True)[0]
    gain_sum = lax.psum(gain_sum, "dp")
    return bank, gain_sum, *[to_shares(t) for t in (states, dx, dmem, halt)]


def local(
    states_in, memory, cotangent, weight_bank, gain_bank, segments, pad_mask, memory_segments, memory_mask, exit_depths
):
    section, sections = lax.axis_index("section"), lax.axis_size("section")
    core = lax.axis_index("dp") % 2
    matrices = weight_bank.shape[1:]
    width = matrices[-1]
    ints = (segments, pad_mask, memory_segments, memory_mask, exit_depths)
    near = sections == 4 and lax.axis_size("dp") == 8
    if near:
        x, mem, top, bank, gains, *ints = gather_all(
            states_in, memory, cotangent, weight_bank[0].reshape(-1, width), gain_bank[0], ints
        )
        bank = bank.reshape((sections,) + matrices)
        row = section
    else:
        (x, mem, top), bank, gains, ints = gather_plain(
            states_in, memory, cotangent, weight_bank[0], gain_bank[0], ints
        )
        ints, row = [t[None, None] for t in ints], jnp.zeros((), i32)
    states, halt, dx, dmem, dw, dgains = row_forward_backward(
        row, core, x, mem, top, bank, gains, ints
    )
    if near:
        grads = [t.reshape(-1, width) for t in dw]
        bank, gain_sum, states, dx, dmem, halt = reduce_all(
            grads, dgains, states, dx, dmem, halt, sections
        )
    else:
        bank, gain_sum, states, dx, dmem, halt = reduce_plain(dw, dgains, states, dx, dmem, halt)
        bank = bank.reshape(-1, width)
    bank, dx, dmem, halt = widen(bank, dx, dmem, halt)
    return states, halt, dx, dmem, bank.reshape((1,) + matrices), gain_sum[None]


def solution(mesh):
    rows = P("dp", None, "section")
    return jax.shard_map(
        local,
        mesh=mesh,
        in_specs=(
            rows, rows, rows, P("section", None, None, None), P("section", None, None),
            P("dp", None), P("dp", None), P("dp", None), P("dp", None), P("dp", None),
        ),
        out_specs=(rows, rows, rows, rows, P("section", None, None, None), P("section", None, None)),
        check_vma=False,
    )
```
